128 devices in a mesh: replica: 32 (over x, y, core), fsdp: 4 (over z).
Axes of the slice: x: 4, y: 4, z: 4, core: 2. Of those that a mesh axis runs over, the one named last changes fastest.
Arguments:
- local_weights: bfloat16 [32, 2, 512, 8192], P('replica', None, 'fsdp'), may hold values from -100000 to 100000
- global_weights: float32 [2, 512, 8192], P(None, 'fsdp'), may hold values from -6 to 6
- momentum: float32 [2, 512, 8192], P(None, 'fsdp', 'replica'), may hold values from -6 to 6
Outputs:
- refreshed: float32 [2, 512, 8192], P(None, 'fsdp')
- new_momentum: float32 [2, 512, 8192], P(None, 'fsdp', 'replica')
The draws below stay inside these ranges and needn't reach their ends.
All inputs are finite; a program needn't handle non-finite values. Where the reference program divides by a largest or mean magnitude, that divisor is 1e-20 or more.
Results may differ from the reference program's by a relative error of at most 0.012.
Values may be sent and summed in bfloat16 or wider, within the bound.
A program may use at most 128 MiB of HBM per device.

```python
import jax
import jax.numpy as jnp
from jax import lax

D = 8192
FRAGS = 2
ROWS = 512
REPLICAS = 32


def shared_global(key):
    return jnp.clip(jax.random.normal(key, (FRAGS, ROWS, D), jnp.float32), -6.0, 6.0)


def log_spread(key, shape):
    return jnp.exp(jax.random.uniform(key, shape, jnp.float32, jnp.log(0.3), jnp.log(3.0)))


def draw_global_weights(key, part):
    return shared_global(key)


def draw_local_weights(key, part):
    base = shared_global(key)
    key = jax.random.fold_in(key, 2)
    first, second, third = jax.random.split(key, 3)
    noise = jnp.clip(jax.random.normal(first, (REPLICAS, FRAGS, ROWS, D), jnp.float32), -6.0, 6.0)
    fragment_level = jnp.where(jnp.arange(FRAGS) == 1, 0.2, 1.0).astype(jnp.float32)
    column_base = 3.0
    replica_rise = 3.0 ** (jnp.arange(REPLICAS, dtype=jnp.float32) / max(REPLICAS - 1, 1))
    row_rise = 3.0 ** (jnp.arange(ROWS, dtype=jnp.float32) / max(ROWS - 1, 1))
    column_rise = column_base ** (jnp.arange(D, dtype=jnp.float32) / max(D - 1, 1))
    row_factor = row_rise[None, :] * log_spread(second, (FRAGS, ROWS)) * fragment_level[:, None]
    column_factor = log_spread(third, (FRAGS, D)) * column_rise[None, :]
    difference = 8.0 * replica_rise[:, None, None, None] * row_factor[None, :, :, None] * column_factor[None, :, None, :] * noise
    return (base[None] - difference).astype(jnp.bfloat16)


def steps_of(rng, extent, shards, least, top_value):
    factor_of = 1.0
    for axis_at, blocks in shards:
        steps = jax.random.uniform(jax.random.fold_in(jax.random.fold_in(rng, 6), axis_at), (blocks,), jnp.float32, least / len(shards), top_value / len(shards))
        factor_of = factor_of * jnp.repeat(jnp.exp(steps), extent[axis_at] // blocks).reshape((-1,) + (1,) * (len(extent) - 1 - axis_at))
    return factor_of


def gaussian(own_key, extent, spread, reach, shards=(), kind=jnp.bfloat16):
    gain = steps_of(own_key, extent, shards, -0.22, 0.18) if shards else 1.0
    values = jax.random.normal(own_key, extent, jnp.float32) * spread * gain
    return jnp.minimum(jnp.maximum(values, -reach), reach).astype(kind)


def setup_inputs(seed: int = 0) -> dict:
    key_of = jax.random.split(jax.random.key(seed), 4)
    return {
        "local_weights": draw_local_weights(jax.random.fold_in(key_of[3], 71), 0),
        "global_weights": draw_global_weights(jax.random.fold_in(key_of[3], 71), 0),
        "momentum": gaussian(key_of[2], (FRAGS, ROWS, D), 1.0, 6.0, ((1, 4), (2, 32)), jnp.float32),
    }


OUTER_MOMENTUM = 0.9
OUTER_RATE = 0.7
CLIP_LEVEL = 1.0
SCALE_EPSILON = 1e-06

def quantize(values):
    blocks = values.reshape(values.shape[:-1] + (values.shape[-1] // 64, 64))
    scales = (lax.optimization_barrier(jnp.max(jnp.abs(blocks), axis=-1)) + SCALE_EPSILON).astype(jnp.bfloat16)
    encoded = (blocks / scales.astype(jnp.float32)[..., None]).astype(jnp.bfloat16)
    return (encoded.reshape(values.shape), scales)

def restore(encoded, scales):
    blocks = encoded.astype(jnp.float32).reshape(encoded.shape[:-1] + (encoded.shape[-1] // 64, 64))
    return (blocks * scales.astype(jnp.float32)[..., None]).reshape(encoded.shape)

def reference(local_weights, global_weights, momentum):

    def accumulate(running, replica_local):
        encoded, scales = quantize(global_weights - replica_local.astype(jnp.float32))
        return (running + restore(encoded, scales), None)
    summed, ignored = lax.scan(accumulate, jnp.zeros((FRAGS, ROWS, D), jnp.float32), local_weights)
    average = summed / REPLICAS
    norm_squared = lax.optimization_barrier(jnp.sum(average * average, axis=(1, 2)))
    factor = jnp.minimum(1.0, CLIP_LEVEL * jnp.sqrt(jnp.float32(ROWS * D)) / jnp.sqrt(norm_squared + 1e-06))
    clipped = average * factor[:, None, None]
    moment = OUTER_MOMENTUM * momentum + clipped
    outer_step = clipped + OUTER_MOMENTUM * moment
    step_codes, step_scales = quantize(outer_step)
    refreshed = global_weights - OUTER_RATE * restore(step_codes, step_scales)
    return (refreshed, moment)
```

```python
import functools

import jax
import jax.numpy as jnp
from jax import lax
from jax.experimental import pallas as pl
from jax.experimental.pallas import tpu as pltpu
from jax.sharding import PartitionSpec as P

OUTER_MOMENTUM = 0.9
OUTER_RATE = 0.7
CLIP_LEVEL = 1.0
MESH = pl.DeviceIdType.MESH
RING = 4
F32, BF16 = jnp.float32, jnp.bfloat16


def kernel(zs, count, copies, lw_hbm, gw_hbm, mom_hbm, out_hbm, mout_hbm,
           gw, lw, mom, mout, ds, dr, s_send, s_mid, s_end, tt, t_send, t_mid, t_end, av, n1, n2, g, h,
           in_sems, out_sems, mom_sems, send_sems, recv_sems, norm_send, norm_recv):
    frags, rows, _ = gw.shape
    width = mom.shape[2]
    half_rows, quarter = rows // 2, rows // 4
    r = lax.axis_index("replica")
    z = lax.axis_index("fsdp")
    core = r % 2
    y = (r // 2) % RING
    x = r // (2 * RING)

    def dev(ox, oy, oc=0, oz=0):
        ax, ay = (x + ox) % RING, (y + oy) % RING
        return ((ax * RING + ay) * 2 + (core + oc) % 2, (z + oz) % zs)

    def along(axis, o):
        return dev(o, 0) if axis == 0 else dev(0, o)

    def column(first, o, j, c):
        ax, ay = (x + (o if first == 0 else j)) % RING, (y + (j if first == 0 else o)) % RING
        return pl.multiple_of(((ax * RING + ay) * 2 + c) * width, width)

    started = []

    def send(src, dst, device):
        i = len(started)
        copy = pltpu.make_async_remote_copy(
            src_ref=src, dst_ref=dst, send_sem=send_sems.at[i], recv_sem=recv_sems.at[i],
            device_id=device, device_id_type=MESH)
        copy.start()
        started.append(copy)
        return copy

    loads = {}
    for f in range(frags):
        for hf in range(2):
            at = pl.ds(hf * half_rows, half_rows)
            loads[f, hf] = [
                pltpu.make_async_copy(gw_hbm.at[f, at], gw.at[f, at], in_sems.at[f, hf, 0]),
                pltpu.make_async_copy(lw_hbm.at[0, f, at], lw.at[f, at], in_sems.at[f, hf, 1])]
            for copy in loads[f, hf]:
                copy.start()
    mom_load = pltpu.make_async_copy(mom_hbm, mom, mom_sems.at[0])
    mom_load.start()

    near = [(0, 0, oc, oz) for oz in range(zs) for oc in range(2) if (oc, oz) != (0, 0)]
    far = [(ox, oy, 0, 0) for ox in range(RING) for oy in range(RING) if (ox, oy) != (0, 0)]
    barrier = pltpu.get_barrier_semaphore()
    for partner in near + far:
        pl.semaphore_signal(barrier, inc=1, device_id=dev(*partner), device_id_type=MESH)
    pl.semaphore_wait(barrier, len(near) + len(far))

    def difference(f, row, n, col):
        at = pl.ds(row, n)
        return gw[f, at, pl.ds(col, width)] - lw[f, at, pl.ds(col, width)].astype(F32)

    core_copies, mid, end, mid2, end2 = {}, {}, {}, {}, {}

    def to_core(f, hf):
        for copy in loads[f, hf]:
            copy.wait()
        for o in (2, 1, 3, 0):
            @pl.loop(0, RING)
            def _(j):
                col = column(hf, o, j, 1 - core)
                ds[f, hf, o, j] = difference(f, hf * half_rows, half_rows, col).astype(BF16)
            core_copies[f, hf, o] = send(ds.at[f, hf, o], dr.at[f, hf, o], dev(0, 0, 1))

    def pair_sum(f, hf, o, j, q, n):
        col = column(hf, o, j, core)
        return (difference(f, hf * half_rows + q * quarter, n * quarter, col)
                + dr[f, hf, o, j, pl.ds(q * quarter, n * quarter)].astype(F32))

    def ring1_open(f, hf):
        core_copies[f, hf, 2].wait_recv()
        for q in range(2):
            @pl.loop(0, RING)
            def _(j):
                s_send[f, hf, 1, q, j] = pair_sum(f, hf, 2, j, q, 1).astype(BF16)
            mid[f, hf, q] = send(s_send.at[f, hf, 1, q], s_mid.at[f, hf, q], along(hf, 1 if q == 0 else -1))
        for o, q, way in ((1, 1, 1), (3, 0, -1)):
            core_copies[f, hf, o].wait_recv()

            @pl.loop(0, RING)
            def _(j):
                s_send[f, hf, o - 1, q, j] = pair_sum(f, hf, o, j, q, 1).astype(BF16)
            k = 0 if way == 1 else 1
            end[f, hf, k, q] = send(s_send.at[f, hf, o - 1, q], s_end.at[f, hf, k, q], along(hf, way))

    def ring1_middle(f, hf):
        for o, q, way in ((1, 0, 1), (3, 1, -1)):
            mid[f, hf, q].wait_recv()

            @pl.loop(0, RING)
            def _(j):
                total = pair_sum(f, hf, o, j, q, 1) + s_mid[f, hf, q, j].astype(F32)
                s_send[f, hf, o - 1, q, j] = total.astype(BF16)
            k = 0 if way == 1 else 1
            end[f, hf, k, q] = send(s_send.at[f, hf, o - 1, q], s_end.at[f, hf, k, q], along(hf, way))

    def ring2_open(f, hf):
        core_copies[f, hf, 0].wait_recv()
        for k in range(2):
            for q in range(2):
                end[f, hf, k, q].wait_recv()

        def whole(j):
            for q in range(2):
                total = pair_sum(f, hf, 0, j, q, 1)
                total = total + s_end[f, hf, 0, q, j].astype(F32) + s_end[f, hf, 1, q, j].astype(F32)
                tt[f, hf, j, q] = total
                if j:
                    t_send[f, hf, j - 1, q] = total.astype(BF16)

        whole(2)
        for q in range(2):
            mid2[f, hf, q] = send(t_send.at[f, hf, 1, q], t_mid.at[f, hf, q], along(1 - hf, 1 if q == 0 else -1))
        whole(1)
        end2[f, hf, 0, 1] = send(t_send.at[f, hf, 0, 1], t_end.at[f, hf, 0, 1], along(1 - hf, 1))
        whole(3)
        end2[f, hf, 1, 0] = send(t_send.at[f, hf, 2, 0], t_end.at[f, hf, 1, 0], along(1 - hf, -1))
        whole(0)

    def ring2_middle(f, hf):
        for j, q, way in ((1, 0, 1), (3, 1, -1)):
            mid2[f, hf, q].wait_recv()
            t_send[f, hf, j - 1, q] = (tt[f, hf, j, q] + t_mid[f, hf, q].astype(F32)).astype(BF16)
            k = 0 if way == 1 else 1
            end2[f, hf, k, q] = send(t_send.at[f, hf, j - 1, q], t_end.at[f, hf, k, q], along(1 - hf, way))

    def ring2_close(f, hf):
        total = 0.0
        for q in range(2):
            for k in range(2):
                end2[f, hf, k, q].wait_recv()
            part = tt[f, hf, 0, q] + t_end[f, hf, 0, q].astype(F32) + t_end[f, hf, 1, q].astype(F32)
            part = part * (1.0 / (2 * RING * RING))
            av[f, pl.ds(hf * half_rows + q * quarter, quarter)] = part
            square = jnp.sum((part * part).reshape(quarter // 8, 8, width), axis=0)
            for c in range(width // 128):
                total = total + square[:, c * 128:(c + 1) * 128]
        return total

    def exchange(f, stage, tiles, partners):
        n = len(partners)
        for i, partner in enumerate(partners):
            pltpu.make_async_remote_copy(
                src_ref=tiles.at[f, n], dst_ref=tiles.at[f, i], send_sem=norm_send.at[f, stage],
                recv_sem=norm_recv.at[f, stage], device_id=dev(*partner), device_id_type=MESH).start()

    def gathered(f, stage, tiles, partners):
        part = tiles.at[f, pl.ds(0, len(partners))]
        pltpu.make_async_copy(part, part, norm_recv.at[f, stage]).wait()
        return jnp.sum(tiles[f], axis=0)

    def norm_open(f, total):
        n1[f, len(near)] = total
        exchange(f, 0, n1, near)

    def norm_middle(f):
        n2[f, len(far)] = gathered(f, 0, n1, near)
        exchange(f, 1, n2, far)

    gathers = {}
    mom_stores = {}

    def outer(f):
        total = gathered(f, 1, n2, far)
        norm_squared = jnp.sum(total, axis=(0, 1), keepdims=True)
        factor = jnp.minimum(1.0, CLIP_LEVEL * jnp.sqrt(F32(count)) / jnp.sqrt(norm_squared + 1e-06))
        for hf in range(2):
            at = pl.ds(hf * half_rows, half_rows)
            clipped = av[f, at] * factor
            moment = OUTER_MOMENTUM * mom[f, at] + clipped
            mout[f, at] = moment
            g[f, hf, 0, 0] = (clipped + OUTER_MOMENTUM * moment).astype(BF16)
            for way in (1, -1):
                pass_on(f, hf, 1, 0, 0, way, None)
            for way in (1, -1):
                pass_on(f, hf, 2, 0, 0, way, None)
        mom_stores[f] = pltpu.make_async_copy(mout.at[f], mout_hbm.at[f], mom_sems.at[1 + f])
        mom_stores[f].start()

    def pass_on(f, hf, ring, o2, o1, way, q):
        axis = 1 - hf if ring == 1 else hf
        to2, to1 = (o2, (o1 - way) % RING) if ring == 1 else ((o2 - way) % RING, o1)
        src, dst = g.at[f, hf, o2, o1], g.at[f, hf, to2, to1]
        if q is not None:
            at = pl.ds(q * quarter, quarter)
            src, dst = src.at[at], dst.at[at]
        gathers[f, hf, to2, to1, q] = send(src, dst, along(axis, way))

    def arrived(f, hf, o2, o1):
        for q in (0, 1) if (o2 == 2 if o2 else o1 == 2) else (None,):
            gathers[f, hf, o2, o1, q].wait_recv()

    def gather1_middle(f, hf):
        for o1, way, q in ((3, 1, 0), (1, -1, 1)):
            arrived(f, hf, 0, o1)
            pass_on(f, hf, 1, 0, o1, way, q)
            for way2 in (1, -1):
                pass_on(f, hf, 2, 0, o1, way2, None)

    def gather1_close(f, hf):
        arrived(f, hf, 0, 2)
        for way in (1, -1):
            pass_on(f, hf, 2, 0, 2, way, None)
        hand_over(f, hf, 0)

    def gather2_middle(f, hf):
        for o1 in (0, 3, 1, 2):
            for o2, way, q in ((3, 1, 0), (1, -1, 1)):
                arrived(f, hf, o2, o1)
                pass_on(f, hf, 2, o2, o1, way, q)
        for o2 in (3, 1):
            hand_over(f, hf, o2)

    def gather2_close(f, hf):
        for o1 in range(RING):
            arrived(f, hf, 2, o1)
        hand_over(f, hf, 2)

    handed = {}

    def hand_over(f, hf, o2):
        handed[f, hf, o2] = send(g.at[f, hf, o2], h.at[f, hf, o2], dev(0, 0, 1))

    def refresh(f, hf, o2, blocks, c):
        at = pl.ds(hf * half_rows, half_rows)

        @pl.loop(0, RING)
        def _(j):
            col = pl.ds(column(hf, o2, j, c), width)
            gw[f, at, col] = gw[f, at, col] - OUTER_RATE * blocks[f, hf, o2, j].astype(F32)

    stores = []

    def store(f, hf, o2):
        at = pl.ds(hf * half_rows, half_rows)
        if hf == 0:
            n = RING * 2 * width
            cols = [pl.ds(pl.multiple_of(((x + o2) % RING) * n, n), n)]
        else:
            n = 2 * width
            cols = [pl.ds(pl.multiple_of((ax * RING + (y + o2) % RING) * n, n), n) for ax in range(RING)]
        for i, col in enumerate(cols):
            copy = pltpu.make_async_copy(gw.at[f, at, col], out_hbm.at[f, at, col], out_sems.at[f, hf, o2, i])
            copy.start()
            stores.append(copy)

    def own(f, hf, o2):
        refresh(f, hf, o2, g, core)

    def other(f, hf, o2):
        handed[f, hf, o2].wait_recv()
        refresh(f, hf, o2, h, 1 - core)
        store(f, hf, o2)

    both = range(2)
    for hf in both:
        to_core(0, hf)
    for hf in both:
        ring1_open(0, hf)
    for hf in both:
        to_core(1, hf)
    for hf in both:
        ring1_middle(0, hf)
    for hf in both:
        ring1_open(1, hf)
    for hf in both:
        ring2_open(0, hf)
    for hf in both:
        ring2_middle(0, hf)
    for hf in both:
        ring1_middle(1, hf)
    norm_open(0, ring2_close(0, 0) + ring2_close(0, 1))
    for hf in both:
        ring2_open(1, hf)
    norm_middle(0)
    for hf in both:
        ring2_middle(1, hf)
    mom_load.wait()
    outer(0)
    norm_open(1, ring2_close(1, 0) + ring2_close(1, 1))
    for hf in both:
        gather1_middle(0, hf)
    norm_middle(1)
    for hf in both:
        gather1_close(0, hf)
    outer(1)
    for hf in both:
        gather2_middle(0, hf)
    for hf in both:
        gather1_middle(1, hf)
    for hf in both:
        gather1_close(1, hf)
    for hf in both:
        gather2_close(0, hf)
    for o2 in (0, 3, 1, 2):
        for hf in both:
            own(0, hf, o2)
            other(0, hf, o2)
    for hf in both:
        gather2_middle(1, hf)
    for hf in both:
        for o2 in (0, 3, 1):
            own(1, hf, o2)
            other(1, hf, o2)
    for hf in both:
        gather2_close(1, hf)
    for hf in both:
        own(1, hf, 2)
    for hf in both:
        other(1, hf, 2)

    assert len(started) == copies, len(started)
    for copy in started:
        copy.wait_send()
    for f in range(frags):
        for stage, tiles, n in ((0, n1, len(near)), (1, n2, len(far))):
            part = tiles.at[f, pl.ds(0, n)]
            pltpu.make_async_copy(part, part, norm_send.at[f, stage]).wait()
        mom_stores[f].wait()
    for copy in stores:
        copy.wait()


COPIES = 160


def synchronize(local_weights, global_weights, momentum):
    frags, rows, cols = global_weights.shape
    width = momentum.shape[2]
    zs = lax.axis_size("fsdp")
    assert lax.axis_size("replica") == 2 * RING * RING and frags == 2
    half_rows, quarter = rows // 2, rows // 4
    vmem = lambda shape, dtype: pltpu.VMEM(shape, dtype)
    anywhere = pl.BlockSpec(memory_space=pl.ANY)
    return pl.pallas_call(
        functools.partial(kernel, zs, rows * zs * cols, COPIES),
        out_shape=(
            jax.ShapeDtypeStruct(global_weights.shape, F32),
            jax.ShapeDtypeStruct(momentum.shape, F32),
        ),
        in_specs=[anywhere] * 3,
        out_specs=(anywhere, anywhere),
        scratch_shapes=[
            vmem((frags, rows, cols), F32),
            vmem((frags, rows, cols), BF16),
            vmem((frags, rows, width), F32),
            vmem((frags, rows, width), F32),
            vmem((frags, 2, RING, RING, half_rows, width), BF16),
            vmem((frags, 2, RING, RING, half_rows, width), BF16),
            vmem((frags, 2, RING - 1, 2, RING, quarter, width), BF16),
            vmem((frags, 2, 2, RING, quarter, width), BF16),
            vmem((frags, 2, 2, 2, RING, quarter, width), BF16),
            vmem((frags, 2, RING, 2, quarter, width), F32),
            vmem((frags, 2, RING - 1, 2, quarter, width), BF16),
            vmem((frags, 2, 2, quarter, width), BF16),
            vmem((frags, 2, 2, 2, quarter, width), BF16),
            vmem((frags, rows, width), F32),
            vmem((frags, 2 * zs, 8, 128), F32),
            vmem((frags, RING * RING, 8, 128), F32),
            vmem((frags, 2, RING, RING, half_rows, width), BF16),
            vmem((frags, 2, RING, RING, half_rows, width), BF16),
            pltpu.SemaphoreType.DMA((frags, 2, 2)),
            pltpu.SemaphoreType.DMA((frags, 2, RING, RING)),
            pltpu.SemaphoreType.DMA((1 + frags,)),
            pltpu.SemaphoreType.DMA((COPIES,)),
            pltpu.SemaphoreType.DMA((COPIES,)),
            pltpu.SemaphoreType.DMA((frags, 2)),
            pltpu.SemaphoreType.DMA((frags, 2)),
        ],
        compiler_params=pltpu.CompilerParams(
            collective_id=0, has_side_effects=True, vmem_limit_bytes=48 * 2**20
        ),
        cost_estimate=pl.CostEstimate(flops=20 * rows * cols, bytes_accessed=20 * frags * rows * cols // 2, transcendentals=0),
    )(local_weights, global_weights, momentum)


def solution(mesh):
    return jax.shard_map(
        synchronize,
        mesh=mesh,
        in_specs=(
            P("replica", None, "fsdp", None),
            P(None, "fsdp", None),
            P(None, "fsdp", "replica"),
        ),
        out_specs=(P(None, "fsdp", None), P(None, "fsdp", "replica")),
        check_vma=False,
    )
```

```python
import functools

import jax
import jax.numpy as jnp
from jax import lax
from jax.experimental import pallas as pl
from jax.experimental.pallas import tpu as pltpu
from jax.sharding import PartitionSpec as P

OUTER_MOMENTUM = 0.9
OUTER_RATE = 0.7
CLIP_LEVEL = 1.0
MESH = pl.DeviceIdType.MESH
RING = 4
OFFSETS = (0, 1, -1, 2)
F32, BF16 = jnp.float32, jnp.bfloat16


def kernel(zs, count, lw_hbm, gw_hbm, mom_hbm, gw, mout,
           lw, mom, ds, dr, s_send, s_mid, s_end, tt, t_send, t_end, av, n1, n2, g, h,
           in_sems, send_sems, norm_sems, core_sems, mid_sems, end_sems, end2_sems, gather_sems, hand_sems):
    frags, rows, _ = gw.shape
    width = mom.shape[2]
    half_rows, quarter = rows // 2, rows // 4
    r = lax.axis_index("replica")
    z = lax.axis_index("fsdp")
    core = r % 2
    y = (r // 2) % RING
    x = r // (2 * RING)
    both = range(2)

    def dev(ox, oy, oc=0, oz=0):
        ax, ay = (x + ox) % RING, (y + oy) % RING
        return ((ax * RING + ay) * 2 + (core + oc) % 2, (z + oz) % zs)

    def along(axis, o):
        return dev(o, 0) if axis == 0 else dev(0, o)

    def column(hf, a, b, c):
        ax, ay = (x + (a if hf == 0 else b)) % RING, (y + (b if hf == 0 else a)) % RING
        return pl.multiple_of(((ax * RING + ay) * 2 + c) * width, width)

    def offset(slot):
        return jnp.where(slot == 2, -1, jnp.where(slot == 3, 2, slot))

    def send(src, dst, family, recv_sem, device):
        pltpu.make_async_remote_copy(
            src_ref=src, dst_ref=dst, send_sem=send_sems.at[family], recv_sem=recv_sem,
            device_id=device, device_id_type=MESH).start()

    def wait(ref, sem):
        pltpu.make_async_copy(ref, ref, sem).wait()

    loads = {}
    for f in range(frags):
        for hf in both:
            at = pl.ds(hf * half_rows, half_rows)
            loads[f, hf] = [
                pltpu.make_async_copy(gw_hbm.at[f, at], gw.at[f, at], in_sems.at[f, hf, 0]),
                pltpu.make_async_copy(lw_hbm.at[0, f, at], lw.at[f, at], in_sems.at[f, hf, 1])]

    def start_loads(f):
        for hf in both:
            for copy in loads[f, hf]:
                copy.start()

    start_loads(0)

    near = [(0, 0, oc, oz) for oz in range(zs) for oc in range(2) if (oc, oz) != (0, 0)]
    far = [(ox, oy, 0, 0) for ox in range(RING) for oy in range(RING) if (ox, oy) != (0, 0)]
    greeted = near + [(1, 0, 0, 0), (-1, 0, 0, 0), (0, 1, 0, 0), (0, -1, 0, 0)]
    barrier = pltpu.get_barrier_semaphore()
    for partner in greeted:
        pl.semaphore_signal(barrier, inc=1, device_id=dev(*partner), device_id_type=MESH)
    pl.semaphore_wait(barrier, len(greeted))

    start_loads(1)
    mom_load = pltpu.make_async_copy(mom_hbm, mom, in_sems.at[0, 0, 2])
    mom_load.start()

    def difference(f, row, n, col):
        at = pl.ds(row, n)
        return gw[f, at, pl.ds(col, width)] - lw[f, at, pl.ds(col, width)].astype(F32)

    def load(f, hf):
        for copy in loads[f, hf]:
            copy.wait()

    def to_core(f, slot, hf):
        @pl.loop(0, RING)
        def _(j):
            col = column(hf, OFFSETS[slot], offset(j), 1 - core)
            ds[f, slot, hf, j] = difference(f, hf * half_rows, half_rows, col).astype(BF16)
        send(ds.at[f, slot, hf], dr.at[f, slot, hf], 0, core_sems.at[f, slot], dev(0, 0, 1))

    def from_core(f, slot):
        wait(dr.at[f, slot], core_sems.at[f, slot])

    def pair_sum(f, hf, slot, j, row, n):
        col = column(hf, OFFSETS[slot], offset(j), core)
        return (difference(f, hf * half_rows + row, n, col)
                + dr[f, slot, hf, j, pl.ds(row, n)].astype(F32))

    def ring1_far(f, hf):
        for q, way in ((0, 1), (1, -1)):
            @pl.loop(0, RING)
            def _(j):
                s_send[f, hf, 2, q, j] = pair_sum(f, hf, 3, j, q * quarter, quarter).astype(BF16)
            send(s_send.at[f, hf, 2, q], s_mid.at[f, hf, q], 1, mid_sems.at[f, hf], along(hf, way))

    def ring1_near(f, hf, slot):
        q, way = (1, 1) if slot == 1 else (0, -1)

        @pl.loop(0, RING)
        def _(j):
            s_send[f, hf, slot - 1, q, j] = pair_sum(f, hf, slot, j, q * quarter, quarter).astype(BF16)
        send(s_send.at[f, hf, slot - 1, q], s_end.at[f, hf, slot - 1, q], 1, end_sems.at[f, hf], along(hf, way))

    def ring1_middle(f, hf):
        wait(s_mid.at[f, hf], mid_sems.at[f, hf])
        for slot, q, way in ((1, 0, 1), (2, 1, -1)):
            @pl.loop(0, RING)
            def _(j):
                total = pair_sum(f, hf, slot, j, q * quarter, quarter) + s_mid[f, hf, q, j].astype(F32)
                s_send[f, hf, slot - 1, q, j] = total.astype(BF16)
            send(s_send.at[f, hf, slot - 1, q], s_end.at[f, hf, slot - 1, q], 1, end_sems.at[f, hf], along(hf, way))

    def ring2_open(f, hf):
        wait(s_end.at[f, hf], end_sems.at[f, hf])

        def whole(j, q):
            total = pair_sum(f, hf, 0, j, q * quarter, quarter)
            return total + s_end[f, hf, 0, q, j].astype(F32) + s_end[f, hf, 1, q, j].astype(F32)

        for slot in (3, 1, 2):
            for q in both:
                t_send[f, hf, slot - 1, pl.ds(q * quarter, quarter)] = whole(slot, q).astype(BF16)
            send(t_send.at[f, hf, slot - 1], t_end.at[f, hf, slot - 1], 2, end2_sems.at[f, hf],
                 along(1 - hf, OFFSETS[slot]))
        for q in both:
            tt[f, hf, pl.ds(q * quarter, quarter)] = whole(0, q)

    def ring2_close(f, hf):
        wait(t_end.at[f, hf], end2_sems.at[f, hf])
        part = tt[f, hf]
        for k in range(RING - 1):
            part = part + t_end[f, hf, k].astype(F32)
        part = part * (1.0 / (2 * RING * RING))
        av[f, pl.ds(hf * half_rows, half_rows)] = part
        square = jnp.sum((part * part).reshape(half_rows // 8, 8, width), axis=0)
        total = square[:, :128]
        for c in range(1, width // 128):
            total = total + square[:, c * 128:(c + 1) * 128]
        return total

    def exchange(f, stage, tiles, partners):
        n = len(partners)
        for i, partner in enumerate(partners):
            send(tiles.at[f, n], tiles.at[f, i], 3 + stage, norm_sems.at[f, stage], dev(*partner))

    def gathered(f, stage, tiles, partners):
        wait(tiles.at[f, pl.ds(0, len(partners))], norm_sems.at[f, stage])
        return jnp.sum(tiles[f], axis=0)

    def norm_open(f):
        n1[f, len(near)] = ring2_close(f, 0) + ring2_close(f, 1)
        exchange(f, 0, n1, near)

    def norm_middle(f):
        n2[f, len(far)] = gathered(f, 0, n1, near)
        exchange(f, 1, n2, far)

    def gather1(f, hf, slot, family, k):
        back = (None, 2, 1, 3)[slot]
        send(g.at[f, hf, 0, 0], g.at[f, hf, 0, back], family, gather_sems.at[f, hf, k], along(1 - hf, OFFSETS[slot]))

    def gather2(f, hf, at, k):
        for slot, back in ((1, 2), (2, 1)):
            send(g.at[f, hf, 0, at], g.at[f, hf, back, at], 6, gather_sems.at[f, hf, k], along(hf, OFFSETS[slot]))

    def gather2_pass(f, hf, at, n, k):
        wait(g.at[f, hf, pl.ds(1, 2), at], gather_sems.at[f, hf, k])
        for back, way, q in ((2, 1, 0), (1, -1, 1)):
            rows_at = pl.ds(q * quarter, quarter)
            send(g.at[f, hf, back, at, rows_at], g.at[f, hf, 3, at, rows_at], 6,
                 gather_sems.at[f, hf, 5], along(hf, way))

    FIRST, NEAR, LAST = pl.ds(0, 1), pl.ds(1, 2), pl.ds(3, 1)

    def outer(f):
        norm_squared = jnp.sum(gathered(f, 1, n2, far), axis=(0, 1), keepdims=True)
        factor = jnp.minimum(1.0, CLIP_LEVEL * jnp.sqrt(F32(count)) / jnp.sqrt(norm_squared + 1e-06))
        for hf in both:
            at = pl.ds(hf * half_rows, half_rows)
            clipped = av[f, at] * factor
            moment = OUTER_MOMENTUM * mom[f, at] + clipped
            mout[f, at] = moment
            g[f, hf, 0, 0] = (clipped + OUTER_MOMENTUM * moment).astype(BF16)
            gather1(f, hf, 1, 5, 0)
            gather1(f, hf, 2, 5, 0)
            gather1(f, hf, 3, 5, 1)
        for hf in both:
            gather2(f, hf, FIRST, 2)

    def gather1_near(f, hf):
        wait(g.at[f, hf, 0, NEAR], gather_sems.at[f, hf, 0])
        gather2(f, hf, NEAR, 3)

    def gather1_far(f, hf):
        wait(g.at[f, hf, 0, LAST], gather_sems.at[f, hf, 1])
        gather2(f, hf, LAST, 4)
        hand_over(f, hf, 0, 1, 0)

    def gather2_first(f, hf):
        gather2_pass(f, hf, FIRST, 1, 2)

    def gather2_near(f, hf):
        gather2_pass(f, hf, NEAR, 2, 3)

    def gather2_far(f, hf):
        gather2_pass(f, hf, LAST, 1, 4)
        hand_over(f, hf, 1, 2, 1)

    def gather2_last(f, hf):
        wait(g.at[f, hf, 3], gather_sems.at[f, hf, 5])
        hand_over(f, hf, 3, 1, 2)

    def hand_over(f, hf, slot, n, k):
        at = pl.ds(slot, n)
        send(g.at[f, hf, at], h.at[f, hf, at], 7, hand_sems.at[f, hf, k], dev(0, 0, 1))

    def refresh(f, hf, slot, blocks, c):
        at = pl.ds(hf * half_rows, half_rows)

        @pl.loop(0, RING)
        def _(j):
            col = pl.ds(column(hf, OFFSETS[slot], offset(j), c), width)
            gw[f, at, col] = gw[f, at, col] - OUTER_RATE * blocks[f, hf, slot, j].astype(F32)

    def own(f, *slots):
        for hf in both:
            for slot in slots:
                refresh(f, hf, slot, g, core)

    def other(f, k):
        slot, n = ((0, 1), (1, 2), (3, 1))[k]
        for hf in both:
            wait(h.at[f, hf, pl.ds(slot, n)], hand_sems.at[f, hf, k])
            for i in range(n):
                refresh(f, hf, slot + i, h, 1 - core)

    steps = []

    def step(work, *args):
        steps.append((work, args))

    def halves(work, f):
        for hf in both:
            work(f, hf)

    def core_step(f, *slots):
        for slot in slots:
            for hf in both:
                if slot == 3:
                    load(f, hf)
                to_core(f, slot, hf)

    def far_step(f):
        from_core(f, 3)
        halves(ring1_far, f)

    def near_step(f):
        for slot in (1, 2):
            from_core(f, slot)
            for hf in both:
                ring1_near(f, hf, slot)

    step(core_step, 0, 3, 1, 2, 0)
    step(far_step, 0)
    step(near_step, 0)
    step(core_step, 1, 3, 1, 2, 0)
    step(halves, ring1_middle, 0)
    step(far_step, 1)
    step(near_step, 1)
    step(from_core, 0, 0)
    step(halves, ring2_open, 0)
    step(halves, ring1_middle, 1)
    step(norm_open, 0)
    step(from_core, 1, 0)
    step(halves, ring2_open, 1)
    step(norm_middle, 0)
    step(norm_open, 1)
    step(mom_load.wait)
    step(norm_middle, 1)
    step(outer, 0)
    step(halves, gather1_near, 0)
    step(halves, gather1_far, 0)
    step(outer, 1)
    step(halves, gather2_first, 0)
    step(halves, gather1_near, 1)
    step(halves, gather1_far, 1)
    step(halves, gather2_near, 0)
    step(halves, gather2_first, 1)
    step(halves, gather2_far, 0)
    step(own, 0, 0)
    step(other, 0, 0)
    step(halves, gather2_near, 1)
    step(own, 1, 0)
    step(halves, gather2_last, 0)
    step(halves, gather2_far, 1)
    step(other, 1, 0)
    step(own, 0, 1, 2)
    step(other, 0, 1)
    step(own, 0, 3)
    step(halves, gather2_last, 1)
    step(other, 0, 2)
    step(own, 1, 1, 2)
    step(other, 1, 1)
    step(own, 1, 3)
    step(other, 1, 2)
    for work, args in steps:
        work(*args)

    wait(ds, send_sems.at[0])
    wait(s_send, send_sems.at[1])
    wait(t_send, send_sems.at[2])
    wait(n1.at[:, pl.ds(0, len(near))], send_sems.at[3])
    wait(n2.at[:, pl.ds(0, len(far))], send_sems.at[4])
    wait(g.at[:, :, 0, pl.ds(0, 3)], send_sems.at[5])
    wait(g.at[:, :, pl.ds(0, 3)], send_sems.at[6])
    wait(h, send_sems.at[7])


def synchronize(local_weights, global_weights, momentum):
    frags, rows, cols = global_weights.shape
    width = momentum.shape[2]
    zs = lax.axis_size("fsdp")
    assert lax.axis_size("replica") == 2 * RING * RING and frags == 2
    half_rows, quarter = rows // 2, rows // 4
    anywhere = pl.BlockSpec(memory_space=pl.ANY)
    in_vmem = pl.BlockSpec(memory_space=pltpu.VMEM)
    dma = pltpu.SemaphoreType.DMA
    return pl.pallas_call(
        functools.partial(kernel, zs, rows * zs * cols),
        out_shape=(pltpu.VMEM(global_weights.shape, F32), pltpu.VMEM(momentum.shape, F32)),
        in_specs=[anywhere] * 3,
        out_specs=(in_vmem, in_vmem),
        scratch_shapes=[
            pltpu.VMEM((frags, rows, cols), BF16),
            pltpu.VMEM((frags, rows, width), F32),
            pltpu.VMEM((frags, RING, 2, RING, half_rows, width), BF16),
            pltpu.VMEM((frags, RING, 2, RING, half_rows, width), BF16),
            pltpu.VMEM((frags, 2, RING - 1, 2, RING, quarter, width), BF16),
            pltpu.VMEM((frags, 2, 2, RING, quarter, width), BF16),
            pltpu.VMEM((frags, 2, 2, 2, RING, quarter, width), BF16),
            pltpu.VMEM((frags, 2, half_rows, width), F32),
            pltpu.VMEM((frags, 2, RING - 1, half_rows, width), BF16),
            pltpu.VMEM((frags, 2, RING - 1, half_rows, width), BF16),
            pltpu.VMEM((frags, rows, width), F32),
            pltpu.VMEM((frags, 2 * zs, 8, 128), F32),
            pltpu.VMEM((frags, RING * RING, 8, 128), F32),
            pltpu.VMEM((frags, 2, RING, RING, half_rows, width), BF16),
            pltpu.VMEM((frags, 2, RING, RING, half_rows, width), BF16),
            dma((frags, 2, 3)),
            dma((8,)),
            dma((frags, 2)),
            dma((frags, RING)),
            dma((frags, 2)),
            dma((frags, 2)),
            dma((frags, 2)),
            dma((frags, 2, 6)),
            dma((frags, 2, 3)),
        ],
        compiler_params=pltpu.CompilerParams(
            collective_id=0, has_side_effects=True, vmem_limit_bytes=50 * 2**20
        ),
        cost_estimate=pl.CostEstimate(flops=20 * rows * cols, bytes_accessed=20 * frags * rows * cols // 2, transcendentals=0),
    )(local_weights, global_weights, momentum)


def solution(mesh):
    return jax.shard_map(
        synchronize,
        mesh=mesh,
        in_specs=(
            P("replica", None, "fsdp", None),
            P(None, "fsdp", None),
            P(None, "fsdp", "replica"),
        ),
        out_specs=(P(None, "fsdp", None), P(None, "fsdp", "replica")),
        check_vma=False,
    )
```

```python
import functools

import jax
import jax.numpy as jnp
from jax import lax
from jax.experimental import pallas as pl
from jax.experimental.pallas import tpu as pltpu
from jax.sharding import PartitionSpec as P

OUTER_MOMENTUM = 0.9
OUTER_RATE = 0.7
CLIP_LEVEL = 1.0
MESH = pl.DeviceIdType.MESH
RING = 4
OFFSETS = (0, 1, -1, 2)
F32, BF16 = jnp.float32, jnp.bfloat16


def kernel(zs, count, lw_hbm, gw_hbm, mom_hbm, gw, mout,
           lw, mom, ds, dr, s_send, s_mid, s_end, tt, t_send, t_end, av, n1, n2, g, h,
           in_sems, send_sems, norm_sems, core_sems, mid_sems, end_sems, end2_sems, gather_sems, hand_sems):
    frags, rows, _ = gw.shape
    width = mom.shape[2]
    half_rows, quarter = rows // 2, rows // 4
    r = lax.axis_index("replica")
    z = lax.axis_index("fsdp")
    core = r % 2
    y = (r // 2) % RING
    x = r // (2 * RING)
    both = range(2)

    def dev(ox, oy, oc=0, oz=0):
        ax, ay = (x + ox) % RING, (y + oy) % RING
        return ((ax * RING + ay) * 2 + (core + oc) % 2, (z + oz) % zs)

    def along(axis, o):
        return dev(o, 0) if axis == 0 else dev(0, o)

    def column(hf, a, b, c):
        ax, ay = (x + (a if hf == 0 else b)) % RING, (y + (b if hf == 0 else a)) % RING
        return pl.multiple_of(((ax * RING + ay) * 2 + c) * width, width)

    def offset(slot):
        return jnp.where(slot == 2, -1, jnp.where(slot == 3, 2, slot))

    def send(src, dst, family, recv_sem, device):
        pltpu.make_async_remote_copy(
            src_ref=src, dst_ref=dst, send_sem=send_sems.at[family], recv_sem=recv_sem,
            device_id=device, device_id_type=MESH).start()

    def wait(ref, sem):
        pltpu.make_async_copy(ref, ref, sem).wait()

    loads = {}
    for f in range(frags):
        for hf in both:
            at = pl.ds(hf * half_rows, half_rows)
            loads[f, hf] = [
                pltpu.make_async_copy(gw_hbm.at[f, at], gw.at[f, at], in_sems.at[f, hf, 0]),
                pltpu.make_async_copy(lw_hbm.at[0, f, at], lw.at[f, at], in_sems.at[f, hf, 1])]

    def start_loads(f):
        for hf in both:
            for copy in loads[f, hf]:
                copy.start()

    mom_load = pltpu.make_async_copy(mom_hbm, mom, in_sems.at[0, 0, 2])
    mom_load.start()
    start_loads(0)

    near = [(0, 0, oc, oz) for oz in range(zs) for oc in range(2) if (oc, oz) != (0, 0)]
    far = [(ox, oy, 0, 0) for ox in range(RING) for oy in range(RING) if (ox, oy) != (0, 0)]
    greeted = near + [(o, 0, 0, 0) for o in OFFSETS[1:]] + [(0, o, 0, 0) for o in OFFSETS[1:]]
    barrier = pltpu.get_barrier_semaphore()
    for partner in greeted:
        pl.semaphore_signal(barrier, inc=1, device_id=dev(*partner), device_id_type=MESH)
    pl.semaphore_wait(barrier, len(greeted))

    start_loads(1)

    def difference(f, row, n, col):
        at = pl.ds(row, n)
        return gw[f, at, pl.ds(col, width)] - lw[f, at, pl.ds(col, width)].astype(F32)

    def load(f, hf):
        for copy in loads[f, hf]:
            copy.wait()

    def to_core(f, slot, hf):
        @pl.loop(0, RING)
        def _(j):
            col = column(hf, OFFSETS[slot], offset(j), 1 - core)
            ds[f, slot, hf, j] = difference(f, hf * half_rows, half_rows, col).astype(BF16)
        send(ds.at[f, slot, hf], dr.at[f, slot, hf], 0, core_sems.at[f, slot], dev(0, 0, 1))

    def from_core(f, slot):
        wait(dr.at[f, slot], core_sems.at[f, slot])

    def pair_sum(f, hf, slot, j, row, n):
        col = column(hf, OFFSETS[slot], offset(j), core)
        return (difference(f, hf * half_rows + row, n, col)
                + dr[f, slot, hf, j, pl.ds(row, n)].astype(F32))

    def ring1_far(f, hf):
        for q, way in ((0, 1), (1, -1)):
            @pl.loop(0, RING)
            def _(j):
                s_send[f, hf, 2, q, j] = pair_sum(f, hf, 3, j, q * quarter, quarter).astype(BF16)
            send(s_send.at[f, hf, 2, q], s_mid.at[f, hf, q], 1, mid_sems.at[f, hf], along(hf, way))

    def ring1_near(f, hf, slot):
        q, way = (1, 1) if slot == 1 else (0, -1)

        @pl.loop(0, RING)
        def _(j):
            s_send[f, hf, slot - 1, q, j] = pair_sum(f, hf, slot, j, q * quarter, quarter).astype(BF16)
        send(s_send.at[f, hf, slot - 1, q], s_end.at[f, hf, slot - 1, q], 1, end_sems.at[f, hf], along(hf, way))

    def ring1_middle(f, hf):
        wait(s_mid.at[f, hf], mid_sems.at[f, hf])
        for slot, q, way in ((1, 0, 1), (2, 1, -1)):
            @pl.loop(0, RING)
            def _(j):
                total = pair_sum(f, hf, slot, j, q * quarter, quarter) + s_mid[f, hf, q, j].astype(F32)
                s_send[f, hf, slot - 1, q, j] = total.astype(BF16)
            send(s_send.at[f, hf, slot - 1, q], s_end.at[f, hf, slot - 1, q], 1, end_sems.at[f, hf], along(hf, way))

    def ring2_open(f, hf):
        wait(s_end.at[f, hf], end_sems.at[f, hf])

        def whole(j, q):
            total = pair_sum(f, hf, 0, j, q * quarter, quarter)
            return total + s_end[f, hf, 0, q, j].astype(F32) + s_end[f, hf, 1, q, j].astype(F32)

        for slot in (3, 1, 2):
            for q in both:
                t_send[f, hf, slot - 1, pl.ds(q * quarter, quarter)] = whole(slot, q).astype(BF16)
            send(t_send.at[f, hf, slot - 1], t_end.at[f, hf, slot - 1], 2, end2_sems.at[f, hf],
                 along(1 - hf, OFFSETS[slot]))
        for q in both:
            tt[f, hf, pl.ds(q * quarter, quarter)] = whole(0, q)

    def ring2_close(f, hf):
        wait(t_end.at[f, hf], end2_sems.at[f, hf])
        part = tt[f, hf]
        for k in range(RING - 1):
            part = part + t_end[f, hf, k].astype(F32)
        part = part * (1.0 / (2 * RING * RING))
        av[f, pl.ds(hf * half_rows, half_rows)] = part
        return part

    def tile(part):
        square = jnp.sum((part * part).reshape(half_rows // 8, 8, width), axis=0)
        total = square[:, :128]
        for c in range(1, width // 128):
            total = total + square[:, c * 128:(c + 1) * 128]
        return total

    def exchange(f, stage, tiles, me, partners):
        for partner in partners:
            send(tiles.at[f, me], tiles.at[f, me], 3 + stage, norm_sems.at[f, stage], dev(*partner))

    def gathered(f, stage, tiles, partners):
        wait(tiles.at[f, pl.ds(0, len(partners))], norm_sems.at[f, stage])
        return jnp.sum(tiles[f], axis=0)

    def norm_open(f):
        at = pl.ds(half_rows, half_rows)
        n1[f, z * 2 + core] = tile(av[f, pl.ds(0, half_rows)]) + tile(av[f, at])
        exchange(f, 0, n1, z * 2 + core, near)

    def norm_middle(f):
        n2[f, x * RING + y] = gathered(f, 0, n1, near)
        exchange(f, 1, n2, x * RING + y, far)

    def factor_of(f):
        norm_squared = jnp.sum(gathered(f, 1, n2, far), axis=(0, 1), keepdims=True)
        return jnp.minimum(1.0, CLIP_LEVEL * jnp.sqrt(F32(count)) / jnp.sqrt(norm_squared + 1e-06))

    STEP, AVERAGE, MOMENT = 0, 1, 2
    FIRST, NEAR, LAST = pl.ds(0, 1), pl.ds(1, 2), pl.ds(3, 1)

    def gather1(s, hf, slot, k):
        back = (None, 2, 1, 3)[slot]
        send(g.at[s, hf, 0, 0], g.at[s, hf, 0, back], 5, gather_sems.at[s, hf, k], along(1 - hf, OFFSETS[slot]))

    def gather2(s, hf, at, k):
        for slot, back in ((1, 2), (2, 1)):
            send(g.at[s, hf, 0, at], g.at[s, hf, back, at], 6, gather_sems.at[s, hf, k], along(hf, OFFSETS[slot]))

    def gather2_pass(s, hf, at, k):
        wait(g.at[s, hf, pl.ds(1, 2), at], gather_sems.at[s, hf, k])
        for back, way, q in ((2, 1, 0), (1, -1, 1)):
            rows_at = pl.ds(q * quarter, quarter)
            send(g.at[s, hf, back, at, rows_at], g.at[s, hf, 3, at, rows_at], 6,
                 gather_sems.at[s, hf, 5], along(hf, way))

    def spread(s):
        for hf in both:
            for slot, k in ((1, 0), (2, 0), (3, 1)):
                gather1(s, hf, slot, k)
        for hf in both:
            gather2(s, hf, FIRST, 2)

    def spread_moment():
        mom_load.wait()
        for hf in both:
            g[MOMENT, hf, 0, 0] = mom[1, pl.ds(hf * half_rows, half_rows)].astype(BF16)
        spread(MOMENT)

    def spread_average():
        for hf in both:
            g[AVERAGE, hf, 0, 0] = ring2_close(1, hf).astype(BF16)
        spread(AVERAGE)

    def spread_step():
        factor = factor_of(0)
        for hf in both:
            at = pl.ds(hf * half_rows, half_rows)
            clipped = av[0, at] * factor
            moment = OUTER_MOMENTUM * mom[0, at] + clipped
            mout[0, at] = moment
            g[STEP, hf, 0, 0] = (clipped + OUTER_MOMENTUM * moment).astype(BF16)
        spread(STEP)

    scales = {STEP: OUTER_RATE, MOMENT: OUTER_RATE * OUTER_MOMENTUM * OUTER_MOMENTUM}

    def clip_average():
        factor = factor_of(1)
        mout[1] = OUTER_MOMENTUM * mom[1] + av[1] * factor
        scales[AVERAGE] = OUTER_RATE * (1.0 + OUTER_MOMENTUM) * factor

    def gather1_near(s, hf):
        wait(g.at[s, hf, 0, NEAR], gather_sems.at[s, hf, 0])
        gather2(s, hf, NEAR, 3)

    def gather1_far(s, hf):
        wait(g.at[s, hf, 0, LAST], gather_sems.at[s, hf, 1])
        gather2(s, hf, LAST, 4)
        hand_over(s, hf, 0, 1, 0)

    def gather2_first(s, hf):
        gather2_pass(s, hf, FIRST, 2)

    def gather2_near(s, hf):
        gather2_pass(s, hf, NEAR, 3)

    def gather2_far(s, hf):
        gather2_pass(s, hf, LAST, 4)
        hand_over(s, hf, 1, 2, 1)

    def gather2_last(s, hf):
        wait(g.at[s, hf, 3], gather_sems.at[s, hf, 5])
        hand_over(s, hf, 3, 1, 2)

    def hand_over(s, hf, slot, n, k):
        at = pl.ds(slot, n)
        send(g.at[s, hf, at], h.at[s, hf, at], 7, hand_sems.at[s, hf, k], dev(0, 0, 1))

    def refresh(s, hf, slot, blocks, c):
        f = 0 if s == STEP else 1
        at = pl.ds(hf * half_rows, half_rows)
        scale = scales[s]

        @pl.loop(0, RING)
        def _(j):
            col = pl.ds(column(hf, OFFSETS[slot], offset(j), c), width)
            gw[f, at, col] = gw[f, at, col] - scale * blocks[s, hf, slot, j].astype(F32)

    def own(s, *slots):
        for hf in both:
            for slot in slots:
                refresh(s, hf, slot, g, core)

    def other(s, k):
        slot, n = ((0, 1), (1, 2), (3, 1))[k]
        for hf in both:
            wait(h.at[s, hf, pl.ds(slot, n)], hand_sems.at[s, hf, k])
            for i in range(n):
                refresh(s, hf, slot + i, h, 1 - core)

    steps = []

    def step(work, *args):
        steps.append((work, args))

    def halves(work, f):
        for hf in both:
            work(f, hf)

    def core_step(f, slot):
        for hf in both:
            if slot == 3:
                load(f, hf)
            to_core(f, slot, hf)

    def far_step(f):
        from_core(f, 3)
        halves(ring1_far, f)

    def near_step(f, slot):
        from_core(f, slot)
        for hf in both:
            ring1_near(f, hf, slot)

    def open_step(f):
        from_core(f, 0)
        halves(ring2_open, f)

    def close_step(f):
        for hf in both:
            ring2_close(f, hf)

    step(core_step, 0, 3)
    step(core_step, 0, 1)
    step(spread_moment)
    step(far_step, 0)
    step(core_step, 0, 2)
    step(near_step, 0, 1)
    step(core_step, 0, 0)
    step(near_step, 0, 2)
    step(core_step, 1, 3)
    step(core_step, 1, 1)
    step(core_step, 1, 2)
    step(far_step, 1)
    step(core_step, 1, 0)
    step(halves, ring1_middle, 0)
    step(near_step, 1, 1)
    step(near_step, 1, 2)
    step(halves, ring1_middle, 1)
    step(open_step, 0)
    step(halves, gather1_near, MOMENT)
    step(open_step, 1)
    step(halves, gather1_far, MOMENT)
    step(halves, gather2_first, MOMENT)
    step(close_step, 0)
    step(norm_open, 0)
    step(halves, gather2_near, MOMENT)
    step(spread_average)
    step(norm_open, 1)
    step(norm_middle, 0)
    step(halves, gather2_far, MOMENT)
    step(own, MOMENT, 0)
    step(halves, gather1_near, AVERAGE)
    step(halves, gather1_far, AVERAGE)
    step(norm_middle, 1)
    step(spread_step)
    step(halves, gather2_first, AVERAGE)
    step(halves, gather2_last, MOMENT)
    step(other, MOMENT, 0)
    step(halves, gather2_near, AVERAGE)
    step(halves, gather1_near, STEP)
    step(halves, gather1_far, STEP)
    step(halves, gather2_far, AVERAGE)
    step(halves, gather2_first, STEP)
    step(clip_average)
    step(own, MOMENT, 1, 2, 3)
    step(other, MOMENT, 1)
    step(halves, gather2_near, STEP)
    step(other, MOMENT, 2)
    step(own, AVERAGE, 0)
    step(other, AVERAGE, 0)
    step(halves, gather2_last, AVERAGE)
    step(halves, gather2_far, STEP)
    step(own, AVERAGE, 1, 2)
    step(other, AVERAGE, 1)
    step(own, STEP, 0)
    step(other, STEP, 0)
    step(own, AVERAGE, 3)
    step(other, AVERAGE, 2)
    step(halves, gather2_last, STEP)
    step(own, STEP, 1, 2)
    step(other, STEP, 1)
    step(own, STEP, 3)
    step(other, STEP, 2)
    for work, args in steps:
        work(*args)

    wait(ds, send_sems.at[0])
    wait(s_send, send_sems.at[1])
    wait(t_send, send_sems.at[2])
    wait(n1.at[:, pl.ds(0, len(near))], send_sems.at[3])
    wait(n2.at[:, pl.ds(0, len(far))], send_sems.at[4])
    wait(g.at[:, :, 0, pl.ds(0, 3)], send_sems.at[5])
    wait(g.at[:, :, pl.ds(0, 3)], send_sems.at[6])
    wait(h, send_sems.at[7])


def synchronize(local_weights, global_weights, momentum):
    frags, rows, cols = global_weights.shape
    width = momentum.shape[2]
    zs = lax.axis_size("fsdp")
    assert lax.axis_size("replica") == 2 * RING * RING and frags == 2
    half_rows, quarter = rows // 2, rows // 4
    anywhere = pl.BlockSpec(memory_space=pl.ANY)
    in_vmem = pl.BlockSpec(memory_space=pltpu.VMEM)
    dma = pltpu.SemaphoreType.DMA
    return pl.pallas_call(
        functools.partial(kernel, zs, rows * zs * cols),
        out_shape=(pltpu.VMEM(global_weights.shape, F32), pltpu.VMEM(momentum.shape, F32)),
        in_specs=[anywhere] * 3,
        out_specs=(in_vmem, in_vmem),
        scratch_shapes=[
            pltpu.VMEM((frags, rows, cols), BF16),
            pltpu.VMEM((frags, rows, width), F32),
            pltpu.VMEM((frags, RING, 2, RING, half_rows, width), BF16),
            pltpu.VMEM((frags, RING, 2, RING, half_rows, width), BF16),
            pltpu.VMEM((frags, 2, RING - 1, 2, RING, quarter, width), BF16),
            pltpu.VMEM((frags, 2, 2, RING, quarter, width), BF16),
            pltpu.VMEM((frags, 2, 2, 2, RING, quarter, width), BF16),
            pltpu.VMEM((frags, 2, half_rows, width), F32),
            pltpu.VMEM((frags, 2, RING - 1, half_rows, width), BF16),
            pltpu.VMEM((frags, 2, RING - 1, half_rows, width), BF16),
            pltpu.VMEM((frags, rows, width), F32),
            pltpu.VMEM((frags, 2 * zs, 8, 128), F32),
            pltpu.VMEM((frags, RING * RING, 8, 128), F32),
            pltpu.VMEM((frags + 1, 2, RING, RING, half_rows, width), BF16),
            pltpu.VMEM((frags + 1, 2, RING, RING, half_rows, width), BF16),
            dma((frags, 2, 3)),
            dma((8,)),
            dma((frags, 2)),
            dma((frags, RING)),
            dma((frags, 2)),
            dma((frags, 2)),
            dma((frags, 2)),
            dma((frags + 1, 2, 6)),
            dma((frags + 1, 2, 3)),
        ],
        compiler_params=pltpu.CompilerParams(
            collective_id=0, has_side_effects=True, vmem_limit_bytes=50 * 2**20
        ),
        cost_estimate=pl.CostEstimate(flops=20 * rows * cols, bytes_accessed=20 * frags * rows * cols // 2, transcendentals=0),
    )(local_weights, global_weights, momentum)


def solution(mesh):
    return jax.shard_map(
        synchronize,
        mesh=mesh,
        in_specs=(
            P("replica", None, "fsdp", None),
            P(None, "fsdp", None),
            P(None, "fsdp", "replica"),
        ),
        out_specs=(P(None, "fsdp", None), P(None, "fsdp", "replica")),
        check_vma=False,
    )
```

```python
import functools

import jax
import jax.numpy as jnp
from jax import lax
from jax.experimental import pallas as pl
from jax.experimental.pallas import tpu as pltpu
from jax.sharding import PartitionSpec as P

OUTER_MOMENTUM = 0.9
OUTER_RATE = 0.7
CLIP_LEVEL = 1.0
MESH = pl.DeviceIdType.MESH
RING = 4
OFFSETS = (0, 1, -1, 2)
F32, BF16 = jnp.float32, jnp.bfloat16


def kernel(zs, count, lw_hbm, gw_hbm, mom_hbm, gw, mout,
           lw, mom, ds, dr, s_send, s_mid, s_end, tt, t_send, t_end, av, n1, n2, g, h,
           in_sems, mom_sem, send_sems, norm_sems, core_sems, mid_sems, end_sems, end2_sems, gather_sems, hand_sems):
    frags, rows, _ = gw.shape
    width = mom.shape[2]
    half_rows, quarter = rows // 2, rows // 4
    r = lax.axis_index("replica")
    z = lax.axis_index("fsdp")
    core = r % 2
    y = (r // 2) % RING
    x = r // (2 * RING)
    both = range(2)

    def dev(ox, oy, oc=0, oz=0):
        ax, ay = (x + ox) % RING, (y + oy) % RING
        return ((ax * RING + ay) * 2 + (core + oc) % 2, (z + oz) % zs)

    def along(axis, o):
        return dev(o, 0) if axis == 0 else dev(0, o)

    def column(hf, a, b, c):
        ax, ay = (x + (a if hf == 0 else b)) % RING, (y + (b if hf == 0 else a)) % RING
        return pl.multiple_of(((ax * RING + ay) * 2 + c) * width, width)

    def offset(slot):
        return jnp.where(slot == 2, -1, jnp.where(slot == 3, 2, slot))

    def send(src, dst, family, recv_sem, device):
        pltpu.make_async_remote_copy(
            src_ref=src, dst_ref=dst, send_sem=send_sems.at[family], recv_sem=recv_sem,
            device_id=device, device_id_type=MESH).start()

    def wait(ref, sem):
        pltpu.make_async_copy(ref, ref, sem).wait()

    loads = {}
    for f in range(frags):
        for hf in both:
            at = pl.ds(hf * half_rows, half_rows)
            loads[f, hf] = [
                pltpu.make_async_copy(gw_hbm.at[f, at], gw.at[f, at], in_sems.at[f, hf, 0]),
                pltpu.make_async_copy(lw_hbm.at[0, f, at], lw.at[f, at], in_sems.at[f, hf, 1])]

    def start_loads(f):
        for hf in both:
            for copy in loads[f, hf]:
                copy.start()

    mom_load = pltpu.make_async_copy(mom_hbm, mom, mom_sem)
    mom_load.start()
    start_loads(0)

    near = [(0, 0, oc, oz) for oz in range(zs) for oc in range(2) if (oc, oz) != (0, 0)]
    far = [(ox, oy, 0, 0) for ox in range(RING) for oy in range(RING) if (ox, oy) != (0, 0)]
    greeted = near + [(o, 0, 0, 0) for o in OFFSETS[1:]] + [(0, o, 0, 0) for o in OFFSETS[1:]]
    barrier = pltpu.get_barrier_semaphore()
    for partner in greeted:
        pl.semaphore_signal(barrier, inc=1, device_id=dev(*partner), device_id_type=MESH)
    pl.semaphore_wait(barrier, len(greeted))

    start_loads(1)

    def difference(f, row, n, col):
        at = pl.ds(row, n)
        return gw[f, at, pl.ds(col, width)] - lw[f, at, pl.ds(col, width)].astype(F32)

    def load(f, hf):
        for copy in loads[f, hf]:
            copy.wait()

    def to_core(f, slot, hf):
        @pl.loop(0, RING)
        def _(j):
            col = column(hf, OFFSETS[slot], offset(j), 1 - core)
            ds[f, slot, hf, j] = difference(f, hf * half_rows, half_rows, col).astype(BF16)
        send(ds.at[f, slot, hf], dr.at[f, slot, hf], 0, core_sems.at[f, slot], dev(0, 0, 1))

    def from_core(f, slot):
        wait(dr.at[f, slot], core_sems.at[f, slot])

    def pair_sum(f, hf, slot, j, row, n):
        col = column(hf, OFFSETS[slot], offset(j), core)
        return (difference(f, hf * half_rows + row, n, col)
                + dr[f, slot, hf, j, pl.ds(row, n)].astype(F32))

    def ring1_far(f, hf):
        for q, way in ((0, 1), (1, -1)):
            @pl.loop(0, RING)
            def _(j):
                s_send[f, hf, 2, q, j] = pair_sum(f, hf, 3, j, q * quarter, quarter).astype(BF16)
            send(s_send.at[f, hf, 2, q], s_mid.at[f, hf, q], 1, mid_sems.at[f], along(hf, way))

    def ring1_near(f, hf, slot):
        q, way = (1, 1) if slot == 1 else (0, -1)

        @pl.loop(0, RING)
        def _(j):
            s_send[f, hf, slot - 1, q, j] = pair_sum(f, hf, slot, j, q * quarter, quarter).astype(BF16)
        send(s_send.at[f, hf, slot - 1, q], s_end.at[f, hf, slot - 1, q], 1, end_sems.at[f], along(hf, way))

    def ring1_middle(f, hf):
        for slot, q, way in ((1, 0, 1), (2, 1, -1)):
            @pl.loop(0, RING)
            def _(j):
                total = pair_sum(f, hf, slot, j, q * quarter, quarter) + s_mid[f, hf, q, j].astype(F32)
                s_send[f, hf, slot - 1, q, j] = total.astype(BF16)
            send(s_send.at[f, hf, slot - 1, q], s_end.at[f, hf, slot - 1, q], 1, end_sems.at[f], along(hf, way))

    def ring2_open(f, hf):
        def whole(j, q):
            total = pair_sum(f, hf, 0, j, q * quarter, quarter)
            return total + s_end[f, hf, 0, q, j].astype(F32) + s_end[f, hf, 1, q, j].astype(F32)

        for slot in (3, 1, 2):
            for q in both:
                t_send[f, hf, slot - 1, pl.ds(q * quarter, quarter)] = whole(slot, q).astype(BF16)
            send(t_send.at[f, hf, slot - 1], t_end.at[f, hf, slot - 1], 2, end2_sems.at[f],
                 along(1 - hf, OFFSETS[slot]))
        for q in both:
            tt[f, hf, pl.ds(q * quarter, quarter)] = whole(0, q)

    def ring2_close(f, hf):
        part = tt[f, hf]
        for k in range(RING - 1):
            part = part + t_end[f, hf, k].astype(F32)
        part = part * (1.0 / (2 * RING * RING))
        av[f, pl.ds(hf * half_rows, half_rows)] = part
        return part

    def tile(part):
        square = jnp.sum((part * part).reshape(half_rows // 8, 8, width), axis=0)
        total = square[:, :128]
        for c in range(1, width // 128):
            total = total + square[:, c * 128:(c + 1) * 128]
        return total

    def exchange(f, stage, tiles, me, partners):
        for partner in partners:
            send(tiles.at[f, me], tiles.at[f, me], 3 + stage, norm_sems.at[f, stage], dev(*partner))

    def gathered(f, stage, tiles, partners):
        wait(tiles.at[f, pl.ds(0, len(partners))], norm_sems.at[f, stage])
        return jnp.sum(tiles[f], axis=0)

    def norm_open(f):
        at = pl.ds(half_rows, half_rows)
        n1[f, z * 2 + core] = tile(av[f, pl.ds(0, half_rows)]) + tile(av[f, at])
        exchange(f, 0, n1, z * 2 + core, near)

    def norm_middle(f):
        n2[f, x * RING + y] = gathered(f, 0, n1, near)
        exchange(f, 1, n2, x * RING + y, far)

    def factor_of(f):
        norm_squared = jnp.sum(gathered(f, 1, n2, far), axis=(0, 1), keepdims=True)
        return jnp.minimum(1.0, CLIP_LEVEL * jnp.sqrt(F32(count)) / jnp.sqrt(norm_squared + 1e-06))

    STEP, AVERAGE, MOMENT = 0, 1, 2
    FIRST, NEAR, LAST = pl.ds(0, 1), pl.ds(1, 2), pl.ds(3, 1)

    def gather1(s, hf, slot, k):
        back = (None, 2, 1, 3)[slot]
        send(g.at[s, hf, 0, 0], g.at[s, hf, 0, back], 5, gather_sems.at[s, k], along(1 - hf, OFFSETS[slot]))

    def gather2(s, hf, at, k):
        for slot, back in ((1, 2), (2, 1)):
            send(g.at[s, hf, 0, at], g.at[s, hf, back, at], 6, gather_sems.at[s, k], along(hf, OFFSETS[slot]))

    def gather2_pass(s, hf, at, k):
        for back, way, q in ((2, 1, 0), (1, -1, 1)):
            rows_at = pl.ds(q * quarter, quarter)
            send(g.at[s, hf, back, at, rows_at], g.at[s, hf, 3, at, rows_at], 6,
                 gather_sems.at[s, 5], along(hf, way))

    def spread(s):
        for hf in both:
            for slot, k in ((1, 0), (2, 0), (3, 1)):
                gather1(s, hf, slot, k)
        for hf in both:
            gather2(s, hf, FIRST, 2)

    def spread_moment():
        mom_load.wait()
        for hf in both:
            g[MOMENT, hf, 0, 0] = mom[1, pl.ds(hf * half_rows, half_rows)].astype(BF16)
        spread(MOMENT)

    def spread_average():
        wait(t_end.at[1], end2_sems.at[1])
        for hf in both:
            g[AVERAGE, hf, 0, 0] = ring2_close(1, hf).astype(BF16)
        spread(AVERAGE)

    def spread_step():
        factor = factor_of(0)
        for hf in both:
            at = pl.ds(hf * half_rows, half_rows)
            clipped = av[0, at] * factor
            moment = OUTER_MOMENTUM * mom[0, at] + clipped
            mout[0, at] = moment
            g[STEP, hf, 0, 0] = (clipped + OUTER_MOMENTUM * moment).astype(BF16)
        spread(STEP)

    scales = {STEP: OUTER_RATE, MOMENT: OUTER_RATE * OUTER_MOMENTUM * OUTER_MOMENTUM}

    def clip_average():
        factor = factor_of(1)
        mout[1] = OUTER_MOMENTUM * mom[1] + av[1] * factor
        scales[AVERAGE] = OUTER_RATE * (1.0 + OUTER_MOMENTUM) * factor

    def gather1_near(s):
        wait(g.at[s, :, 0, NEAR], gather_sems.at[s, 0])
        for hf in both:
            gather2(s, hf, NEAR, 3)

    def gather1_far(s):
        wait(g.at[s, :, 0, LAST], gather_sems.at[s, 1])
        for hf in both:
            gather2(s, hf, LAST, 4)
        for hf in both:
            hand_over(s, hf, 0, 1, 0)

    def gather2_passes(s, at, k):
        wait(g.at[s, :, pl.ds(1, 2), at], gather_sems.at[s, k])
        for hf in both:
            gather2_pass(s, hf, at, k)

    def gather2_first(s):
        gather2_passes(s, FIRST, 2)

    def gather2_near(s):
        gather2_passes(s, NEAR, 3)

    def gather2_far(s):
        gather2_passes(s, LAST, 4)
        for hf in both:
            hand_over(s, hf, 1, 2, 1)

    def gather2_last(s):
        wait(g.at[s, :, 3], gather_sems.at[s, 5])
        for hf in both:
            hand_over(s, hf, 3, 1, 2)

    def hand_over(s, hf, slot, n, k):
        at = pl.ds(slot, n)
        send(g.at[s, hf, at], h.at[s, hf, at], 7, hand_sems.at[s, k], dev(0, 0, 1))

    def refresh(s, hf, slot, blocks, c):
        f = 0 if s == STEP else 1
        at = pl.ds(hf * half_rows, half_rows)
        scale = scales[s]

        @pl.loop(0, RING)
        def _(j):
            col = pl.ds(column(hf, OFFSETS[slot], offset(j), c), width)
            gw[f, at, col] = gw[f, at, col] - scale * blocks[s, hf, slot, j].astype(F32)

    def own(s, *slots):
        for hf in both:
            for slot in slots:
                refresh(s, hf, slot, g, core)

    def other(s, k):
        slot, n = ((0, 1), (1, 2), (3, 1))[k]
        wait(h.at[s, :, pl.ds(slot, n)], hand_sems.at[s, k])
        for hf in both:
            for i in range(n):
                refresh(s, hf, slot + i, h, 1 - core)

    steps = []

    def step(work, *args):
        steps.append((work, args))

    def halves(work, f):
        for hf in both:
            work(f, hf)

    def core_step(f, slot):
        for hf in both:
            if slot == 3:
                load(f, hf)
            to_core(f, slot, hf)

    def far_step(f):
        from_core(f, 3)
        halves(ring1_far, f)

    def near_step(f, slot):
        from_core(f, slot)
        for hf in both:
            ring1_near(f, hf, slot)

    def middle_step(f):
        wait(s_mid.at[f], mid_sems.at[f])
        halves(ring1_middle, f)

    def open_step(f):
        from_core(f, 0)
        wait(s_end.at[f], end_sems.at[f])
        halves(ring2_open, f)

    def close_step(f):
        wait(t_end.at[f], end2_sems.at[f])
        halves(ring2_close, f)

    step(spread_moment)
    step(core_step, 0, 3)
    step(core_step, 0, 1)
    step(far_step, 0)
    step(core_step, 0, 2)
    step(near_step, 0, 1)
    step(core_step, 0, 0)
    step(near_step, 0, 2)
    step(core_step, 1, 3)
    step(core_step, 1, 1)
    step(core_step, 1, 2)
    step(far_step, 1)
    step(core_step, 1, 0)
    step(middle_step, 0)
    step(near_step, 1, 1)
    step(near_step, 1, 2)
    step(middle_step, 1)
    step(open_step, 0)
    step(gather1_near, MOMENT)
    step(open_step, 1)
    step(close_step, 0)
    step(norm_open, 0)
    step(gather1_far, MOMENT)
    step(gather2_first, MOMENT)
    step(gather2_near, MOMENT)
    step(spread_average)
    step(norm_middle, 0)
    step(norm_open, 1)
    step(gather2_far, MOMENT)
    step(own, MOMENT, 0)
    step(gather1_near, AVERAGE)
    step(norm_middle, 1)
    step(gather1_far, AVERAGE)
    step(gather2_first, AVERAGE)
    step(spread_step)
    step(gather2_last, MOMENT)
    step(other, MOMENT, 0)
    step(gather2_near, AVERAGE)
    step(gather2_far, AVERAGE)
    step(gather1_near, STEP)
    step(gather1_far, STEP)
    step(own, MOMENT, 1)
    step(gather2_first, STEP)
    step(clip_average)
    step(own, MOMENT, 2, 3)
    step(other, MOMENT, 1)
    step(gather2_last, AVERAGE)
    step(gather2_near, STEP)
    step(gather2_far, STEP)
    step(other, MOMENT, 2)
    step(own, AVERAGE, 0, 1, 2)
    step(other, AVERAGE, 0)
    step(own, STEP, 0)
    step(gather2_last, STEP)
    step(other, STEP, 0)
    step(other, AVERAGE, 1)
    step(own, AVERAGE, 3)
    step(other, AVERAGE, 2)
    step(own, STEP, 1, 2)
    step(other, STEP, 1)
    step(own, STEP, 3)
    step(other, STEP, 2)
    for work, args in steps:
        work(*args)

    wait(ds, send_sems.at[0])
    wait(s_send, send_sems.at[1])
    wait(t_send, send_sems.at[2])
    wait(n1.at[:, pl.ds(0, len(near))], send_sems.at[3])
    wait(n2.at[:, pl.ds(0, len(far))], send_sems.at[4])
    wait(g.at[:, :, 0, pl.ds(0, 3)], send_sems.at[5])
    wait(g.at[:, :, pl.ds(0, 3)], send_sems.at[6])
    wait(h, send_sems.at[7])


def synchronize(local_weights, global_weights, momentum):
    frags, rows, cols = global_weights.shape
    width = momentum.shape[2]
    zs = lax.axis_size("fsdp")
    assert lax.axis_size("replica") == 2 * RING * RING and frags == 2
    half_rows, quarter = rows // 2, rows // 4
    anywhere = pl.BlockSpec(memory_space=pl.ANY)
    in_vmem = pl.BlockSpec(memory_space=pltpu.VMEM)
    dma = pltpu.SemaphoreType.DMA
    return pl.pallas_call(
        functools.partial(kernel, zs, rows * zs * cols),
        out_shape=(pltpu.VMEM(global_weights.shape, F32), pltpu.VMEM(momentum.shape, F32)),
        in_specs=[anywhere] * 3,
        out_specs=(in_vmem, in_vmem),
        scratch_shapes=[
            pltpu.VMEM((frags, rows, cols), BF16),
            pltpu.VMEM((frags, rows, width), F32),
            pltpu.VMEM((frags, RING, 2, RING, half_rows, width), BF16),
            pltpu.VMEM((frags, RING, 2, RING, half_rows, width), BF16),
            pltpu.VMEM((frags, 2, RING - 1, 2, RING, quarter, width), BF16),
            pltpu.VMEM((frags, 2, 2, RING, quarter, width), BF16),
            pltpu.VMEM((frags, 2, 2, 2, RING, quarter, width), BF16),
            pltpu.VMEM((frags, 2, half_rows, width), F32),
            pltpu.VMEM((frags, 2, RING - 1, half_rows, width), BF16),
            pltpu.VMEM((frags, 2, RING - 1, half_rows, width), BF16),
            pltpu.VMEM((frags, rows, width), F32),
            pltpu.VMEM((frags, 2 * zs, 8, 128), F32),
            pltpu.VMEM((frags, RING * RING, 8, 128), F32),
            pltpu.VMEM((frags + 1, 2, RING, RING, half_rows, width), BF16),
            pltpu.VMEM((frags + 1, 2, RING, RING, half_rows, width), BF16),
            dma((frags, 2, 2)),
            dma,
            dma((8,)),
            dma((frags, 2)),
            dma((frags, RING)),
            dma((frags,)),
            dma((frags,)),
            dma((frags,)),
            dma((frags + 1, 6)),
            dma((frags + 1, 3)),
        ],
        compiler_params=pltpu.CompilerParams(
            collective_id=0, has_side_effects=True, vmem_limit_bytes=50 * 2**20
        ),
        cost_estimate=pl.CostEstimate(flops=20 * rows * cols, bytes_accessed=20 * frags * rows * cols // 2, transcendentals=0),
    )(local_weights, global_weights, momentum)


def solution(mesh):
    return jax.shard_map(
        synchronize,
        mesh=mesh,
        in_specs=(
            P("replica", None, "fsdp", None),
            P(None, "fsdp", None),
            P(None, "fsdp", "replica"),
        ),
        out_specs=(P(None, "fsdp", None), P(None, "fsdp", "replica")),
        check_vma=False,
    )
```

```python
import functools

import jax
import jax.numpy as jnp
from jax import lax
from jax.experimental import pallas as pl
from jax.experimental.pallas import tpu as pltpu
from jax.sharding import PartitionSpec as P

OUTER_MOMENTUM = 0.9
OUTER_RATE = 0.7
CLIP_LEVEL = 1.0
MESH = pl.DeviceIdType.MESH
RING = 4
OFFSETS = (0, 1, -1, 2)
F32, BF16 = jnp.float32, jnp.bfloat16


def kernel(zs, count, lw_hbm, gw_hbm, mom_hbm, gw, mout,
           lw, mom, ds, dr, s_send, s_mid, s_end, tt, t_send, t_end, av, n1, n2, g, h,
           in_sems, mom_sem, late_sem, send_sems, norm_sems, core_sems, mid_sems, end_sems, end2_sems, gather_sems, hand_sems):
    frags, rows, _ = gw.shape
    width = mom.shape[2]
    half_rows, quarter = rows // 2, rows // 4
    r = lax.axis_index("replica")
    z = lax.axis_index("fsdp")
    core = r % 2
    y = (r // 2) % RING
    x = r // (2 * RING)
    both = range(2)

    def dev(ox, oy, oc=0, oz=0):
        ax, ay = (x + ox) % RING, (y + oy) % RING
        return ((ax * RING + ay) * 2 + (core + oc) % 2, (z + oz) % zs)

    def along(axis, o):
        return dev(o, 0) if axis == 0 else dev(0, o)

    def column(hf, a, b, c):
        ax, ay = (x + (a if hf == 0 else b)) % RING, (y + (b if hf == 0 else a)) % RING
        return pl.multiple_of(((ax * RING + ay) * 2 + c) * width, width)

    def offset(slot):
        return jnp.where(slot == 2, -1, jnp.where(slot == 3, 2, slot))

    def send(src, dst, family, recv_sem, device):
        pltpu.make_async_remote_copy(
            src_ref=src, dst_ref=dst, send_sem=send_sems.at[family], recv_sem=recv_sem,
            device_id=device, device_id_type=MESH).start()

    def wait(ref, sem):
        pltpu.make_async_copy(ref, ref, sem).wait()

    mom_load = pltpu.make_async_copy(mom_hbm, mom, mom_sem)
    group = RING * 2 * width

    def start_load(slot):
        for hf in both:
            at = pl.ds(hf * half_rows, half_rows)
            a = (x if hf == 0 else y) + OFFSETS[slot] + RING
            if hf == 0:
                columns = [pl.ds(pl.multiple_of(a % RING * group, group), group)]
            else:
                n = 2 * width
                columns = [pl.ds(pl.multiple_of((b * RING + a % RING) * n, n), n) for b in range(RING)]
            for col in columns:
                pltpu.make_async_copy(gw_hbm.at[0, at, col], gw.at[0, at, col], in_sems.at[slot, 0]).start()
                pltpu.make_async_copy(lw_hbm.at[0, 0, at, col], lw.at[0, at, col], in_sems.at[slot, 1]).start()

    later = [
        (pltpu.make_async_copy(gw_hbm.at[1], gw.at[1], in_sems.at[RING, 0])),
        (pltpu.make_async_copy(lw_hbm.at[0, 1], lw.at[1], in_sems.at[RING, 1]))]

    def load(f, slot):
        if f == 0:
            wait(gw.at[0, :, pl.ds(0, group)], in_sems.at[slot, 0])
            wait(lw.at[0, :, pl.ds(0, group)], in_sems.at[slot, 1])
        elif slot == 3:
            for copy in later:
                copy.wait()

    start_load(3)
    mom_load.start()

    near = [(0, 0, oc, oz) for oz in range(zs) for oc in range(2) if (oc, oz) != (0, 0)]
    far = [(ox, oy, 0, 0) for ox in range(RING) for oy in range(RING) if (ox, oy) != (0, 0)]
    greeted = [(0, 0, 1, 0)] + [p for o in (1, -1) for p in ((o, 0, 0, 0), (0, o, 0, 0), (0, 0, 0, o))]
    barrier = pltpu.get_barrier_semaphore()
    for partner in greeted:
        pl.semaphore_signal(barrier, inc=1, device_id=dev(*partner), device_id_type=MESH)
    for slot in (1, 2, 0):
        start_load(slot)
    pl.semaphore_wait(barrier, len(greeted))

    for o in (1, -1):
        pl.semaphore_signal(late_sem, inc=1, device_id=dev(0, 0, 0, o), device_id_type=MESH)
    for copy in later:
        copy.start()

    def known():
        pl.semaphore_wait(late_sem, 2)

    def difference(f, row, n, col):
        at = pl.ds(row, n)
        return gw[f, at, pl.ds(col, width)] - lw[f, at, pl.ds(col, width)].astype(F32)

    def to_core(f, slot, hf):
        @pl.loop(0, RING)
        def _(j):
            col = column(hf, OFFSETS[slot], offset(j), 1 - core)
            ds[f, slot, hf, j] = difference(f, hf * half_rows, half_rows, col).astype(BF16)
        send(ds.at[f, slot, hf], dr.at[f, slot, hf], 0, core_sems.at[f, slot], dev(0, 0, 1))

    def from_core(f, slot):
        wait(dr.at[f, slot], core_sems.at[f, slot])

    def pair_sum(f, hf, slot, j, row, n):
        col = column(hf, OFFSETS[slot], offset(j), core)
        return (difference(f, hf * half_rows + row, n, col)
                + dr[f, slot, hf, j, pl.ds(row, n)].astype(F32))

    def ring1_far(f, hf):
        for q, way in ((0, 1), (1, -1)):
            @pl.loop(0, RING)
            def _(j):
                s_send[f, hf, 2, q, j] = pair_sum(f, hf, 3, j, q * quarter, quarter).astype(BF16)
            send(s_send.at[f, hf, 2, q], s_mid.at[f, hf, q], 1, mid_sems.at[f], along(hf, way))

    def ring1_near(f, hf, slot):
        q, way = (1, 1) if slot == 1 else (0, -1)

        @pl.loop(0, RING)
        def _(j):
            s_send[f, hf, slot - 1, q, j] = pair_sum(f, hf, slot, j, q * quarter, quarter).astype(BF16)
        send(s_send.at[f, hf, slot - 1, q], s_end.at[f, hf, slot - 1, q], 1, end_sems.at[f], along(hf, way))

    def ring1_middle(f, hf):
        for slot, q, way in ((1, 0, 1), (2, 1, -1)):
            @pl.loop(0, RING)
            def _(j):
                total = pair_sum(f, hf, slot, j, q * quarter, quarter) + s_mid[f, hf, q, j].astype(F32)
                s_send[f, hf, slot - 1, q, j] = total.astype(BF16)
            send(s_send.at[f, hf, slot - 1, q], s_end.at[f, hf, slot - 1, q], 1, end_sems.at[f], along(hf, way))

    def ring2_open(f, hf):
        def whole(j, q):
            total = pair_sum(f, hf, 0, j, q * quarter, quarter)
            return total + s_end[f, hf, 0, q, j].astype(F32) + s_end[f, hf, 1, q, j].astype(F32)

        for slot in (3, 1, 2):
            for q in both:
                t_send[f, hf, slot - 1, pl.ds(q * quarter, quarter)] = whole(slot, q).astype(BF16)
            send(t_send.at[f, hf, slot - 1], t_end.at[f, hf, slot - 1], 2, end2_sems.at[f],
                 along(1 - hf, OFFSETS[slot]))
        for q in both:
            tt[f, hf, pl.ds(q * quarter, quarter)] = whole(0, q)

    def ring2_close(f, hf):
        part = tt[f, hf]
        for k in range(RING - 1):
            part = part + t_end[f, hf, k].astype(F32)
        part = part * (1.0 / (2 * RING * RING))
        av[f, pl.ds(hf * half_rows, half_rows)] = part

    def tile(part):
        square = jnp.sum((part * part).reshape(half_rows // 8, 8, width), axis=0)
        total = square[:, :128]
        for c in range(1, width // 128):
            total = total + square[:, c * 128:(c + 1) * 128]
        return total

    def exchange(f, stage, tiles, me, partners):
        for partner in partners:
            send(tiles.at[f, me], tiles.at[f, me], 3 + stage, norm_sems.at[f, stage], dev(*partner))

    def gathered(f, stage, tiles, partners):
        wait(tiles.at[f, pl.ds(0, len(partners))], norm_sems.at[f, stage])
        return jnp.sum(tiles[f], axis=0)

    def norm_open(f):
        at = pl.ds(half_rows, half_rows)
        n2[f, x * RING + y] = tile(av[f, pl.ds(0, half_rows)]) + tile(av[f, at])
        exchange(f, 1, n2, x * RING + y, far)

    def norm_middle(f):
        n1[f, z * 2 + core] = gathered(f, 1, n2, far)
        exchange(f, 0, n1, z * 2 + core, near)

    def factor_of(f):
        norm_squared = jnp.sum(gathered(f, 0, n1, near), axis=(0, 1), keepdims=True)
        return jnp.minimum(1.0, CLIP_LEVEL * jnp.sqrt(F32(count)) / jnp.sqrt(norm_squared + 1e-06))

    STEP, AVERAGE, MOMENT = 0, 1, 2
    FIRST, NEAR, LAST = pl.ds(0, 1), pl.ds(1, 2), pl.ds(3, 1)

    def gather1(s, hf, slot, k):
        back = (None, 2, 1, 3)[slot]
        send(g.at[s, hf, 0, 0], g.at[s, hf, 0, back], 5, gather_sems.at[s, k], along(1 - hf, OFFSETS[slot]))

    def gather2(s, hf, at, k):
        for slot, back in ((1, 2), (2, 1)):
            send(g.at[s, hf, 0, at], g.at[s, hf, back, at], 6, gather_sems.at[s, k], along(hf, OFFSETS[slot]))

    def gather2_pass(s, hf, at, k):
        k = 6 if k == 4 else 5
        for back, way, q in ((2, 1, 0), (1, -1, 1)):
            rows_at = pl.ds(q * quarter, quarter)
            send(g.at[s, hf, back, at, rows_at], g.at[s, hf, 3, at, rows_at], 6,
                 gather_sems.at[s, k], along(hf, way))

    def spread(s):
        for hf in both:
            for slot in (1, 2, 3)[:2 if s == MOMENT else 3]:
                gather1(s, hf, slot, slot // 3)
        for hf in both:
            gather2(s, hf, FIRST, 2)

    def spread_moment():
        mom_load.wait()
        for hf in both:
            g[MOMENT, hf, 0, 0] = mom[1, pl.ds(hf * half_rows, half_rows)].astype(BF16)
        spread(MOMENT)

    def spread_average():
        for hf in both:
            g[AVERAGE, hf, 0, 0] = av[1, pl.ds(hf * half_rows, half_rows)].astype(BF16)
        spread(AVERAGE)

    def spread_step():
        factor = factor_of(0)
        for hf in both:
            at = pl.ds(hf * half_rows, half_rows)
            clipped = av[0, at] * factor
            moment = OUTER_MOMENTUM * mom[0, at] + clipped
            mout[0, at] = moment
            g[STEP, hf, 0, 0] = (clipped + OUTER_MOMENTUM * moment).astype(BF16)
        spread(STEP)

    def spread_far(s):
        for hf in both:
            gather1(s, hf, 3, 1)

    scales = {STEP: OUTER_RATE, MOMENT: OUTER_RATE * OUTER_MOMENTUM * OUTER_MOMENTUM}

    def clip_average():
        factor = factor_of(1)
        mout[1] = OUTER_MOMENTUM * mom[1] + av[1] * factor
        scales[AVERAGE] = OUTER_RATE * (1.0 + OUTER_MOMENTUM) * factor

    def gather1_near(s):
        wait(g.at[s, :, 0, NEAR], gather_sems.at[s, 0])
        for hf in both:
            gather2(s, hf, NEAR, 3)

    def gather1_far(s):
        wait(g.at[s, :, 0, LAST], gather_sems.at[s, 1])
        for hf in both:
            gather2(s, hf, LAST, 4)
        for hf in both:
            hand_over(s, hf, 0, 1, 0)

    def gather2_passes(s, at, k):
        wait(g.at[s, :, pl.ds(1, 2), at], gather_sems.at[s, k])
        for hf in both:
            gather2_pass(s, hf, at, k)

    def gather2_first(s):
        gather2_passes(s, FIRST, 2)

    def gather2_near(s):
        gather2_passes(s, NEAR, 3)

    def gather2_far(s):
        gather2_passes(s, LAST, 4)
        for hf in both:
            hand_over(s, hf, 1, 2, 1)

    def gather2_last(s):
        most = pl.ds(0, RING - 1)
        wait(g.at[s, :, 3, most], gather_sems.at[s, 5])
        for hf in both:
            send(g.at[s, hf, 3, most], h.at[s, hf, 3, most], 7, hand_sems.at[s, 2], dev(0, 0, 1))

    def gather2_end(s):
        wait(g.at[s, :, 3, LAST], gather_sems.at[s, 6])
        for hf in both:
            send(g.at[s, hf, 3, LAST], h.at[s, hf, 3, LAST], 7, hand_sems.at[s, 3], dev(0, 0, 1))

    def hand_over(s, hf, slot, n, k):
        at = pl.ds(slot, n)
        send(g.at[s, hf, at], h.at[s, hf, at], 7, hand_sems.at[s, k], dev(0, 0, 1))

    def refresh(s, hf, slot, blocks, c, first=0, last=RING):
        f = 0 if s == STEP else 1
        at = pl.ds(hf * half_rows, half_rows)
        scale = scales[s]

        @pl.loop(first, last)
        def _(j):
            col = pl.ds(column(hf, OFFSETS[slot], offset(j), c), width)
            gw[f, at, col] = gw[f, at, col] - scale * blocks[s, hf, slot, j].astype(F32)

    def own(s, *slots):
        for hf in both:
            for slot in slots:
                refresh(s, hf, slot, g, core)

    def other(s, k):
        if k < 2:
            slot, n = ((0, 1), (1, 2))[k]
            wait(h.at[s, :, pl.ds(slot, n)], hand_sems.at[s, k])
            for hf in both:
                for i in range(n):
                    refresh(s, hf, slot + i, h, 1 - core)
        else:
            for k, first, last in ((2, 0, RING - 1), (3, RING - 1, RING)):
                wait(h.at[s, :, 3, pl.ds(first, last - first)], hand_sems.at[s, k])
                for hf in both:
                    refresh(s, hf, 3, h, 1 - core, first, last)

    steps = []

    def step(work, *args):
        steps.append((work, args))

    def halves(work, f):
        for hf in both:
            work(f, hf)

    def core_step(f, slot):
        load(f, slot)
        for hf in both:
            to_core(f, slot, hf)

    def far_step(f):
        from_core(f, 3)
        halves(ring1_far, f)

    def near_step(f, slot):
        from_core(f, slot)
        for hf in both:
            ring1_near(f, hf, slot)

    def middle_step(f):
        wait(s_mid.at[f], mid_sems.at[f])
        halves(ring1_middle, f)

    def open_step(f):
        from_core(f, 0)
        wait(s_end.at[f], end_sems.at[f])
        halves(ring2_open, f)

    def close_step(f):
        wait(t_end.at[f], end2_sems.at[f])
        halves(ring2_close, f)

    step(spread_moment)
    step(core_step, 0, 3)
    step(core_step, 0, 1)
    step(far_step, 0)
    step(core_step, 0, 2)
    step(near_step, 0, 1)
    step(core_step, 0, 0)
    step(near_step, 0, 2)
    step(known)
    step(core_step, 1, 3)
    step(core_step, 1, 1)
    step(core_step, 1, 2)
    step(far_step, 1)
    step(core_step, 1, 0)
    step(middle_step, 0)
    step(near_step, 1, 1)
    step(near_step, 1, 2)
    step(middle_step, 1)
    step(spread_far, MOMENT)
    step(open_step, 0)
    step(gather1_near, MOMENT)
    step(open_step, 1)
    step(close_step, 0)
    step(norm_open, 0)
    step(gather1_far, MOMENT)
    step(gather2_first, MOMENT)
    step(close_step, 1)
    step(norm_open, 1)
    step(spread_average)
    step(gather2_near, MOMENT)
    step(norm_middle, 0)
    step(gather2_far, MOMENT)
    step(own, MOMENT, 0)
    step(gather1_near, AVERAGE)
    step(gather1_far, AVERAGE)
    step(spread_step)
    step(gather2_first, AVERAGE)
    step(norm_middle, 1)
    step(gather2_near, AVERAGE)
    step(gather2_far, AVERAGE)
    step(gather1_near, STEP)
    step(gather1_far, STEP)
    step(gather2_first, STEP)
    step(own, MOMENT, 1, 2)
    step(gather2_near, STEP)
    step(gather2_far, STEP)
    step(gather2_last, MOMENT)
    step(gather2_end, MOMENT)
    step(other, MOMENT, 0)
    step(other, MOMENT, 1)
    step(own, MOMENT, 3)
    step(clip_average)
    step(gather2_last, AVERAGE)
    step(gather2_end, AVERAGE)
    step(other, MOMENT, 2)
    step(own, AVERAGE, 0, 1, 2, 3)
    step(other, AVERAGE, 0)
    step(other, AVERAGE, 1)
    step(other, AVERAGE, 2)
    step(gather2_last, STEP)
    step(own, STEP, 0)
    step(gather2_end, STEP)
    step(other, STEP, 0)
    step(own, STEP, 1, 2)
    step(other, STEP, 1)
    step(own, STEP, 3)
    step(other, STEP, 2)

    for work, args in steps:
        work(*args)

    wait(ds, send_sems.at[0])
    wait(s_send, send_sems.at[1])
    wait(t_send, send_sems.at[2])
    wait(n1.at[:, pl.ds(0, len(near))], send_sems.at[3])
    wait(n2.at[:, pl.ds(0, len(far))], send_sems.at[4])
    wait(g.at[:, :, 0, pl.ds(0, 3)], send_sems.at[5])
    wait(g.at[:, :, pl.ds(0, 3)], send_sems.at[6])
    wait(h, send_sems.at[7])


def synchronize(local_weights, global_weights, momentum):
    frags, rows, cols = global_weights.shape
    width = momentum.shape[2]
    zs = lax.axis_size("fsdp")
    assert lax.axis_size("replica") == 2 * RING * RING and frags == 2
    half_rows, quarter = rows // 2, rows // 4
    anywhere = pl.BlockSpec(memory_space=pl.ANY)
    in_vmem = pl.BlockSpec(memory_space=pltpu.VMEM)
    dma = pltpu.SemaphoreType.DMA
    return pl.pallas_call(
        functools.partial(kernel, zs, rows * zs * cols),
        out_shape=(pltpu.VMEM(global_weights.shape, F32), pltpu.VMEM(momentum.shape, F32)),
        in_specs=[anywhere] * 3,
        out_specs=(in_vmem, in_vmem),
        scratch_shapes=[
            pltpu.VMEM((frags, rows, cols), BF16),
            pltpu.VMEM((frags, rows, width), F32),
            pltpu.VMEM((frags, RING, 2, RING, half_rows, width), BF16),
            pltpu.VMEM((frags, RING, 2, RING, half_rows, width), BF16),
            pltpu.VMEM((frags, 2, RING - 1, 2, RING, quarter, width), BF16),
            pltpu.VMEM((frags, 2, 2, RING, quarter, width), BF16),
            pltpu.VMEM((frags, 2, 2, 2, RING, quarter, width), BF16),
            pltpu.VMEM((frags, 2, half_rows, width), F32),
            pltpu.VMEM((frags, 2, RING - 1, half_rows, width), BF16),
            pltpu.VMEM((frags, 2, RING - 1, half_rows, width), BF16),
            pltpu.VMEM((frags, rows, width), F32),
            pltpu.VMEM((frags, 2 * zs, 8, 128), F32),
            pltpu.VMEM((frags, RING * RING, 8, 128), F32),
            pltpu.VMEM((frags + 1, 2, RING, RING, half_rows, width), BF16),
            pltpu.VMEM((frags + 1, 2, RING, RING, half_rows, width), BF16),
            dma((RING + 1, 2)),
            dma,
            pltpu.SemaphoreType.REGULAR,
            dma((8,)),
            dma((frags, 2)),
            dma((frags, RING)),
            dma((frags,)),
            dma((frags,)),
            dma((frags,)),
            dma((frags + 1, 7)),
            dma((frags + 1, 4)),
        ],
        compiler_params=pltpu.CompilerParams(
            collective_id=0, has_side_effects=True, vmem_limit_bytes=50 * 2**20
        ),
        cost_estimate=pl.CostEstimate(flops=20 * rows * cols, bytes_accessed=20 * frags * rows * cols // 2, transcendentals=0),
    )(local_weights, global_weights, momentum)


def solution(mesh):
    return jax.shard_map(
        synchronize,
        mesh=mesh,
        in_specs=(
            P("replica", None, "fsdp", None),
            P(None, "fsdp", None),
            P(None, "fsdp", "replica"),
        ),
        out_specs=(P(None, "fsdp", None), P(None, "fsdp", "replica")),
        check_vma=False,
    )
```

```python
import functools

import jax
import jax.numpy as jnp
from jax import lax
from jax.experimental import pallas as pl
from jax.experimental.pallas import tpu as pltpu
from jax.sharding import PartitionSpec as P

OUTER_MOMENTUM = 0.9
OUTER_RATE = 0.7
CLIP_LEVEL = 1.0
MESH = pl.DeviceIdType.MESH
RING = 4
OFFSETS = (0, 1, -1, 2)
F32, BF16 = jnp.float32, jnp.bfloat16


def kernel(zs, count, lw_hbm, gw_hbm, mom_hbm, gw, mout,
           lw, mom, ds, dr, s_send, s_mid, s_end, tt, t_send, t_end, av, n1, n2, g, h, p,
           in_sems, mom_sem, late_sem, send_sems, norm_sems, core_sems, mid_sems, end_sems, end2_sems, gather_sems, hand_sems, share_sems):
    frags, rows, _ = gw.shape
    width = mom.shape[2]
    half_rows, quarter = rows // 2, rows // 4
    r = lax.axis_index("replica")
    z = lax.axis_index("fsdp")
    core = r % 2
    y = (r // 2) % RING
    x = r // (2 * RING)
    both = range(2)

    def dev(ox, oy, oc=0, oz=0):
        ax, ay = (x + ox) % RING, (y + oy) % RING
        return ((ax * RING + ay) * 2 + (core + oc) % 2, (z + oz) % zs)

    def along(axis, o):
        return dev(o, 0) if axis == 0 else dev(0, o)

    def column(hf, a, b, c):
        ax, ay = (x + (a if hf == 0 else b)) % RING, (y + (b if hf == 0 else a)) % RING
        return pl.multiple_of(((ax * RING + ay) * 2 + c) * width, width)

    def offset(slot):
        return jnp.where(slot == 2, -1, jnp.where(slot == 3, 2, slot))

    def send(src, dst, family, recv_sem, device):
        pltpu.make_async_remote_copy(
            src_ref=src, dst_ref=dst, send_sem=send_sems.at[family], recv_sem=recv_sem,
            device_id=device, device_id_type=MESH).start()

    def wait(ref, sem):
        pltpu.make_async_copy(ref, ref, sem).wait()

    mom_load = pltpu.make_async_copy(mom_hbm, mom, mom_sem)
    group = RING * 2 * width

    def start_load(slot):
        for hf in both:
            at = pl.ds(hf * half_rows, half_rows)
            a = (x if hf == 0 else y) + OFFSETS[slot] + RING
            if hf == 0:
                columns = [pl.ds(pl.multiple_of(a % RING * group, group), group)]
            else:
                n = 2 * width
                columns = [pl.ds(pl.multiple_of((b * RING + a % RING) * n, n), n) for b in range(RING)]
            for col in columns:
                pltpu.make_async_copy(gw_hbm.at[0, at, col], gw.at[0, at, col], in_sems.at[slot, 0]).start()
                pltpu.make_async_copy(lw_hbm.at[0, 0, at, col], lw.at[0, at, col], in_sems.at[slot, 1]).start()

    later = [
        (pltpu.make_async_copy(gw_hbm.at[1], gw.at[1], in_sems.at[RING, 0])),
        (pltpu.make_async_copy(lw_hbm.at[0, 1], lw.at[1], in_sems.at[RING, 1]))]

    def load(f, slot):
        if f == 0:
            wait(gw.at[0, :, pl.ds(0, group)], in_sems.at[slot, 0])
            wait(lw.at[0, :, pl.ds(0, group)], in_sems.at[slot, 1])
        elif slot == 3:
            for copy in later:
                copy.wait()

    start_load(3)
    mom_load.start()

    near = [(0, 0, oc, oz) for oz in range(zs) for oc in range(2) if (oc, oz) != (0, 0)]
    far = [(ox, oy, 0, 0) for ox in range(RING) for oy in range(RING) if (ox, oy) != (0, 0)]
    greeted = [(0, 0, 1, 0)] + [p for o in (1, -1) for p in ((o, 0, 0, 0), (0, o, 0, 0), (0, 0, 0, o))]
    barrier = pltpu.get_barrier_semaphore()
    for partner in greeted:
        pl.semaphore_signal(barrier, inc=1, device_id=dev(*partner), device_id_type=MESH)
    for slot in (1, 2, 0):
        start_load(slot)
    pl.semaphore_wait(barrier, len(greeted))

    for o in (1, -1):
        pl.semaphore_signal(late_sem, inc=1, device_id=dev(0, 0, 0, o), device_id_type=MESH)
    for copy in later:
        copy.start()

    def known():
        pl.semaphore_wait(late_sem, 2)

    def difference(f, row, n, col):
        at = pl.ds(row, n)
        return gw[f, at, pl.ds(col, width)] - lw[f, at, pl.ds(col, width)].astype(F32)

    def to_core(f, slot, hf):
        @pl.loop(0, RING)
        def _(j):
            col = column(hf, OFFSETS[slot], offset(j), 1 - core)
            ds[f, slot, hf, j] = difference(f, hf * half_rows, half_rows, col).astype(BF16)
        send(ds.at[f, slot, hf], dr.at[f, slot, hf], 0, core_sems.at[f, slot], dev(0, 0, 1))

    def from_core(f, slot):
        wait(dr.at[f, slot], core_sems.at[f, slot])

    def pair_sum(f, hf, slot, j, row, n):
        col = column(hf, OFFSETS[slot], offset(j), core)
        return (difference(f, hf * half_rows + row, n, col)
                + dr[f, slot, hf, j, pl.ds(row, n)].astype(F32))

    def ring1_far(f, hf):
        for q, way in ((0, 1), (1, -1)):
            @pl.loop(0, RING)
            def _(j):
                s_send[f, hf, 2, q, j] = pair_sum(f, hf, 3, j, q * quarter, quarter).astype(BF16)
            send(s_send.at[f, hf, 2, q], s_mid.at[f, hf, q], 1, mid_sems.at[f], along(hf, way))

    def ring1_near(f, hf, slot):
        q, way = (1, 1) if slot == 1 else (0, -1)

        @pl.loop(0, RING)
        def _(j):
            s_send[f, hf, slot - 1, q, j] = pair_sum(f, hf, slot, j, q * quarter, quarter).astype(BF16)
        send(s_send.at[f, hf, slot - 1, q], s_end.at[f, hf, slot - 1, q], 1, end_sems.at[f], along(hf, way))

    def ring1_middle(f, hf):
        for slot, q, way in ((1, 0, 1), (2, 1, -1)):
            @pl.loop(0, RING)
            def _(j):
                total = pair_sum(f, hf, slot, j, q * quarter, quarter) + s_mid[f, hf, q, j].astype(F32)
                s_send[f, hf, slot - 1, q, j] = total.astype(BF16)
            send(s_send.at[f, hf, slot - 1, q], s_end.at[f, hf, slot - 1, q], 1, end_sems.at[f], along(hf, way))

    def ring2_open(f, hf):
        def whole(j, q):
            total = pair_sum(f, hf, 0, j, q * quarter, quarter)
            return total + s_end[f, hf, 0, q, j].astype(F32) + s_end[f, hf, 1, q, j].astype(F32)

        for slot in (3, 1, 2):
            for q in both:
                t_send[f, hf, slot - 1, pl.ds(q * quarter, quarter)] = whole(slot, q).astype(BF16)
            send(t_send.at[f, hf, slot - 1], t_end.at[f, hf, slot - 1], 2, end2_sems.at[f],
                 along(1 - hf, OFFSETS[slot]))
        for q in both:
            tt[f, hf, pl.ds(q * quarter, quarter)] = whole(0, q)

    def ring2_close(f, hf):
        part = tt[f, hf]
        for k in range(RING - 1):
            part = part + t_end[f, hf, k].astype(F32)
        part = part * (1.0 / (2 * RING * RING))
        av[f, pl.ds(hf * half_rows, half_rows)] = part

    def tile(part):
        square = jnp.sum((part * part).reshape(half_rows // 8, 8, width), axis=0)
        total = square[:, :128]
        for c in range(1, width // 128):
            total = total + square[:, c * 128:(c + 1) * 128]
        return total

    def exchange(f, stage, tiles, me, partners):
        for partner in partners:
            send(tiles.at[f, me], tiles.at[f, me], 3 + stage, norm_sems.at[f, stage], dev(*partner))

    def gathered(f, stage, tiles, partners):
        wait(tiles.at[f, pl.ds(0, len(partners))], norm_sems.at[f, stage])
        return jnp.sum(tiles[f], axis=0)

    def norm_open(f):
        at = pl.ds(half_rows, half_rows)
        n2[f, x * RING + y] = tile(av[f, pl.ds(0, half_rows)]) + tile(av[f, at])
        exchange(f, 1, n2, x * RING + y, far)

    def norm_middle(f):
        n1[f, z * 2 + core] = gathered(f, 1, n2, far)
        exchange(f, 0, n1, z * 2 + core, near)

    def factor_of(f):
        norm_squared = jnp.sum(gathered(f, 0, n1, near), axis=(0, 1), keepdims=True)
        return jnp.minimum(1.0, CLIP_LEVEL * jnp.sqrt(F32(count)) / jnp.sqrt(norm_squared + 1e-06))

    STEP, AVERAGE, MOMENT = 0, 1, 2
    FIRST, NEAR, LAST = pl.ds(0, 1), pl.ds(1, 2), pl.ds(3, 1)

    def gather1(s, hf, slot, k):
        back = (None, 2, 1, 3)[slot]
        send(g.at[s, hf, 0, 0], g.at[s, hf, 0, back], 5, gather_sems.at[s, k], along(1 - hf, OFFSETS[slot]))

    def gather2(s, hf, at, k):
        for slot, back in ((1, 2), (2, 1)):
            send(g.at[s, hf, 0, at], g.at[s, hf, back, at], 6, gather_sems.at[s, k], along(hf, OFFSETS[slot]))

    def gather2_pass(s, hf, at, k):
        k = 6 if k == 4 else 5
        for back, way, q in ((2, 1, 0), (1, -1, 1)):
            rows_at = pl.ds(q * quarter, quarter)
            send(g.at[s, hf, back, at, rows_at], g.at[s, hf, 3, at, rows_at], 6,
                 gather_sems.at[s, k], along(hf, way))

    def spread(s):
        for hf in both:
            for slot in (1, 2, 3)[:2 if s == MOMENT else 3]:
                gather1(s, hf, slot, slot // 3)
        for hf in both:
            gather2(s, hf, FIRST, 2)

    def share(i, *slots):
        for hf in both:
            for slot in slots:
                back = (None, 2, 1, 3)[slot]
                send(p.at[i, hf, 0], p.at[i, hf, back], 8, share_sems.at[i, slot // 3], along(1 - hf, OFFSETS[slot]))

    def share_average():
        for hf in both:
            p[0, hf, 0] = av[0, pl.ds(hf * half_rows, half_rows)].astype(BF16)
        share(0, 1, 2, 3)

    def spread_moment():
        mom_load.wait()
        for hf in both:
            at = pl.ds(hf * half_rows, half_rows)
            g[MOMENT, hf, 0, 0] = mom[1, at].astype(BF16)
            p[1, hf, 0] = mom[0, at].astype(BF16)
        spread(MOMENT)
        share(1, 1, 2)

    def spread_average():
        for hf in both:
            g[AVERAGE, hf, 0, 0] = av[1, pl.ds(hf * half_rows, half_rows)].astype(BF16)
        spread(AVERAGE)

    def spread_step():
        factor = factor_of(0)
        for i in (1, 0):
            wait(p.at[i, :, NEAR], share_sems.at[i, 0])
            wait(p.at[i, :, LAST], share_sems.at[i, 1])
        for at, slots, k in ((FIRST, (0,), 2), (NEAR, (1, 2), 3), (LAST, (3,), 4)):
            for hf in both:
                for slot in slots:
                    clipped = p[0, hf, slot].astype(F32) * factor
                    moment = OUTER_MOMENTUM * p[1, hf, slot].astype(F32) + clipped
                    g[STEP, hf, 0, slot] = (clipped + OUTER_MOMENTUM * moment).astype(BF16)
                gather2(STEP, hf, at, k)
        for hf in both:
            hand_over(STEP, hf, 0, 1, 0)
        mout[0] = OUTER_MOMENTUM * mom[0] + av[0] * factor

    def spread_far(s):
        for hf in both:
            gather1(s, hf, 3, 1)
        share(1, 3)

    scales = {STEP: OUTER_RATE, MOMENT: OUTER_RATE * OUTER_MOMENTUM * OUTER_MOMENTUM}

    def clip_average():
        factor = factor_of(1)
        mout[1] = OUTER_MOMENTUM * mom[1] + av[1] * factor
        scales[AVERAGE] = OUTER_RATE * (1.0 + OUTER_MOMENTUM) * factor

    def gather1_near(s):
        wait(g.at[s, :, 0, NEAR], gather_sems.at[s, 0])
        for hf in both:
            gather2(s, hf, NEAR, 3)

    def gather1_far(s):
        wait(g.at[s, :, 0, LAST], gather_sems.at[s, 1])
        for hf in both:
            gather2(s, hf, LAST, 4)
        for hf in both:
            hand_over(s, hf, 0, 1, 0)

    def gather2_passes(s, at, k):
        wait(g.at[s, :, pl.ds(1, 2), at], gather_sems.at[s, k])
        for hf in both:
            gather2_pass(s, hf, at, k)

    def gather2_first(s):
        gather2_passes(s, FIRST, 2)

    def gather2_near(s):
        gather2_passes(s, NEAR, 3)

    def gather2_far(s):
        gather2_passes(s, LAST, 4)
        for hf in both:
            hand_over(s, hf, 1, 2, 1)

    def gather2_last(s):
        most = pl.ds(0, RING - 1)
        wait(g.at[s, :, 3, most], gather_sems.at[s, 5])
        for hf in both:
            send(g.at[s, hf, 3, most], h.at[s, hf, 3, most], 7, hand_sems.at[s, 2], dev(0, 0, 1))

    def gather2_end(s):
        wait(g.at[s, :, 3, LAST], gather_sems.at[s, 6])
        for hf in both:
            send(g.at[s, hf, 3, LAST], h.at[s, hf, 3, LAST], 7, hand_sems.at[s, 3], dev(0, 0, 1))

    def hand_over(s, hf, slot, n, k):
        at = pl.ds(slot, n)
        send(g.at[s, hf, at], h.at[s, hf, at], 7, hand_sems.at[s, k], dev(0, 0, 1))

    def refresh(s, hf, slot, blocks, c, first=0, last=RING):
        f = 0 if s == STEP else 1
        at = pl.ds(hf * half_rows, half_rows)
        scale = scales[s]

        @pl.loop(first, last)
        def _(j):
            col = pl.ds(column(hf, OFFSETS[slot], offset(j), c), width)
            gw[f, at, col] = gw[f, at, col] - scale * blocks[s, hf, slot, j].astype(F32)

    def own(s, *slots):
        for hf in both:
            for slot in slots:
                refresh(s, hf, slot, g, core)

    def other(s, k):
        if k < 2:
            slot, n = ((0, 1), (1, 2))[k]
            wait(h.at[s, :, pl.ds(slot, n)], hand_sems.at[s, k])
            for hf in both:
                for i in range(n):
                    refresh(s, hf, slot + i, h, 1 - core)
        else:
            for k, first, last in ((2, 0, RING - 1), (3, RING - 1, RING)):
                wait(h.at[s, :, 3, pl.ds(first, last - first)], hand_sems.at[s, k])
                for hf in both:
                    refresh(s, hf, 3, h, 1 - core, first, last)

    steps = []

    def step(work, *args):
        steps.append((work, args))

    def halves(work, f):
        for hf in both:
            work(f, hf)

    def core_step(f, slot):
        load(f, slot)
        for hf in both:
            to_core(f, slot, hf)

    def far_step(f):
        from_core(f, 3)
        halves(ring1_far, f)

    def near_step(f, slot):
        from_core(f, slot)
        for hf in both:
            ring1_near(f, hf, slot)

    def middle_step(f):
        wait(s_mid.at[f], mid_sems.at[f])
        halves(ring1_middle, f)

    def open_step(f):
        from_core(f, 0)
        wait(s_end.at[f], end_sems.at[f])
        halves(ring2_open, f)

    def close_step(f):
        wait(t_end.at[f], end2_sems.at[f])
        halves(ring2_close, f)

    step(spread_moment)
    step(core_step, 0, 3)
    step(core_step, 0, 1)
    step(far_step, 0)
    step(core_step, 0, 2)
    step(near_step, 0, 1)
    step(core_step, 0, 0)
    step(near_step, 0, 2)
    step(known)
    step(core_step, 1, 3)
    step(core_step, 1, 1)
    step(core_step, 1, 2)
    step(far_step, 1)
    step(core_step, 1, 0)
    step(middle_step, 0)
    step(near_step, 1, 1)
    step(near_step, 1, 2)
    step(middle_step, 1)
    step(spread_far, MOMENT)
    step(open_step, 0)
    step(gather1_near, MOMENT)
    step(open_step, 1)
    step(close_step, 0)
    step(norm_open, 0)
    step(share_average)
    step(gather1_far, MOMENT)
    step(gather2_first, MOMENT)
    step(close_step, 1)
    step(norm_open, 1)
    step(spread_average)
    step(gather2_near, MOMENT)
    step(norm_middle, 0)
    step(gather2_far, MOMENT)
    step(own, MOMENT, 0)
    step(gather1_near, AVERAGE)
    step(gather1_far, AVERAGE)
    step(spread_step)
    step(gather2_first, AVERAGE)
    step(norm_middle, 1)
    step(gather2_near, AVERAGE)
    step(gather2_first, STEP)
    step(gather2_far, AVERAGE)
    step(own, MOMENT, 1, 2)
    step(gather2_near, STEP)
    step(gather2_far, STEP)
    step(gather2_last, MOMENT)
    step(gather2_end, MOMENT)
    step(other, MOMENT, 0)
    step(other, MOMENT, 1)
    step(own, MOMENT, 3)
    step(clip_average)
    step(gather2_last, AVERAGE)
    step(gather2_end, AVERAGE)
    step(other, MOMENT, 2)
    step(own, AVERAGE, 0, 1, 2, 3)
    step(other, AVERAGE, 0)
    step(other, AVERAGE, 1)
    step(other, AVERAGE, 2)
    step(gather2_last, STEP)
    step(own, STEP, 0)
    step(gather2_end, STEP)
    step(other, STEP, 0)
    step(own, STEP, 1, 2)
    step(other, STEP, 1)
    step(own, STEP, 3)
    step(other, STEP, 2)

    for work, args in steps:
        work(*args)

    wait(ds, send_sems.at[0])
    wait(s_send, send_sems.at[1])
    wait(t_send, send_sems.at[2])
    wait(n1.at[:, pl.ds(0, len(near))], send_sems.at[3])
    wait(n2.at[:, pl.ds(0, len(far))], send_sems.at[4])
    wait(g.at[pl.ds(1, frags), :, 0, pl.ds(0, 3)], send_sems.at[5])
    wait(g.at[:, :, pl.ds(0, 3)], send_sems.at[6])
    wait(h, send_sems.at[7])
    wait(p.at[:, :, pl.ds(0, 3)], send_sems.at[8])


def synchronize(local_weights, global_weights, momentum):
    frags, rows, cols = global_weights.shape
    width = momentum.shape[2]
    zs = lax.axis_size("fsdp")
    assert lax.axis_size("replica") == 2 * RING * RING and frags == 2
    half_rows, quarter = rows // 2, rows // 4
    anywhere = pl.BlockSpec(memory_space=pl.ANY)
    in_vmem = pl.BlockSpec(memory_space=pltpu.VMEM)
    dma = pltpu.SemaphoreType.DMA
    return pl.pallas_call(
        functools.partial(kernel, zs, rows * zs * cols),
        out_shape=(pltpu.VMEM(global_weights.shape, F32), pltpu.VMEM(momentum.shape, F32)),
        in_specs=[anywhere] * 3,
        out_specs=(in_vmem, in_vmem),
        scratch_shapes=[
            pltpu.VMEM((frags, rows, cols), BF16),
            pltpu.VMEM((frags, rows, width), F32),
            pltpu.VMEM((frags, RING, 2, RING, half_rows, width), BF16),
            pltpu.VMEM((frags, RING, 2, RING, half_rows, width), BF16),
            pltpu.VMEM((frags, 2, RING - 1, 2, RING, quarter, width), BF16),
            pltpu.VMEM((frags, 2, 2, RING, quarter, width), BF16),
            pltpu.VMEM((frags, 2, 2, 2, RING, quarter, width), BF16),
            pltpu.VMEM((frags, 2, half_rows, width), F32),
            pltpu.VMEM((frags, 2, RING - 1, half_rows, width), BF16),
            pltpu.VMEM((frags, 2, RING - 1, half_rows, width), BF16),
            pltpu.VMEM((frags, rows, width), F32),
            pltpu.VMEM((frags, 2 * zs, 8, 128), F32),
            pltpu.VMEM((frags, RING * RING, 8, 128), F32),
            pltpu.VMEM((frags + 1, 2, RING, RING, half_rows, width), BF16),
            pltpu.VMEM((frags + 1, 2, RING, RING, half_rows, width), BF16),
            pltpu.VMEM((2, 2, RING, half_rows, width), BF16),
            dma((RING + 1, 2)),
            dma,
            pltpu.SemaphoreType.REGULAR,
            dma((9,)),
            dma((frags, 2)),
            dma((frags, RING)),
            dma((frags,)),
            dma((frags,)),
            dma((frags,)),
            dma((frags + 1, 7)),
            dma((frags + 1, 4)),
            dma((2, 2)),
        ],
        compiler_params=pltpu.CompilerParams(
            collective_id=0, has_side_effects=True, vmem_limit_bytes=50 * 2**20
        ),
        cost_estimate=pl.CostEstimate(flops=20 * rows * cols, bytes_accessed=20 * frags * rows * cols // 2, transcendentals=0),
    )(local_weights, global_weights, momentum)


def solution(mesh):
    return jax.shard_map(
        synchronize,
        mesh=mesh,
        in_specs=(
            P("replica", None, "fsdp", None),
            P(None, "fsdp", None),
            P(None, "fsdp", "replica"),
        ),
        out_specs=(P(None, "fsdp", None), P(None, "fsdp", "replica")),
        check_vma=False,
    )
```

```python
import functools

import jax
import jax.numpy as jnp
from jax import lax
from jax.experimental import pallas as pl
from jax.experimental.pallas import tpu as pltpu
from jax.sharding import PartitionSpec as P

OUTER_MOMENTUM = 0.9
OUTER_RATE = 0.7
CLIP_LEVEL = 1.0
MESH = pl.DeviceIdType.MESH
RING = 4
OFFSETS = (0, 1, -1, 2)
F32, BF16 = jnp.float32, jnp.bfloat16


def kernel(zs, count, lw_hbm, gw_hbm, mom_hbm, gw, mout,
           lw, mom, ds, dr, s_send, s_mid, s_end, tt, t_send, t_end, av, n1, n2, g, h, p,
           in_sems, mom_sem, late_sem, send_sems, norm_sems, core_sems, mid_sems, end_sems, end2_sems, gather_sems, hand_sems, share_sems):
    frags, rows, _ = gw.shape
    width = mom.shape[2]
    half_rows, quarter = rows // 2, rows // 4
    r = lax.axis_index("replica")
    z = lax.axis_index("fsdp")
    core = r % 2
    y = (r // 2) % RING
    x = r // (2 * RING)
    both = range(2)

    def dev(ox, oy, oc=0, oz=0):
        ax, ay = (x + ox) % RING, (y + oy) % RING
        return ((ax * RING + ay) * 2 + (core + oc) % 2, (z + oz) % zs)

    def along(axis, o):
        return dev(o, 0) if axis == 0 else dev(0, o)

    def column(hf, a, b, c):
        ax, ay = (x + (a if hf == 0 else b)) % RING, (y + (b if hf == 0 else a)) % RING
        return pl.multiple_of(((ax * RING + ay) * 2 + c) * width, width)

    def offset(slot):
        return jnp.where(slot == 2, -1, jnp.where(slot == 3, 2, slot))

    def send(src, dst, family, recv_sem, device):
        pltpu.make_async_remote_copy(
            src_ref=src, dst_ref=dst, send_sem=send_sems.at[family], recv_sem=recv_sem,
            device_id=device, device_id_type=MESH).start()

    def wait(ref, sem):
        pltpu.make_async_copy(ref, ref, sem).wait()

    mom_load = pltpu.make_async_copy(mom_hbm, mom, mom_sem)
    group = RING * 2 * width

    def start_load(slot):
        for hf in both:
            at = pl.ds(hf * half_rows, half_rows)
            a = (x if hf == 0 else y) + OFFSETS[slot] + RING
            if hf == 0:
                columns = [pl.ds(pl.multiple_of(a % RING * group, group), group)]
            else:
                n = 2 * width
                columns = [pl.ds(pl.multiple_of((b * RING + a % RING) * n, n), n) for b in range(RING)]
            for col in columns:
                pltpu.make_async_copy(gw_hbm.at[0, at, col], gw.at[0, at, col], in_sems.at[slot, 0]).start()
                pltpu.make_async_copy(lw_hbm.at[0, 0, at, col], lw.at[0, at, col], in_sems.at[slot, 1]).start()

    later = [
        (pltpu.make_async_copy(gw_hbm.at[1], gw.at[1], in_sems.at[RING, 0])),
        (pltpu.make_async_copy(lw_hbm.at[0, 1], lw.at[1], in_sems.at[RING, 1]))]

    def load(f, slot):
        if f == 0:
            wait(gw.at[0, :, pl.ds(0, group)], in_sems.at[slot, 0])
            wait(lw.at[0, :, pl.ds(0, group)], in_sems.at[slot, 1])
        elif slot == 3:
            for copy in later:
                copy.wait()

    start_load(3)
    mom_load.start()

    near = [(0, 0, oc, oz) for oz in range(zs) for oc in range(2) if (oc, oz) != (0, 0)]
    far = [(ox, oy, 0, 0) for ox in range(RING) for oy in range(RING) if (ox, oy) != (0, 0)]
    greeted = [(0, 0, 1, 0)] + [p for o in (1, -1) for p in ((o, 0, 0, 0), (0, o, 0, 0), (0, 0, 0, o))]
    barrier = pltpu.get_barrier_semaphore()
    for partner in greeted:
        pl.semaphore_signal(barrier, inc=1, device_id=dev(*partner), device_id_type=MESH)
    for slot in (1, 2, 0):
        start_load(slot)
    pl.semaphore_wait(barrier, len(greeted))

    for o in (1, -1):
        pl.semaphore_signal(late_sem, inc=1, device_id=dev(0, 0, 0, o), device_id_type=MESH)
    for copy in later:
        copy.start()

    def known():
        pl.semaphore_wait(late_sem, 2)

    def difference(f, row, n, col):
        at = pl.ds(row, n)
        return gw[f, at, pl.ds(col, width)] - lw[f, at, pl.ds(col, width)].astype(F32)

    def to_core(f, slot, hf):
        @pl.loop(0, RING)
        def _(j):
            col = column(hf, OFFSETS[slot], offset(j), 1 - core)
            ds[f, slot, hf, j] = difference(f, hf * half_rows, half_rows, col).astype(BF16)
        send(ds.at[f, slot, hf], dr.at[f, slot, hf], 0, core_sems.at[f, slot], dev(0, 0, 1))

    def from_core(f, slot):
        wait(dr.at[f, slot], core_sems.at[f, slot])

    def pair_sum(f, hf, slot, j, row, n):
        col = column(hf, OFFSETS[slot], offset(j), core)
        return (difference(f, hf * half_rows + row, n, col)
                + dr[f, slot, hf, j, pl.ds(row, n)].astype(F32))

    def ring1_far(f, hf):
        for q, way in ((0, 1), (1, -1)):
            @pl.loop(0, RING)
            def _(j):
                s_send[f, hf, 2, q, j] = pair_sum(f, hf, 3, j, q * quarter, quarter).astype(BF16)
            send(s_send.at[f, hf, 2, q], s_mid.at[f, hf, q], 1, mid_sems.at[f], along(hf, way))

    def ring1_near(f, hf, slot):
        q, way = (1, 1) if slot == 1 else (0, -1)

        @pl.loop(0, RING)
        def _(j):
            s_send[f, hf, slot - 1, q, j] = pair_sum(f, hf, slot, j, q * quarter, quarter).astype(BF16)
        send(s_send.at[f, hf, slot - 1, q], s_end.at[f, hf, slot - 1, q], 1, end_sems.at[f], along(hf, way))

    def ring1_middle(f, hf):
        for slot, q, way in ((1, 0, 1), (2, 1, -1)):
            @pl.loop(0, RING)
            def _(j):
                total = pair_sum(f, hf, slot, j, q * quarter, quarter) + s_mid[f, hf, q, j].astype(F32)
                s_send[f, hf, slot - 1, q, j] = total.astype(BF16)
            send(s_send.at[f, hf, slot - 1, q], s_end.at[f, hf, slot - 1, q], 1, end_sems.at[f], along(hf, way))

    def ring2_open(f, hf):
        def whole(j, q):
            total = pair_sum(f, hf, 0, j, q * quarter, quarter)
            return total + s_end[f, hf, 0, q, j].astype(F32) + s_end[f, hf, 1, q, j].astype(F32)

        for slot in (3, 1, 2):
            for q in both:
                t_send[f, hf, slot - 1, pl.ds(q * quarter, quarter)] = whole(slot, q).astype(BF16)
            send(t_send.at[f, hf, slot - 1], t_end.at[f, hf, slot - 1], 2, end2_sems.at[f],
                 along(1 - hf, OFFSETS[slot]))
        for q in both:
            tt[f, hf, pl.ds(q * quarter, quarter)] = whole(0, q)

    def ring2_close(f, hf):
        part = tt[f, hf]
        for k in range(RING - 1):
            part = part + t_end[f, hf, k].astype(F32)
        part = part * (1.0 / (2 * RING * RING))
        av[f, pl.ds(hf * half_rows, half_rows)] = part

    def tile(part):
        square = jnp.sum((part * part).reshape(half_rows // 8, 8, width), axis=0)
        total = square[:, :128]
        for c in range(1, width // 128):
            total = total + square[:, c * 128:(c + 1) * 128]
        return total

    def exchange(f, stage, tiles, me, partners):
        for partner in partners:
            send(tiles.at[f, me], tiles.at[f, me], 3 + stage, norm_sems.at[f, stage], dev(*partner))

    def gathered(f, stage, tiles, partners):
        wait(tiles.at[f, pl.ds(0, len(partners))], norm_sems.at[f, stage])
        return jnp.sum(tiles[f], axis=0)

    def norm_open(f):
        at = pl.ds(half_rows, half_rows)
        n2[f, x * RING + y] = tile(av[f, pl.ds(0, half_rows)]) + tile(av[f, at])
        exchange(f, 1, n2, x * RING + y, far)

    def norm_middle(f):
        n1[f, z * 2 + core] = gathered(f, 1, n2, far)
        exchange(f, 0, n1, z * 2 + core, near)

    def factor_of(f):
        norm_squared = jnp.sum(gathered(f, 0, n1, near), axis=(0, 1), keepdims=True)
        return jnp.minimum(1.0, CLIP_LEVEL * jnp.sqrt(F32(count)) / jnp.sqrt(norm_squared + 1e-06))

    FIRST, NEAR, LAST = pl.ds(0, 1), pl.ds(1, 2), pl.ds(3, 1)

    def share(f, i, *slots):
        for hf in both:
            for slot in slots:
                back = (None, 2, 1, 3)[slot]
                send(p.at[f, i, hf, 0], p.at[f, i, hf, back], 5, share_sems.at[f, i, slot // 3],
                     along(1 - hf, OFFSETS[slot]))

    def share_average(f):
        for hf in both:
            p[f, 0, hf, 0] = av[f, pl.ds(hf * half_rows, half_rows)].astype(BF16)
        share(f, 0, 1, 2, 3)

    def share_moment(f):
        for hf in both:
            p[f, 1, hf, 0] = mom[f, pl.ds(hf * half_rows, half_rows)].astype(BF16)
        share(f, 1, 1, 2)

    def share_moment_far(f):
        share(f, 1, 3)

    def gather2(f, hf, at, k):
        for slot, back in ((1, 2), (2, 1)):
            send(g.at[f, hf, 0, at], g.at[f, hf, back, at], 6, gather_sems.at[f, k], along(hf, OFFSETS[slot]))

    def spread_step(f):
        factor = factor_of(f)
        for i in (1, 0):
            wait(p.at[f, i, :, NEAR], share_sems.at[f, i, 0])
            wait(p.at[f, i, :, LAST], share_sems.at[f, i, 1])
        for k, at, slots in ((0, FIRST, (0,)), (1, NEAR, (1, 2)), (2, LAST, (3,))):
            for hf in both:
                for slot in slots:
                    clipped = p[f, 0, hf, slot].astype(F32) * factor
                    moment = OUTER_MOMENTUM * p[f, 1, hf, slot].astype(F32) + clipped
                    g[f, hf, 0, slot] = (clipped + OUTER_MOMENTUM * moment).astype(BF16)
                gather2(f, hf, at, k)
        for hf in both:
            hand_over(f, hf, 0, 1, 0)
        mout[f] = OUTER_MOMENTUM * mom[f] + av[f] * factor

    def gather2_pass(f, hf, at, k):
        for back, way, q in ((2, 1, 0), (1, -1, 1)):
            rows_at = pl.ds(q * quarter, quarter)
            send(g.at[f, hf, back, at, rows_at], g.at[f, hf, 3, at, rows_at], 6,
                 gather_sems.at[f, 4 if k == 2 else 3], along(hf, way))

    def gather2_passes(f, at, k):
        wait(g.at[f, :, pl.ds(1, 2), at], gather_sems.at[f, k])
        for hf in both:
            gather2_pass(f, hf, at, k)

    def gather2_first(f):
        gather2_passes(f, FIRST, 0)

    def gather2_near(f):
        gather2_passes(f, NEAR, 1)

    def gather2_far(f):
        gather2_passes(f, LAST, 2)
        for hf in both:
            hand_over(f, hf, 1, 2, 1)

    def gather2_last(f):
        most = pl.ds(0, RING - 1)
        wait(g.at[f, :, 3, most], gather_sems.at[f, 3])
        for hf in both:
            send(g.at[f, hf, 3, most], h.at[f, hf, 3, most], 7, hand_sems.at[f, 2], dev(0, 0, 1))

    def gather2_end(f):
        wait(g.at[f, :, 3, LAST], gather_sems.at[f, 4])
        for hf in both:
            send(g.at[f, hf, 3, LAST], h.at[f, hf, 3, LAST], 7, hand_sems.at[f, 3], dev(0, 0, 1))

    def hand_over(f, hf, slot, n, k):
        at = pl.ds(slot, n)
        send(g.at[f, hf, at], h.at[f, hf, at], 7, hand_sems.at[f, k], dev(0, 0, 1))

    def refresh(f, hf, slot, blocks, c, first=0, last=RING):
        at = pl.ds(hf * half_rows, half_rows)

        @pl.loop(first, last)
        def _(j):
            col = pl.ds(column(hf, OFFSETS[slot], offset(j), c), width)
            gw[f, at, col] = gw[f, at, col] - OUTER_RATE * blocks[f, hf, slot, j].astype(F32)

    def own(f, *slots):
        for hf in both:
            for slot in slots:
                refresh(f, hf, slot, g, core)

    def other(f, k):
        slot, n = ((0, 1), (1, 2), (3, 1), (3, 1))[k]
        first, last = ((0, RING), (0, RING), (0, RING - 1), (RING - 1, RING))[k]
        wait(h.at[f, :, pl.ds(slot, n), pl.ds(first, last - first)], hand_sems.at[f, k])
        for hf in both:
            for i in range(n):
                refresh(f, hf, slot + i, h, 1 - core, first, last)

    steps = []

    def step(work, *args):
        steps.append((work, args))

    def halves(work, f):
        for hf in both:
            work(f, hf)

    def core_step(f, slot):
        load(f, slot)
        for hf in both:
            to_core(f, slot, hf)

    def far_step(f):
        from_core(f, 3)
        halves(ring1_far, f)

    def near_step(f, slot):
        from_core(f, slot)
        for hf in both:
            ring1_near(f, hf, slot)

    def middle_step(f):
        wait(s_mid.at[f], mid_sems.at[f])
        halves(ring1_middle, f)

    def open_step(f):
        from_core(f, 0)
        wait(s_end.at[f], end_sems.at[f])
        halves(ring2_open, f)

    def close_step(f):
        wait(t_end.at[f], end2_sems.at[f])
        halves(ring2_close, f)

    step(mom_load.wait)
    step(share_moment, 0)
    step(share_moment, 1)
    step(core_step, 0, 3)
    step(core_step, 0, 1)
    step(far_step, 0)
    step(core_step, 0, 2)
    step(near_step, 0, 1)
    step(core_step, 0, 0)
    step(near_step, 0, 2)
    step(known)
    step(core_step, 1, 3)
    step(core_step, 1, 1)
    step(core_step, 1, 2)
    step(far_step, 1)
    step(core_step, 1, 0)
    step(middle_step, 0)
    step(near_step, 1, 1)
    step(near_step, 1, 2)
    step(middle_step, 1)
    step(open_step, 0)
    step(open_step, 1)
    step(close_step, 0)
    step(norm_open, 0)
    step(share_average, 0)
    step(share_moment_far, 0)
    step(close_step, 1)
    step(norm_open, 1)
    step(share_average, 1)
    step(share_moment_far, 1)
    step(norm_middle, 0)
    step(norm_middle, 1)
    step(spread_step, 0)
    step(gather2_first, 0)
    step(spread_step, 1)
    step(gather2_near, 0)
    step(gather2_far, 0)
    step(own, 0, 0)
    step(gather2_first, 1)
    step(gather2_last, 0)
    step(gather2_end, 0)
    step(gather2_near, 1)
    step(gather2_far, 1)
    step(other, 0, 0)
    step(own, 0, 1, 2)
    step(own, 1, 0)
    step(other, 0, 1)
    step(other, 1, 0)
    step(own, 0, 3)
    step(other, 0, 2)
    step(other, 0, 3)
    step(gather2_last, 1)
    step(own, 1, 1)
    step(gather2_end, 1)
    step(own, 1, 2)
    step(other, 1, 1)
    step(own, 1, 3)
    step(other, 1, 2)
    step(other, 1, 3)
    for work, args in steps:
        work(*args)

    wait(ds, send_sems.at[0])
    wait(s_send, send_sems.at[1])
    wait(t_send, send_sems.at[2])
    wait(n1.at[:, pl.ds(0, len(near))], send_sems.at[3])
    wait(n2.at[:, pl.ds(0, len(far))], send_sems.at[4])
    wait(p.at[:, :, :, pl.ds(0, 3)], send_sems.at[5])
    wait(g.at[:, :, pl.ds(0, 3)], send_sems.at[6])
    wait(h, send_sems.at[7])


def synchronize(local_weights, global_weights, momentum):
    frags, rows, cols = global_weights.shape
    width = momentum.shape[2]
    zs = lax.axis_size("fsdp")
    assert lax.axis_size("replica") == 2 * RING * RING and frags == 2
    half_rows, quarter = rows // 2, rows // 4
    anywhere = pl.BlockSpec(memory_space=pl.ANY)
    in_vmem = pl.BlockSpec(memory_space=pltpu.VMEM)
    dma = pltpu.SemaphoreType.DMA
    return pl.pallas_call(
        functools.partial(kernel, zs, rows * zs * cols),
        out_shape=(pltpu.VMEM(global_weights.shape, F32), pltpu.VMEM(momentum.shape, F32)),
        in_specs=[anywhere] * 3,
        out_specs=(in_vmem, in_vmem),
        scratch_shapes=[
            pltpu.VMEM((frags, rows, cols), BF16),
            pltpu.VMEM((frags, rows, width), F32),
            pltpu.VMEM((frags, RING, 2, RING, half_rows, width), BF16),
            pltpu.VMEM((frags, RING, 2, RING, half_rows, width), BF16),
            pltpu.VMEM((frags, 2, RING - 1, 2, RING, quarter, width), BF16),
            pltpu.VMEM((frags, 2, 2, RING, quarter, width), BF16),
            pltpu.VMEM((frags, 2, 2, 2, RING, quarter, width), BF16),
            pltpu.VMEM((frags, 2, half_rows, width), F32),
            pltpu.VMEM((frags, 2, RING - 1, half_rows, width), BF16),
            pltpu.VMEM((frags, 2, RING - 1, half_rows, width), BF16),
            pltpu.VMEM((frags, rows, width), F32),
            pltpu.VMEM((frags, 2 * zs, 8, 128), F32),
            pltpu.VMEM((frags, RING * RING, 8, 128), F32),
            pltpu.VMEM((frags, 2, RING, RING, half_rows, width), BF16),
            pltpu.VMEM((frags, 2, RING, RING, half_rows, width), BF16),
            pltpu.VMEM((frags, 2, 2, RING, half_rows, width), BF16),
            dma((RING + 1, 2)),
            dma,
            pltpu.SemaphoreType.REGULAR,
            dma((8,)),
            dma((frags, 2)),
            dma((frags, RING)),
            dma((frags,)),
            dma((frags,)),
            dma((frags,)),
            dma((frags, 5)),
            dma((frags, 4)),
            dma((frags, 2, 2)),
        ],
        compiler_params=pltpu.CompilerParams(
            collective_id=0, has_side_effects=True, vmem_limit_bytes=50 * 2**20
        ),
        cost_estimate=pl.CostEstimate(flops=20 * rows * cols, bytes_accessed=20 * frags * rows * cols // 2, transcendentals=0),
    )(local_weights, global_weights, momentum)


def solution(mesh):
    return jax.shard_map(
        synchronize,
        mesh=mesh,
        in_specs=(
            P("replica", None, "fsdp", None),
            P(None, "fsdp", None),
            P(None, "fsdp", "replica"),
        ),
        out_specs=(P(None, "fsdp", None), P(None, "fsdp", "replica")),
        check_vma=False,
    )
```

```python
import functools

import jax
import jax.numpy as jnp
from jax import lax
from jax.experimental import pallas as pl
from jax.experimental.pallas import tpu as pltpu
from jax.sharding import PartitionSpec as P

OUTER_MOMENTUM = 0.9
OUTER_RATE = 0.7
CLIP_LEVEL = 1.0
MESH = pl.DeviceIdType.MESH
RING = 4
PARTS = 2
OFFSETS = (0, 1, -1, 2)
F32, BF16 = jnp.float32, jnp.bfloat16


def kernel(zs, count, lw_hbm, gw_hbm, mom_hbm, gw, mout,
           lw, mom, ds, dr, s_send, s_mid, s_end, tt, t_send, t_end, av, n1, n2, g, h, p,
           in_sems, mom_sem, late_sem, send_sems, norm_sems, core_sems, mid_sems, end_sems, end2_sems, gather_sems, hand_sems, share_sems):
    frags, rows, _ = gw.shape
    width = mom.shape[2]
    half_rows, quarter = rows // 2, rows // 4
    r = lax.axis_index("replica")
    z = lax.axis_index("fsdp")
    core = r % 2
    y = (r // 2) % RING
    x = r // (2 * RING)
    both = range(2)

    def dev(ox, oy, oc=0, oz=0):
        ax, ay = (x + ox) % RING, (y + oy) % RING
        return ((ax * RING + ay) * 2 + (core + oc) % 2, (z + oz) % zs)

    def along(axis, o):
        return dev(o, 0) if axis == 0 else dev(0, o)

    def column(hf, a, b, c):
        ax, ay = (x + (a if hf == 0 else b)) % RING, (y + (b if hf == 0 else a)) % RING
        return pl.multiple_of(((ax * RING + ay) * 2 + c) * width, width)

    def offset(slot):
        return jnp.where(slot == 2, -1, jnp.where(slot == 3, 2, slot))

    def send(src, dst, family, recv_sem, device):
        pltpu.make_async_remote_copy(
            src_ref=src, dst_ref=dst, send_sem=send_sems.at[family], recv_sem=recv_sem,
            device_id=device, device_id_type=MESH).start()

    def wait(ref, sem):
        pltpu.make_async_copy(ref, ref, sem).wait()

    mom_load = pltpu.make_async_copy(mom_hbm, mom, mom_sem)
    group = RING * 2 * width

    def start_load(slot):
        for hf in both:
            at = pl.ds(hf * half_rows, half_rows)
            a = (x if hf == 0 else y) + OFFSETS[slot] + RING
            if hf == 0:
                columns = [pl.ds(pl.multiple_of(a % RING * group, group), group)]
            else:
                n = 2 * width
                columns = [pl.ds(pl.multiple_of((b * RING + a % RING) * n, n), n) for b in range(RING)]
            for col in columns:
                pltpu.make_async_copy(gw_hbm.at[0, at, col], gw.at[0, at, col], in_sems.at[slot, 0]).start()
                pltpu.make_async_copy(lw_hbm.at[0, 0, at, col], lw.at[0, at, col], in_sems.at[slot, 1]).start()

    later = [
        (pltpu.make_async_copy(gw_hbm.at[1], gw.at[1], in_sems.at[RING, 0])),
        (pltpu.make_async_copy(lw_hbm.at[0, 1], lw.at[1], in_sems.at[RING, 1]))]

    def load(f, slot):
        if f == 0:
            wait(gw.at[0, :, pl.ds(0, group)], in_sems.at[slot, 0])
            wait(lw.at[0, :, pl.ds(0, group)], in_sems.at[slot, 1])
        elif slot == 3:
            for copy in later:
                copy.wait()

    start_load(3)
    mom_load.start()

    near = [(0, 0, oc, oz) for oz in range(zs) for oc in range(2) if (oc, oz) != (0, 0)]
    far = [(ox, oy, 0, 0) for ox in range(RING) for oy in range(RING) if (ox, oy) != (0, 0)]
    greeted = [(0, 0, 1, 0)] + [p for o in (1, -1) for p in ((o, 0, 0, 0), (0, o, 0, 0), (0, 0, 0, o))]
    barrier = pltpu.get_barrier_semaphore()
    for partner in greeted:
        pl.semaphore_signal(barrier, inc=1, device_id=dev(*partner), device_id_type=MESH)
    for slot in (1, 2, 0):
        start_load(slot)
    pl.semaphore_wait(barrier, len(greeted))

    for o in (1, -1):
        pl.semaphore_signal(late_sem, inc=1, device_id=dev(0, 0, 0, o), device_id_type=MESH)
    for copy in later:
        copy.start()

    def known():
        pl.semaphore_wait(late_sem, 2)

    def difference(f, row, n, col):
        at = pl.ds(row, n)
        return gw[f, at, pl.ds(col, width)] - lw[f, at, pl.ds(col, width)].astype(F32)

    def to_core(f, slot, hf):
        @pl.loop(0, RING)
        def _(j):
            col = column(hf, OFFSETS[slot], offset(j), 1 - core)
            ds[f, slot, hf, j] = difference(f, hf * half_rows, half_rows, col).astype(BF16)
        send(ds.at[f, slot, hf], dr.at[f, slot, hf], 0, core_sems.at[f, slot], dev(0, 0, 1))

    def from_core(f, slot):
        wait(dr.at[f, slot], core_sems.at[f, slot])

    def pair_sum(f, hf, slot, j, row, n):
        col = column(hf, OFFSETS[slot], offset(j), core)
        return (difference(f, hf * half_rows + row, n, col)
                + dr[f, slot, hf, j, pl.ds(row, n)].astype(F32))

    def ring1_far(f, hf):
        for q, way in ((0, 1), (1, -1)):
            @pl.loop(0, RING)
            def _(j):
                s_send[f, hf, 2, q, j] = pair_sum(f, hf, 3, j, q * quarter, quarter).astype(BF16)
            send(s_send.at[f, hf, 2, q], s_mid.at[f, hf, q], 1, mid_sems.at[f], along(hf, way))

    def ring1_near(f, hf, slot):
        q, way = (1, 1) if slot == 1 else (0, -1)

        @pl.loop(0, RING)
        def _(j):
            s_send[f, hf, slot - 1, q, j] = pair_sum(f, hf, slot, j, q * quarter, quarter).astype(BF16)
        send(s_send.at[f, hf, slot - 1, q], s_end.at[f, hf, slot - 1, q], 1, end_sems.at[f], along(hf, way))

    def ring1_middle(f, hf):
        for slot, q, way in ((1, 0, 1), (2, 1, -1)):
            @pl.loop(0, RING)
            def _(j):
                total = pair_sum(f, hf, slot, j, q * quarter, quarter) + s_mid[f, hf, q, j].astype(F32)
                s_send[f, hf, slot - 1, q, j] = total.astype(BF16)
            send(s_send.at[f, hf, slot - 1, q], s_end.at[f, hf, slot - 1, q], 1, end_sems.at[f], along(hf, way))

    def ring2_open(f, hf):
        def whole(j, q):
            total = pair_sum(f, hf, 0, j, q * quarter, quarter)
            return total + s_end[f, hf, 0, q, j].astype(F32) + s_end[f, hf, 1, q, j].astype(F32)

        for slot in (3, 1, 2):
            for q in both:
                t_send[f, hf, slot - 1, pl.ds(q * quarter, quarter)] = whole(slot, q).astype(BF16)
            send(t_send.at[f, hf, slot - 1], t_end.at[f, hf, slot - 1], 2, end2_sems.at[f],
                 along(1 - hf, OFFSETS[slot]))
        for q in both:
            tt[f, hf, pl.ds(q * quarter, quarter)] = whole(0, q)

    def ring2_close(f, hf):
        part = tt[f, hf]
        for k in range(RING - 1):
            part = part + t_end[f, hf, k].astype(F32)
        part = part * (1.0 / (2 * RING * RING))
        av[f, pl.ds(hf * half_rows, half_rows)] = part

    def tile(part):
        square = jnp.sum((part * part).reshape(half_rows // 8, 8, width), axis=0)
        total = square[:, :128]
        for c in range(1, width // 128):
            total = total + square[:, c * 128:(c + 1) * 128]
        return total

    def exchange(f, stage, tiles, me, partners):
        for partner in partners:
            send(tiles.at[f, me], tiles.at[f, me], 3 + stage, norm_sems.at[f, stage], dev(*partner))

    def gathered(f, stage, tiles, partners):
        wait(tiles.at[f, pl.ds(0, len(partners))], norm_sems.at[f, stage])
        return jnp.sum(tiles[f], axis=0)

    def norm_open(f):
        at = pl.ds(half_rows, half_rows)
        n2[f, x * RING + y] = tile(av[f, pl.ds(0, half_rows)]) + tile(av[f, at])
        exchange(f, 1, n2, x * RING + y, far)

    def norm_middle(f):
        n1[f, z * 2 + core] = gathered(f, 1, n2, far)
        exchange(f, 0, n1, z * 2 + core, near)

    def factor_of(f):
        norm_squared = jnp.sum(gathered(f, 0, n1, near), axis=(0, 1), keepdims=True)
        return jnp.minimum(1.0, CLIP_LEVEL * jnp.sqrt(F32(count)) / jnp.sqrt(norm_squared + 1e-06))

    STEP, AVERAGE, MOMENT = 0, 1, 2
    FIRST, NEAR, LAST = pl.ds(0, 1), pl.ds(1, 2), pl.ds(3, 1)

    def gather1(s, hf, slot, k):
        back = (None, 2, 1, 3)[slot]
        send(g.at[s, hf, 0, 0], g.at[s, hf, 0, back], 5, gather_sems.at[s, k], along(1 - hf, OFFSETS[slot]))

    def gather2(s, hf, at, k):
        for slot, back in ((1, 2), (2, 1)):
            send(g.at[s, hf, 0, at], g.at[s, hf, back, at], 6, gather_sems.at[s, k], along(hf, OFFSETS[slot]))

    def gather2_pass(s, hf, at, k):
        k = 6 if k == 4 else 5
        for back, way, q in ((2, 1, 0), (1, -1, 1)):
            rows_at = pl.ds(q * quarter, quarter)
            send(g.at[s, hf, back, at, rows_at], g.at[s, hf, 3, at, rows_at], 6,
                 gather_sems.at[s, k], along(hf, way))

    def spread(s):
        for hf in both:
            for slot in (1, 2, 3)[:2 if s == MOMENT else 3]:
                gather1(s, hf, slot, slot // 3)
        for hf in both:
            gather2(s, hf, FIRST, 2)

    def share(i, *slots):
        for hf in both:
            for slot in slots:
                back = (None, 2, 1, 3)[slot]
                send(p.at[i, hf, 0], p.at[i, hf, back], 8, share_sems.at[i, slot // 3], along(1 - hf, OFFSETS[slot]))

    def share_average():
        for hf in both:
            p[0, hf, 0] = av[0, pl.ds(hf * half_rows, half_rows)].astype(BF16)
        share(0, 1, 2, 3)

    def spread_moment():
        mom_load.wait()
        for hf in both:
            at = pl.ds(hf * half_rows, half_rows)
            g[MOMENT, hf, 0, 0] = mom[1, at].astype(BF16)
            p[1, hf, 0] = mom[0, at].astype(BF16)
        spread(MOMENT)
        share(1, 1, 2)

    def spread_average():
        for hf in both:
            g[AVERAGE, hf, 0, 0] = av[1, pl.ds(hf * half_rows, half_rows)].astype(BF16)
        spread(AVERAGE)

    def spread_step():
        factor = factor_of(0)
        for i in (1, 0):
            wait(p.at[i, :, NEAR], share_sems.at[i, 0])
            wait(p.at[i, :, LAST], share_sems.at[i, 1])
        for at, slots, k in ((FIRST, (0,), 2), (NEAR, (1, 2), 3), (LAST, (3,), 4)):
            for hf in both:
                for slot in slots:
                    clipped = p[0, hf, slot].astype(F32) * factor
                    moment = OUTER_MOMENTUM * p[1, hf, slot].astype(F32) + clipped
                    g[STEP, hf, 0, slot] = (clipped + OUTER_MOMENTUM * moment).astype(BF16)
                gather2(STEP, hf, at, k)
        for hf in both:
            hand_over(STEP, hf, 0, 1, 0)
        mout[0] = OUTER_MOMENTUM * mom[0] + av[0] * factor

    def spread_far(s):
        for hf in both:
            gather1(s, hf, 3, 1)
        share(1, 3)

    scales = {STEP: OUTER_RATE, MOMENT: OUTER_RATE * OUTER_MOMENTUM * OUTER_MOMENTUM}

    def clip_average():
        factor = factor_of(1)
        mout[1] = OUTER_MOMENTUM * mom[1] + av[1] * factor
        scales[AVERAGE] = OUTER_RATE * (1.0 + OUTER_MOMENTUM) * factor

    def gather1_near(s):
        wait(g.at[s, :, 0, NEAR], gather_sems.at[s, 0])
        for hf in both:
            gather2(s, hf, NEAR, 3)

    def gather1_far(s):
        wait(g.at[s, :, 0, LAST], gather_sems.at[s, 1])
        for hf in both:
            gather2(s, hf, LAST, 4)
        for hf in both:
            hand_over(s, hf, 0, 1, 0)

    def gather2_passes(s, at, k):
        wait(g.at[s, :, pl.ds(1, 2), at], gather_sems.at[s, k])
        for hf in both:
            gather2_pass(s, hf, at, k)

    def gather2_first(s):
        gather2_passes(s, FIRST, 2)

    def gather2_near(s):
        gather2_passes(s, NEAR, 3)

    def gather2_far(s):
        gather2_passes(s, LAST, 4)
        for hf in both:
            hand_over(s, hf, 1, 2, 1)

    def gather2_last(s):
        most = pl.ds(0, RING - 1)
        wait(g.at[s, :, 3, most], gather_sems.at[s, 5])
        for hf in both:
            send(g.at[s, hf, 3, most], h.at[s, hf, 3, most], 7, hand_sems.at[s, 2], dev(0, 0, 1))

    def gather2_end(s):
        wait(g.at[s, :, 3, LAST], gather_sems.at[s, 6])
        for hf in both:
            send(g.at[s, hf, 3, LAST], h.at[s, hf, 3, LAST], 7, hand_sems.at[s, 3], dev(0, 0, 1))

    def hand_over(s, hf, slot, n, k):
        at = pl.ds(slot, n)
        send(g.at[s, hf, at], h.at[s, hf, at], 7, hand_sems.at[s, k], dev(0, 0, 1))

    def refresh(s, hf, slot, blocks, c, first=0, last=RING):
        f = 0 if s == STEP else 1
        at = pl.ds(hf * half_rows, half_rows)
        scale = scales[s]

        @pl.loop(first, last)
        def _(j):
            col = pl.ds(column(hf, OFFSETS[slot], offset(j), c), width)
            gw[f, at, col] = gw[f, at, col] - scale * blocks[s, hf, slot, j].astype(F32)

    def own(s, *slots):
        for hf in both:
            for slot in slots:
                refresh(s, hf, slot, g, core)

    def other(s, k):
        if k < 2:
            slot, n = ((0, 1), (1, 2))[k]
            wait(h.at[s, :, pl.ds(slot, n)], hand_sems.at[s, k])
            for hf in both:
                for i in range(n):
                    refresh(s, hf, slot + i, h, 1 - core)
        else:
            for k, first, last in ((2, 0, RING - 1), (3, RING - 1, RING)):
                wait(h.at[s, :, 3, pl.ds(first, last - first)], hand_sems.at[s, k])
                for hf in both:
                    refresh(s, hf, 3, h, 1 - core, first, last)

    steps = []

    def step(work, *args):
        steps.append((work, args))

    def halves(work, f):
        for hf in both:
            work(f, hf)

    def core_step(f, slot):
        load(f, slot)
        for hf in both:
            to_core(f, slot, hf)

    def far_step(f):
        from_core(f, 3)
        halves(ring1_far, f)

    def near_step(f, slot):
        from_core(f, slot)
        for hf in both:
            ring1_near(f, hf, slot)

    def middle_step(f):
        wait(s_mid.at[f], mid_sems.at[f])
        halves(ring1_middle, f)

    def open_step(f):
        from_core(f, 0)
        wait(s_end.at[f], end_sems.at[f])
        halves(ring2_open, f)

    def close_step(f):
        wait(t_end.at[f], end2_sems.at[f])
        halves(ring2_close, f)

    step(spread_moment)
    step(core_step, 0, 3)
    step(core_step, 0, 1)
    step(far_step, 0)
    step(core_step, 0, 2)
    step(near_step, 0, 1)
    step(core_step, 0, 0)
    step(near_step, 0, 2)
    step(known)
    step(core_step, 1, 3)
    step(core_step, 1, 1)
    step(core_step, 1, 2)
    step(far_step, 1)
    step(core_step, 1, 0)
    step(middle_step, 0)
    step(near_step, 1, 1)
    step(near_step, 1, 2)
    step(middle_step, 1)
    step(spread_far, MOMENT)
    step(open_step, 0)
    step(gather1_near, MOMENT)
    step(open_step, 1)
    step(close_step, 0)
    step(norm_open, 0)
    step(share_average)
    step(gather1_far, MOMENT)
    step(gather2_first, MOMENT)
    step(close_step, 1)
    step(norm_open, 1)
    step(spread_average)
    step(gather2_near, MOMENT)
    step(norm_middle, 0)
    step(gather2_far, MOMENT)
    step(own, MOMENT, 0)
    step(gather1_near, AVERAGE)
    step(gather1_far, AVERAGE)
    step(spread_step)
    step(gather2_first, AVERAGE)
    step(norm_middle, 1)
    step(gather2_near, AVERAGE)
    step(gather2_first, STEP)
    step(gather2_far, AVERAGE)
    step(own, MOMENT, 1, 2)
    step(gather2_near, STEP)
    step(gather2_far, STEP)
    step(gather2_last, MOMENT)
    step(gather2_end, MOMENT)
    step(other, MOMENT, 0)
    step(other, MOMENT, 1)
    step(own, MOMENT, 3)
    step(clip_average)
    step(gather2_last, AVERAGE)
    step(gather2_end, AVERAGE)
    step(other, MOMENT, 2)
    step(own, AVERAGE, 0, 1, 2, 3)
    step(other, AVERAGE, 0)
    step(other, AVERAGE, 1)
    step(other, AVERAGE, 2)
    step(gather2_last, STEP)
    step(own, STEP, 0)
    step(gather2_end, STEP)
    step(other, STEP, 0)
    step(own, STEP, 1, 2)
    step(other, STEP, 1)
    step(own, STEP, 3)
    step(other, STEP, 2)

    for work, args in steps:
        work(*args)

    wait(ds, send_sems.at[0])
    wait(s_send, send_sems.at[1])
    wait(t_send, send_sems.at[2])
    wait(n1.at[:, pl.ds(0, len(near))], send_sems.at[3])
    wait(n2.at[:, pl.ds(0, len(far))], send_sems.at[4])
    wait(g.at[pl.ds(1, frags), :, 0, pl.ds(0, 3)], send_sems.at[5])
    wait(g.at[:, :, pl.ds(0, 3)], send_sems.at[6])
    wait(h, send_sems.at[7])
    wait(p.at[:, :, pl.ds(0, 3)], send_sems.at[8])


def store(refreshed, moment, refreshed_out, moment_out, sems):
    frags, rows, _ = refreshed.shape
    n = rows // PARTS
    copies = [pltpu.make_async_copy(moment, moment_out, sems.at[frags * PARTS])]
    for f in range(frags):
        for i in range(PARTS):
            at = pl.ds(i * n, n)
            copies.append(pltpu.make_async_copy(refreshed.at[f, at], refreshed_out.at[f, at], sems.at[f * PARTS + i]))
    for copy in copies:
        copy.start()
    for copy in copies:
        copy.wait()


def synchronize(local_weights, global_weights, momentum):
    frags, rows, cols = global_weights.shape
    width = momentum.shape[2]
    zs = lax.axis_size("fsdp")
    assert lax.axis_size("replica") == 2 * RING * RING and frags == 2
    half_rows, quarter = rows // 2, rows // 4
    anywhere = pl.BlockSpec(memory_space=pl.ANY)
    in_vmem = pl.BlockSpec(memory_space=pltpu.VMEM)
    dma = pltpu.SemaphoreType.DMA
    refreshed, moment = pl.pallas_call(
        functools.partial(kernel, zs, rows * zs * cols),
        out_shape=(pltpu.VMEM(global_weights.shape, F32), pltpu.VMEM(momentum.shape, F32)),
        in_specs=[anywhere] * 3,
        out_specs=(in_vmem, in_vmem),
        scratch_shapes=[
            pltpu.VMEM((frags, rows, cols), BF16),
            pltpu.VMEM((frags, rows, width), F32),
            pltpu.VMEM((frags, RING, 2, RING, half_rows, width), BF16),
            pltpu.VMEM((frags, RING, 2, RING, half_rows, width), BF16),
            pltpu.VMEM((frags, 2, RING - 1, 2, RING, quarter, width), BF16),
            pltpu.VMEM((frags, 2, 2, RING, quarter, width), BF16),
            pltpu.VMEM((frags, 2, 2, 2, RING, quarter, width), BF16),
            pltpu.VMEM((frags, 2, half_rows, width), F32),
            pltpu.VMEM((frags, 2, RING - 1, half_rows, width), BF16),
            pltpu.VMEM((frags, 2, RING - 1, half_rows, width), BF16),
            pltpu.VMEM((frags, rows, width), F32),
            pltpu.VMEM((frags, 2 * zs, 8, 128), F32),
            pltpu.VMEM((frags, RING * RING, 8, 128), F32),
            pltpu.VMEM((frags + 1, 2, RING, RING, half_rows, width), BF16),
            pltpu.VMEM((frags + 1, 2, RING, RING, half_rows, width), BF16),
            pltpu.VMEM((2, 2, RING, half_rows, width), BF16),
            dma((RING + 1, 2)),
            dma,
            pltpu.SemaphoreType.REGULAR,
            dma((9,)),
            dma((frags, 2)),
            dma((frags, RING)),
            dma((frags,)),
            dma((frags,)),
            dma((frags,)),
            dma((frags + 1, 7)),
            dma((frags + 1, 4)),
            dma((2, 2)),
        ],
        compiler_params=pltpu.CompilerParams(
            collective_id=0, has_side_effects=True, vmem_limit_bytes=50 * 2**20
        ),
        cost_estimate=pl.CostEstimate(flops=20 * rows * cols, bytes_accessed=20 * frags * rows * cols // 2, transcendentals=0),
    )(local_weights, global_weights, momentum)
    return pl.pallas_call(
        store,
        out_shape=(
            jax.ShapeDtypeStruct(global_weights.shape, F32),
            jax.ShapeDtypeStruct(momentum.shape, F32),
        ),
        in_specs=[in_vmem, in_vmem],
        out_specs=(anywhere, anywhere),
        scratch_shapes=[dma((frags * PARTS + 1,))],
        compiler_params=pltpu.CompilerParams(vmem_limit_bytes=2 * 2**20),
    )(refreshed, moment)


def solution(mesh):
    return jax.shard_map(
        synchronize,
        mesh=mesh,
        in_specs=(
            P("replica", None, "fsdp", None),
            P(None, "fsdp", None),
            P(None, "fsdp", "replica"),
        ),
        out_specs=(P(None, "fsdp", None), P(None, "fsdp", "replica")),
        check_vma=False,
    )
```

```python
import functools

import jax
import jax.numpy as jnp
from jax import lax
from jax.experimental import pallas as pl
from jax.experimental.pallas import tpu as pltpu
from jax.sharding import PartitionSpec as P

OUTER_MOMENTUM = 0.9
OUTER_RATE = 0.7
CLIP_LEVEL = 1.0
MESH = pl.DeviceIdType.MESH
RING = 4
PARTS = 2
OFFSETS = (0, 1, -1, 2)
F32, BF16 = jnp.float32, jnp.bfloat16


def kernel(zs, count, lw_hbm, gw_hbm, mom_hbm, gw, mout,
           lw, mom, ds, dr, s_send, s_mid, s_end, tt, t_send, t_end, av, n1, n2, g, h, p,
           in_sems, mom_sem, late_sem, send_sems, norm_sems, core_sems, mid_sems, end_sems, end2_sems, gather_sems, hand_sems, share_sems):
    frags, rows, _ = gw.shape
    width = mom.shape[2]
    half_rows, quarter = rows // 2, rows // 4
    r = lax.axis_index("replica")
    z = lax.axis_index("fsdp")
    core = r % 2
    y = (r // 2) % RING
    x = r // (2 * RING)
    both = range(2)

    def dev(ox, oy, oc=0, oz=0):
        ax, ay = (x + ox) % RING, (y + oy) % RING
        return ((ax * RING + ay) * 2 + (core + oc) % 2, (z + oz) % zs)

    def along(axis, o):
        return dev(o, 0) if axis == 0 else dev(0, o)

    def column(hf, a, b, c):
        ax, ay = (x + (a if hf == 0 else b)) % RING, (y + (b if hf == 0 else a)) % RING
        return pl.multiple_of(((ax * RING + ay) * 2 + c) * width, width)

    def offset(slot):
        return jnp.where(slot == 2, -1, jnp.where(slot == 3, 2, slot))

    def send(src, dst, family, recv_sem, device):
        pltpu.make_async_remote_copy(
            src_ref=src, dst_ref=dst, send_sem=send_sems.at[family], recv_sem=recv_sem,
            device_id=device, device_id_type=MESH).start()

    def wait(ref, sem):
        pltpu.make_async_copy(ref, ref, sem).wait()

    mom_load = pltpu.make_async_copy(mom_hbm, mom, mom_sem)
    group = RING * 2 * width

    def start_load(slot):
        for hf in both:
            at = pl.ds(hf * half_rows, half_rows)
            a = (x if hf == 0 else y) + OFFSETS[slot] + RING
            if hf == 0:
                columns = [pl.ds(pl.multiple_of(a % RING * group, group), group)]
            else:
                n = 2 * width
                columns = [pl.ds(pl.multiple_of((b * RING + a % RING) * n, n), n) for b in range(RING)]
            for col in columns:
                pltpu.make_async_copy(gw_hbm.at[0, at, col], gw.at[0, at, col], in_sems.at[slot, 0]).start()
                pltpu.make_async_copy(lw_hbm.at[0, 0, at, col], lw.at[0, at, col], in_sems.at[slot, 1]).start()

    later = [
        (pltpu.make_async_copy(gw_hbm.at[1], gw.at[1], in_sems.at[RING, 0])),
        (pltpu.make_async_copy(lw_hbm.at[0, 1], lw.at[1], in_sems.at[RING, 1]))]

    def load(f, slot):
        if f == 0:
            wait(gw.at[0, :, pl.ds(0, group)], in_sems.at[slot, 0])
            wait(lw.at[0, :, pl.ds(0, group)], in_sems.at[slot, 1])
        elif slot == 3:
            for copy in later:
                copy.wait()

    start_load(3)
    mom_load.start()

    near = [(0, 0, oc, oz) for oz in range(zs) for oc in range(2) if (oc, oz) != (0, 0)]
    far = [(ox, oy, 0, 0) for ox in range(RING) for oy in range(RING) if (ox, oy) != (0, 0)]
    greeted = [(0, 0, 1, 0)] + [p for o in (1, -1) for p in ((o, 0, 0, 0), (0, o, 0, 0), (0, 0, 0, o))]
    barrier = pltpu.get_barrier_semaphore()
    for partner in greeted:
        pl.semaphore_signal(barrier, inc=1, device_id=dev(*partner), device_id_type=MESH)
    for slot in (1, 2, 0):
        start_load(slot)
    pl.semaphore_wait(barrier, len(greeted))

    for o in (1, -1):
        pl.semaphore_signal(late_sem, inc=1, device_id=dev(0, 0, 0, o), device_id_type=MESH)
    for copy in later:
        copy.start()

    def known():
        pl.semaphore_wait(late_sem, 2)

    def difference(f, row, n, col):
        at = pl.ds(row, n)
        return gw[f, at, pl.ds(col, width)] - lw[f, at, pl.ds(col, width)].astype(F32)

    def to_core(f, slot, hf):
        @pl.loop(0, RING)
        def _(j):
            col = column(hf, OFFSETS[slot], offset(j), 1 - core)
            ds[f, slot, hf, j] = difference(f, hf * half_rows, half_rows, col).astype(BF16)
        send(ds.at[f, slot, hf], dr.at[f, slot, hf], 0, core_sems.at[f, slot], dev(0, 0, 1))

    def from_core(f, slot):
        wait(dr.at[f, slot], core_sems.at[f, slot])

    def pair_sum(f, hf, slot, j, row, n):
        col = column(hf, OFFSETS[slot], offset(j), core)
        return (difference(f, hf * half_rows + row, n, col)
                + dr[f, slot, hf, j, pl.ds(row, n)].astype(F32))

    def ring1_far(f, hf):
        for q, way in ((0, 1), (1, -1)):
            @pl.loop(0, RING)
            def _(j):
                s_send[f, hf, 2, q, j] = pair_sum(f, hf, 3, j, q * quarter, quarter).astype(BF16)
            send(s_send.at[f, hf, 2, q], s_mid.at[f, hf, q], 1, mid_sems.at[f], along(hf, way))

    def ring1_near(f, hf, slot):
        q, way = (1, 1) if slot == 1 else (0, -1)

        @pl.loop(0, RING)
        def _(j):
            s_send[f, hf, slot - 1, q, j] = pair_sum(f, hf, slot, j, q * quarter, quarter).astype(BF16)
        send(s_send.at[f, hf, slot - 1, q], s_end.at[f, hf, slot - 1, q], 1, end_sems.at[f], along(hf, way))

    def ring1_middle(f, hf):
        for slot, q, way in ((1, 0, 1), (2, 1, -1)):
            @pl.loop(0, RING)
            def _(j):
                total = pair_sum(f, hf, slot, j, q * quarter, quarter) + s_mid[f, hf, q, j].astype(F32)
                s_send[f, hf, slot - 1, q, j] = total.astype(BF16)
            send(s_send.at[f, hf, slot - 1, q], s_end.at[f, hf, slot - 1, q], 1, end_sems.at[f], along(hf, way))

    def ring2_open(f, hf):
        def whole(j, q):
            total = pair_sum(f, hf, 0, j, q * quarter, quarter)
            return total + s_end[f, hf, 0, q, j].astype(F32) + s_end[f, hf, 1, q, j].astype(F32)

        for slot in (3, 1, 2):
            for q in both:
                t_send[f, hf, slot - 1, pl.ds(q * quarter, quarter)] = whole(slot, q).astype(BF16)
            send(t_send.at[f, hf, slot - 1], t_end.at[f, hf, slot - 1], 2, end2_sems.at[f],
                 along(1 - hf, OFFSETS[slot]))
        for q in both:
            tt[f, hf, pl.ds(q * quarter, quarter)] = whole(0, q)

    def ring2_close(f, hf):
        part = tt[f, hf]
        for k in range(RING - 1):
            part = part + t_end[f, hf, k].astype(F32)
        part = part * (1.0 / (2 * RING * RING))
        av[f, pl.ds(hf * half_rows, half_rows)] = part

    def tile(part):
        square = jnp.sum((part * part).reshape(half_rows // 8, 8, width), axis=0)
        total = square[:, :128]
        for c in range(1, width // 128):
            total = total + square[:, c * 128:(c + 1) * 128]
        return total

    def exchange(f, stage, tiles, me, partners):
        for partner in partners:
            send(tiles.at[f, me], tiles.at[f, me], 3 + stage, norm_sems.at[f, stage], dev(*partner))

    def gathered(f, stage, tiles, partners):
        wait(tiles.at[f, pl.ds(0, len(partners))], norm_sems.at[f, stage])
        return jnp.sum(tiles[f], axis=0)

    def norm_open(f):
        at = pl.ds(half_rows, half_rows)
        n2[f, x * RING + y] = tile(av[f, pl.ds(0, half_rows)]) + tile(av[f, at])
        exchange(f, 1, n2, x * RING + y, far)

    def norm_middle(f):
        n1[f, z * 2 + core] = gathered(f, 1, n2, far)
        exchange(f, 0, n1, z * 2 + core, near)

    def factor_of(f):
        norm_squared = jnp.sum(gathered(f, 0, n1, near), axis=(0, 1), keepdims=True)
        return jnp.minimum(1.0, CLIP_LEVEL * jnp.sqrt(F32(count)) / jnp.sqrt(norm_squared + 1e-06))

    STEP, AVERAGE, MOMENT = 0, 1, 2
    FIRST, NEAR, LAST = pl.ds(0, 1), pl.ds(1, 2), pl.ds(3, 1)

    def gather1(s, hf, slot, k):
        back = (None, 2, 1, 3)[slot]
        send(g.at[s, hf, 0, 0], g.at[s, hf, 0, back], 5, gather_sems.at[s, k], along(1 - hf, OFFSETS[slot]))

    def gather2(s, hf, at, k):
        for slot, back in ((1, 2), (2, 1)):
            send(g.at[s, hf, 0, at], g.at[s, hf, back, at], 6, gather_sems.at[s, k], along(hf, OFFSETS[slot]))

    def gather2_pass(s, hf, at, k):
        k = 6 if k == 4 else 5
        for back, way, q in ((2, 1, 0), (1, -1, 1)):
            rows_at = pl.ds(q * quarter, quarter)
            send(g.at[s, hf, back, at, rows_at], g.at[s, hf, 3, at, rows_at], 6,
                 gather_sems.at[s, k], along(hf, way))

    def spread(s):
        for hf in both:
            for slot in (1, 2, 3)[:2 if s == MOMENT else 3]:
                gather1(s, hf, slot, slot // 3)
        for hf in both:
            gather2(s, hf, FIRST, 2)

    def share(i, *slots):
        for hf in both:
            for slot in slots:
                back = (None, 2, 1, 3)[slot]
                send(p.at[i, hf, 0], p.at[i, hf, back], 8, share_sems.at[i, slot // 3], along(1 - hf, OFFSETS[slot]))

    def share_average():
        for hf in both:
            p[0, hf, 0] = av[0, pl.ds(hf * half_rows, half_rows)].astype(BF16)
        share(0, 1, 2, 3)

    def spread_moment():
        mom_load.wait()
        for hf in both:
            at = pl.ds(hf * half_rows, half_rows)
            g[MOMENT, hf, 0, 0] = mom[1, at].astype(BF16)
            p[1, hf, 0] = mom[0, at].astype(BF16)
        spread(MOMENT)
        share(1, 1, 2)

    def spread_average():
        for hf in both:
            g[AVERAGE, hf, 0, 0] = av[1, pl.ds(hf * half_rows, half_rows)].astype(BF16)
        spread(AVERAGE)

    def spread_step():
        factor = factor_of(0)
        for i in (1, 0):
            wait(p.at[i, :, NEAR], share_sems.at[i, 0])
            wait(p.at[i, :, LAST], share_sems.at[i, 1])
        for at, slots, k in ((FIRST, (0,), 2), (NEAR, (1, 2), 3), (LAST, (3,), 4)):
            for hf in both:
                for slot in slots:
                    clipped = p[0, hf, slot].astype(F32) * factor
                    moment = OUTER_MOMENTUM * p[1, hf, slot].astype(F32) + clipped
                    g[STEP, hf, 0, slot] = (clipped + OUTER_MOMENTUM * moment).astype(BF16)
                gather2(STEP, hf, at, k)
        for hf in both:
            hand_over(STEP, hf, 0, 1, 0)
        mout[0] = OUTER_MOMENTUM * mom[0] + av[0] * factor

    def spread_far(s):
        for hf in both:
            gather1(s, hf, 3, 1)
        share(1, 3)

    scales = {STEP: OUTER_RATE, MOMENT: OUTER_RATE * OUTER_MOMENTUM * OUTER_MOMENTUM}

    def clip_average():
        factor = factor_of(1)
        mout[1] = OUTER_MOMENTUM * mom[1] + av[1] * factor
        scales[AVERAGE] = OUTER_RATE * (1.0 + OUTER_MOMENTUM) * factor

    def gather1_near(s):
        wait(g.at[s, :, 0, NEAR], gather_sems.at[s, 0])
        for hf in both:
            gather2(s, hf, NEAR, 3)

    def gather1_far(s):
        wait(g.at[s, :, 0, LAST], gather_sems.at[s, 1])
        for hf in both:
            gather2(s, hf, LAST, 4)
        for hf in both:
            hand_over(s, hf, 0, 1, 0)

    def gather2_passes(s, at, k):
        wait(g.at[s, :, pl.ds(1, 2), at], gather_sems.at[s, k])
        for hf in both:
            gather2_pass(s, hf, at, k)

    def gather2_first(s):
        gather2_passes(s, FIRST, 2)

    def gather2_near(s):
        gather2_passes(s, NEAR, 3)

    def gather2_far(s):
        gather2_passes(s, LAST, 4)
        for hf in both:
            hand_over(s, hf, 1, 2, 1)

    def gather2_last(s):
        most = pl.ds(0, RING - 1)
        wait(g.at[s, :, 3, most], gather_sems.at[s, 5])
        for hf in both:
            send(g.at[s, hf, 3, most], h.at[s, hf, 3, most], 7, hand_sems.at[s, 2], dev(0, 0, 1))

    def gather2_end(s):
        wait(g.at[s, :, 3, LAST], gather_sems.at[s, 6])
        for hf in both:
            send(g.at[s, hf, 3, LAST], h.at[s, hf, 3, LAST], 7, hand_sems.at[s, 3], dev(0, 0, 1))

    def hand_over(s, hf, slot, n, k):
        at = pl.ds(slot, n)
        send(g.at[s, hf, at], h.at[s, hf, at], 7, hand_sems.at[s, k], dev(0, 0, 1))

    def refresh(s, hf, slot, blocks, c, first=0, last=RING):
        f = 0 if s == STEP else 1
        at = pl.ds(hf * half_rows, half_rows)
        scale = scales[s]

        @pl.loop(first, last)
        def _(j):
            col = pl.ds(column(hf, OFFSETS[slot], offset(j), c), width)
            gw[f, at, col] = gw[f, at, col] - scale * blocks[s, hf, slot, j].astype(F32)

    def own(s, *slots):
        for hf in both:
            for slot in slots:
                refresh(s, hf, slot, g, core)

    def other(s, k):
        if k < 2:
            slot, n = ((0, 1), (1, 2))[k]
            wait(h.at[s, :, pl.ds(slot, n)], hand_sems.at[s, k])
            for hf in both:
                for i in range(n):
                    refresh(s, hf, slot + i, h, 1 - core)
        else:
            for k, first, last in ((2, 0, RING - 1), (3, RING - 1, RING)):
                wait(h.at[s, :, 3, pl.ds(first, last - first)], hand_sems.at[s, k])
                for hf in both:
                    refresh(s, hf, 3, h, 1 - core, first, last)

    steps = []

    def step(work, *args):
        steps.append((work, args))

    def halves(work, f):
        for hf in both:
            work(f, hf)

    def core_step(f, slot):
        load(f, slot)
        for hf in both:
            to_core(f, slot, hf)

    def far_step(f):
        from_core(f, 3)
        halves(ring1_far, f)

    def near_step(f, slot):
        from_core(f, slot)
        for hf in both:
            ring1_near(f, hf, slot)

    def middle_step(f):
        wait(s_mid.at[f], mid_sems.at[f])
        halves(ring1_middle, f)

    def open_step(f):
        from_core(f, 0)
        wait(s_end.at[f], end_sems.at[f])
        halves(ring2_open, f)

    def close_step(f):
        wait(t_end.at[f], end2_sems.at[f])
        halves(ring2_close, f)

    step(spread_moment)
    step(core_step, 0, 3)
    step(core_step, 0, 1)
    step(far_step, 0)
    step(core_step, 0, 2)
    step(near_step, 0, 1)
    step(core_step, 0, 0)
    step(near_step, 0, 2)
    step(known)
    step(core_step, 1, 3)
    step(core_step, 1, 1)
    step(core_step, 1, 2)
    step(far_step, 1)
    step(core_step, 1, 0)
    step(middle_step, 0)
    step(spread_far, MOMENT)
    step(near_step, 1, 1)
    step(near_step, 1, 2)
    step(middle_step, 1)
    step(open_step, 0)
    step(gather1_near, MOMENT)
    step(gather1_far, MOMENT)
    step(open_step, 1)
    step(close_step, 0)
    step(norm_open, 0)
    step(share_average)
    step(gather2_first, MOMENT)
    step(close_step, 1)
    step(spread_average)
    step(norm_open, 1)
    step(gather2_near, MOMENT)
    step(norm_middle, 0)
    step(gather2_far, MOMENT)
    step(own, MOMENT, 0)
    step(gather1_near, AVERAGE)
    step(gather1_far, AVERAGE)
    step(own, MOMENT, 1)
    step(gather2_first, AVERAGE)
    step(spread_step)
    step(own, MOMENT, 2)
    step(gather2_last, MOMENT)
    step(gather2_end, MOMENT)
    step(other, MOMENT, 0)
    step(gather2_near, AVERAGE)
    step(norm_middle, 1)
    step(gather2_first, STEP)
    step(gather2_far, AVERAGE)
    step(other, MOMENT, 1)
    step(own, MOMENT, 3)
    step(gather2_near, STEP)
    step(gather2_far, STEP)
    step(other, MOMENT, 2)
    step(clip_average)
    step(own, AVERAGE, 0, 1, 2)
    step(other, AVERAGE, 0)
    step(gather2_last, AVERAGE)
    step(gather2_end, AVERAGE)
    step(own, STEP, 0, 1, 2)
    step(other, STEP, 0)
    step(other, AVERAGE, 1)
    step(gather2_last, STEP)
    step(own, AVERAGE, 3)
    step(gather2_end, STEP)
    step(other, STEP, 1)
    step(other, AVERAGE, 2)
    step(own, STEP, 3)
    step(other, STEP, 2)

    for work, args in steps:
        work(*args)

    wait(ds, send_sems.at[0])
    wait(s_send, send_sems.at[1])
    wait(t_send, send_sems.at[2])
    wait(n1.at[:, pl.ds(0, len(near))], send_sems.at[3])
    wait(n2.at[:, pl.ds(0, len(far))], send_sems.at[4])
    wait(g.at[pl.ds(1, frags), :, 0, pl.ds(0, 3)], send_sems.at[5])
    wait(g.at[:, :, pl.ds(0, 3)], send_sems.at[6])
    wait(h, send_sems.at[7])
    wait(p.at[:, :, pl.ds(0, 3)], send_sems.at[8])


def store(refreshed, moment, refreshed_out, moment_out, sems):
    frags, rows, _ = refreshed.shape
    n = rows // PARTS
    copies = [pltpu.make_async_copy(moment, moment_out, sems.at[frags * PARTS])]
    for f in range(frags):
        for i in range(PARTS):
            at = pl.ds(i * n, n)
            copies.append(pltpu.make_async_copy(refreshed.at[f, at], refreshed_out.at[f, at], sems.at[f * PARTS + i]))
    for copy in copies:
        copy.start()
    for copy in copies:
        copy.wait()


def synchronize(local_weights, global_weights, momentum):
    frags, rows, cols = global_weights.shape
    width = momentum.shape[2]
    zs = lax.axis_size("fsdp")
    assert lax.axis_size("replica") == 2 * RING * RING and frags == 2
    half_rows, quarter = rows // 2, rows // 4
    anywhere = pl.BlockSpec(memory_space=pl.ANY)
    in_vmem = pl.BlockSpec(memory_space=pltpu.VMEM)
    dma = pltpu.SemaphoreType.DMA
    refreshed, moment = pl.pallas_call(
        functools.partial(kernel, zs, rows * zs * cols),
        out_shape=(pltpu.VMEM(global_weights.shape, F32), pltpu.VMEM(momentum.shape, F32)),
        in_specs=[anywhere] * 3,
        out_specs=(in_vmem, in_vmem),
        scratch_shapes=[
            pltpu.VMEM((frags, rows, cols), BF16),
            pltpu.VMEM((frags, rows, width), F32),
            pltpu.VMEM((frags, RING, 2, RING, half_rows, width), BF16),
            pltpu.VMEM((frags, RING, 2, RING, half_rows, width), BF16),
            pltpu.VMEM((frags, 2, RING - 1, 2, RING, quarter, width), BF16),
            pltpu.VMEM((frags, 2, 2, RING, quarter, width), BF16),
            pltpu.VMEM((frags, 2, 2, 2, RING, quarter, width), BF16),
            pltpu.VMEM((frags, 2, half_rows, width), F32),
            pltpu.VMEM((frags, 2, RING - 1, half_rows, width), BF16),
            pltpu.VMEM((frags, 2, RING - 1, half_rows, width), BF16),
            pltpu.VMEM((frags, rows, width), F32),
            pltpu.VMEM((frags, 2 * zs, 8, 128), F32),
            pltpu.VMEM((frags, RING * RING, 8, 128), F32),
            pltpu.VMEM((frags + 1, 2, RING, RING, half_rows, width), BF16),
            pltpu.VMEM((frags + 1, 2, RING, RING, half_rows, width), BF16),
            pltpu.VMEM((2, 2, RING, half_rows, width), BF16),
            dma((RING + 1, 2)),
            dma,
            pltpu.SemaphoreType.REGULAR,
            dma((9,)),
            dma((frags, 2)),
            dma((frags, RING)),
            dma((frags,)),
            dma((frags,)),
            dma((frags,)),
            dma((frags + 1, 7)),
            dma((frags + 1, 4)),
            dma((2, 2)),
        ],
        compiler_params=pltpu.CompilerParams(
            collective_id=0, has_side_effects=True, vmem_limit_bytes=50 * 2**20
        ),
        cost_estimate=pl.CostEstimate(flops=20 * rows * cols, bytes_accessed=20 * frags * rows * cols // 2, transcendentals=0),
    )(local_weights, global_weights, momentum)
    return pl.pallas_call(
        store,
        out_shape=(
            jax.ShapeDtypeStruct(global_weights.shape, F32),
            jax.ShapeDtypeStruct(momentum.shape, F32),
        ),
        in_specs=[in_vmem, in_vmem],
        out_specs=(anywhere, anywhere),
        scratch_shapes=[dma((frags * PARTS + 1,))],
        compiler_params=pltpu.CompilerParams(vmem_limit_bytes=2 * 2**20),
    )(refreshed, moment)


def solution(mesh):
    return jax.shard_map(
        synchronize,
        mesh=mesh,
        in_specs=(
            P("replica", None, "fsdp", None),
            P(None, "fsdp", None),
            P(None, "fsdp", "replica"),
        ),
        out_specs=(P(None, "fsdp", None), P(None, "fsdp", "replica")),
        check_vma=False,
    )
```

```python
import functools

import jax
import jax.numpy as jnp
from jax import lax
from jax.experimental import pallas as pl
from jax.experimental.pallas import tpu as pltpu
from jax.sharding import PartitionSpec as P

OUTER_MOMENTUM = 0.9
OUTER_RATE = 0.7
CLIP_LEVEL = 1.0
MESH = pl.DeviceIdType.MESH
RING = 4
PARTS = 2
OFFSETS = (0, 1, -1, 2)
F32, BF16 = jnp.float32, jnp.bfloat16


def kernel(zs, count, lw_hbm, gw_hbm, mom_hbm, gw, mout,
           lw, mom, ds, dr, s_send, s_mid, s_end, tt, t_send, t_end, av, n1, n2, g, h, p,
           in_sems, mom_sem, late_sem, send_sems, norm_sems, core_sems, mid_sems, end_sems, end2_sems, gather_sems, hand_sems, share_sems):
    frags, rows, _ = gw.shape
    width = mom.shape[2]
    half_rows, quarter = rows // 2, rows // 4
    r = lax.axis_index("replica")
    z = lax.axis_index("fsdp")
    core = r % 2
    y = (r // 2) % RING
    x = r // (2 * RING)
    both = range(2)

    def dev(ox, oy, oc=0, oz=0):
        ax, ay = (x + ox) % RING, (y + oy) % RING
        return ((ax * RING + ay) * 2 + (core + oc) % 2, (z + oz) % zs)

    def along(axis, o):
        return dev(o, 0) if axis == 0 else dev(0, o)

    def column(hf, a, b, c):
        ax, ay = (x + (a if hf == 0 else b)) % RING, (y + (b if hf == 0 else a)) % RING
        return pl.multiple_of(((ax * RING + ay) * 2 + c) * width, width)

    def offset(slot):
        return jnp.where(slot == 2, -1, jnp.where(slot == 3, 2, slot))

    def send(src, dst, family, recv_sem, device):
        pltpu.make_async_remote_copy(
            src_ref=src, dst_ref=dst, send_sem=send_sems.at[family], recv_sem=recv_sem,
            device_id=device, device_id_type=MESH).start()

    def wait(ref, sem):
        pltpu.make_async_copy(ref, ref, sem).wait()

    mom_load = pltpu.make_async_copy(mom_hbm, mom, mom_sem)
    group = RING * 2 * width

    def start_load(slot):
        for hf in both:
            at = pl.ds(hf * half_rows, half_rows)
            a = (x if hf == 0 else y) + OFFSETS[slot] + RING
            if hf == 0:
                columns = [pl.ds(pl.multiple_of(a % RING * group, group), group)]
            else:
                n = 2 * width
                columns = [pl.ds(pl.multiple_of((b * RING + a % RING) * n, n), n) for b in range(RING)]
            for col in columns:
                pltpu.make_async_copy(gw_hbm.at[0, at, col], gw.at[0, at, col], in_sems.at[slot, 0]).start()
                pltpu.make_async_copy(lw_hbm.at[0, 0, at, col], lw.at[0, at, col], in_sems.at[slot, 1]).start()

    later = [
        (pltpu.make_async_copy(gw_hbm.at[1], gw.at[1], in_sems.at[RING, 0])),
        (pltpu.make_async_copy(lw_hbm.at[0, 1], lw.at[1], in_sems.at[RING, 1]))]

    def load(f, slot):
        if f == 0:
            wait(gw.at[0, :, pl.ds(0, group)], in_sems.at[slot, 0])
            wait(lw.at[0, :, pl.ds(0, group)], in_sems.at[slot, 1])
        elif slot == 3:
            for copy in later:
                copy.wait()

    near = [(0, 0, oc, oz) for oz in range(zs) for oc in range(2) if (oc, oz) != (0, 0)]
    far = [(ox, oy, 0, 0) for ox in range(RING) for oy in range(RING) if (ox, oy) != (0, 0)]
    greeted = [(0, 0, 1, 0)] + [p for o in (1, -1) for p in ((o, 0, 0, 0), (0, o, 0, 0), (0, 0, 0, o))]
    barrier = pltpu.get_barrier_semaphore()
    for partner in greeted:
        pl.semaphore_signal(barrier, inc=1, device_id=dev(*partner), device_id_type=MESH)
    start_load(3)
    mom_load.start()
    for slot in (1, 2, 0):
        start_load(slot)
    pl.semaphore_wait(barrier, len(greeted))

    for o in (1, -1):
        pl.semaphore_signal(late_sem, inc=1, device_id=dev(0, 0, 0, o), device_id_type=MESH)
    for copy in later:
        copy.start()

    def known():
        pl.semaphore_wait(late_sem, 2)

    def difference(f, row, n, col):
        at = pl.ds(row, n)
        return gw[f, at, pl.ds(col, width)] - lw[f, at, pl.ds(col, width)].astype(F32)

    def to_core(f, slot, hf):
        @pl.loop(0, RING)
        def _(j):
            col = column(hf, OFFSETS[slot], offset(j), 1 - core)
            ds[f, slot, hf, j] = difference(f, hf * half_rows, half_rows, col).astype(BF16)
        send(ds.at[f, slot, hf], dr.at[f, slot, hf], 0, core_sems.at[f, slot], dev(0, 0, 1))

    def from_core(f, slot):
        wait(dr.at[f, slot], core_sems.at[f, slot])

    def pair_sum(f, hf, slot, j, row, n):
        col = column(hf, OFFSETS[slot], offset(j), core)
        return (difference(f, hf * half_rows + row, n, col)
                + dr[f, slot, hf, j, pl.ds(row, n)].astype(F32))

    def ring1_far(f, hf):
        for q, way in ((0, 1), (1, -1)):
            @pl.loop(0, RING)
            def _(j):
                s_send[f, hf, 2, q, j] = pair_sum(f, hf, 3, j, q * quarter, quarter).astype(BF16)
            send(s_send.at[f, hf, 2, q], s_mid.at[f, hf, q], 1, mid_sems.at[f], along(hf, way))

    def ring1_near(f, hf, slot):
        q, way = (1, 1) if slot == 1 else (0, -1)

        @pl.loop(0, RING)
        def _(j):
            s_send[f, hf, slot - 1, q, j] = pair_sum(f, hf, slot, j, q * quarter, quarter).astype(BF16)
        send(s_send.at[f, hf, slot - 1, q], s_end.at[f, hf, slot - 1, q], 1, end_sems.at[f], along(hf, way))

    def ring1_middle(f, hf):
        for slot, q, way in ((1, 0, 1), (2, 1, -1)):
            @pl.loop(0, RING)
            def _(j):
                total = pair_sum(f, hf, slot, j, q * quarter, quarter) + s_mid[f, hf, q, j].astype(F32)
                s_send[f, hf, slot - 1, q, j] = total.astype(BF16)
            send(s_send.at[f, hf, slot - 1, q], s_end.at[f, hf, slot - 1, q], 1, end_sems.at[f], along(hf, way))

    def ring2_open(f, hf):
        def whole(j, q):
            total = pair_sum(f, hf, 0, j, q * quarter, quarter)
            return total + s_end[f, hf, 0, q, j].astype(F32) + s_end[f, hf, 1, q, j].astype(F32)

        for slot in (3, 1, 2):
            for q in both:
                t_send[f, hf, slot - 1, pl.ds(q * quarter, quarter)] = whole(slot, q).astype(BF16)
            send(t_send.at[f, hf, slot - 1], t_end.at[f, hf, slot - 1], 2, end2_sems.at[f],
                 along(1 - hf, OFFSETS[slot]))
        for q in both:
            tt[f, hf, pl.ds(q * quarter, quarter)] = whole(0, q)

    def ring2_close(f, hf):
        part = tt[f, hf]
        for k in range(RING - 1):
            part = part + t_end[f, hf, k].astype(F32)
        part = part * (1.0 / (2 * RING * RING))
        av[f, pl.ds(hf * half_rows, half_rows)] = part

    def tile(part):
        square = jnp.sum((part * part).reshape(half_rows // 8, 8, width), axis=0)
        total = square[:, :128]
        for c in range(1, width // 128):
            total = total + square[:, c * 128:(c + 1) * 128]
        return total

    def exchange(f, stage, tiles, me, partners):
        for partner in partners:
            send(tiles.at[f, me], tiles.at[f, me], 3 + stage, norm_sems.at[f, stage], dev(*partner))

    def gathered(f, stage, tiles, partners):
        wait(tiles.at[f, pl.ds(0, len(partners))], norm_sems.at[f, stage])
        return jnp.sum(tiles[f], axis=0)

    def norm_open(f):
        at = pl.ds(half_rows, half_rows)
        n2[f, x * RING + y] = tile(av[f, pl.ds(0, half_rows)]) + tile(av[f, at])
        exchange(f, 1, n2, x * RING + y, far)

    def norm_middle(f):
        n1[f, z * 2 + core] = gathered(f, 1, n2, far)
        exchange(f, 0, n1, z * 2 + core, near)

    def factor_of(f):
        norm_squared = jnp.sum(gathered(f, 0, n1, near), axis=(0, 1), keepdims=True)
        return jnp.minimum(1.0, CLIP_LEVEL * jnp.sqrt(F32(count)) / jnp.sqrt(norm_squared + 1e-06))

    STEP, AVERAGE, MOMENT = 0, 1, 2
    FIRST, NEAR, LAST = pl.ds(0, 1), pl.ds(1, 2), pl.ds(3, 1)

    def gather1(s, hf, slot, k):
        back = (None, 2, 1, 3)[slot]
        send(g.at[s, hf, 0, 0], g.at[s, hf, 0, back], 5, gather_sems.at[s, k], along(1 - hf, OFFSETS[slot]))

    def gather2(s, hf, at, k):
        for slot, back in ((1, 2), (2, 1)):
            send(g.at[s, hf, 0, at], g.at[s, hf, back, at], 6, gather_sems.at[s, k], along(hf, OFFSETS[slot]))

    def gather2_pass(s, hf, at, k):
        k = 6 if k == 4 else 5
        for back, way, q in ((2, 1, 0), (1, -1, 1)):
            rows_at = pl.ds(q * quarter, quarter)
            send(g.at[s, hf, back, at, rows_at], g.at[s, hf, 3, at, rows_at], 6,
                 gather_sems.at[s, k], along(hf, way))

    def spread(s):
        for hf in both:
            for slot in (1, 2, 3)[:2 if s == MOMENT else 3]:
                gather1(s, hf, slot, slot // 3)
        for hf in both:
            gather2(s, hf, FIRST, 2)

    def share(i, *slots):
        for hf in both:
            for slot in slots:
                back = (None, 2, 1, 3)[slot]
                send(p.at[i, hf, 0], p.at[i, hf, back], 8, share_sems.at[i, slot // 3], along(1 - hf, OFFSETS[slot]))

    def share_average():
        for hf in both:
            p[0, hf, 0] = av[0, pl.ds(hf * half_rows, half_rows)].astype(BF16)
        share(0, 1, 2, 3)

    def spread_moment():
        mom_load.wait()
        for hf in both:
            at = pl.ds(hf * half_rows, half_rows)
            g[MOMENT, hf, 0, 0] = mom[1, at].astype(BF16)
            p[1, hf, 0] = mom[0, at].astype(BF16)
        spread(MOMENT)
        share(1, 1, 2)

    def spread_average():
        for hf in both:
            g[AVERAGE, hf, 0, 0] = av[1, pl.ds(hf * half_rows, half_rows)].astype(BF16)
        spread(AVERAGE)

    def spread_step():
        factor = factor_of(0)
        for i in (1, 0):
            wait(p.at[i, :, NEAR], share_sems.at[i, 0])
            wait(p.at[i, :, LAST], share_sems.at[i, 1])
        for at, slots, k in ((FIRST, (0,), 2), (NEAR, (1, 2), 3), (LAST, (3,), 4)):
            for hf in both:
                for slot in slots:
                    clipped = p[0, hf, slot].astype(F32) * factor
                    moment = OUTER_MOMENTUM * p[1, hf, slot].astype(F32) + clipped
                    g[STEP, hf, 0, slot] = (clipped + OUTER_MOMENTUM * moment).astype(BF16)
                gather2(STEP, hf, at, k)
        for hf in both:
            hand_over(STEP, hf, 0, 1, 0)
        mout[0] = OUTER_MOMENTUM * mom[0] + av[0] * factor

    def spread_far(s):
        for hf in both:
            gather1(s, hf, 3, 1)
        share(1, 3)

    scales = {STEP: OUTER_RATE, MOMENT: OUTER_RATE * OUTER_MOMENTUM * OUTER_MOMENTUM}

    def clip_average():
        factor = factor_of(1)
        mout[1] = OUTER_MOMENTUM * mom[1] + av[1] * factor
        scales[AVERAGE] = OUTER_RATE * (1.0 + OUTER_MOMENTUM) * factor

    def gather1_near(s):
        wait(g.at[s, :, 0, NEAR], gather_sems.at[s, 0])
        for hf in both:
            gather2(s, hf, NEAR, 3)

    def gather1_far(s):
        wait(g.at[s, :, 0, LAST], gather_sems.at[s, 1])
        for hf in both:
            gather2(s, hf, LAST, 4)
        for hf in both:
            hand_over(s, hf, 0, 1, 0)

    def gather2_passes(s, at, k):
        wait(g.at[s, :, pl.ds(1, 2), at], gather_sems.at[s, k])
        for hf in both:
            gather2_pass(s, hf, at, k)

    def gather2_first(s):
        gather2_passes(s, FIRST, 2)

    def gather2_near(s):
        gather2_passes(s, NEAR, 3)

    def gather2_far(s):
        gather2_passes(s, LAST, 4)
        for hf in both:
            hand_over(s, hf, 1, 2, 1)

    def gather2_last(s):
        most = pl.ds(0, RING - 1)
        wait(g.at[s, :, 3, most], gather_sems.at[s, 5])
        for hf in both:
            send(g.at[s, hf, 3, most], h.at[s, hf, 3, most], 7, hand_sems.at[s, 2], dev(0, 0, 1))

    def gather2_end(s):
        wait(g.at[s, :, 3, LAST], gather_sems.at[s, 6])
        for hf in both:
            send(g.at[s, hf, 3, LAST], h.at[s, hf, 3, LAST], 7, hand_sems.at[s, 3], dev(0, 0, 1))

    def hand_over(s, hf, slot, n, k):
        at = pl.ds(slot, n)
        send(g.at[s, hf, at], h.at[s, hf, at], 7, hand_sems.at[s, k], dev(0, 0, 1))

    def refresh(s, hf, slot, blocks, c, first=0, last=RING):
        f = 0 if s == STEP else 1
        at = pl.ds(hf * half_rows, half_rows)
        scale = scales[s]

        @pl.loop(first, last)
        def _(j):
            col = pl.ds(column(hf, OFFSETS[slot], offset(j), c), width)
            gw[f, at, col] = gw[f, at, col] - scale * blocks[s, hf, slot, j].astype(F32)

    def own(s, *slots):
        for hf in both:
            for slot in slots:
                refresh(s, hf, slot, g, core)

    def other(s, k):
        if k < 2:
            slot, n = ((0, 1), (1, 2))[k]
            wait(h.at[s, :, pl.ds(slot, n)], hand_sems.at[s, k])
            for hf in both:
                for i in range(n):
                    refresh(s, hf, slot + i, h, 1 - core)
        else:
            for k, first, last in ((2, 0, RING - 1), (3, RING - 1, RING)):
                wait(h.at[s, :, 3, pl.ds(first, last - first)], hand_sems.at[s, k])
                for hf in both:
                    refresh(s, hf, 3, h, 1 - core, first, last)

    steps = []

    def step(work, *args):
        steps.append((work, args))

    def halves(work, f):
        for hf in both:
            work(f, hf)

    def core_step(f, slot):
        load(f, slot)
        for hf in both:
            to_core(f, slot, hf)

    def far_step(f):
        from_core(f, 3)
        halves(ring1_far, f)

    def near_step(f, slot):
        from_core(f, slot)
        for hf in both:
            ring1_near(f, hf, slot)

    def middle_step(f):
        wait(s_mid.at[f], mid_sems.at[f])
        halves(ring1_middle, f)

    def open_step(f):
        from_core(f, 0)
        wait(s_end.at[f], end_sems.at[f])
        halves(ring2_open, f)

    def close_step(f):
        wait(t_end.at[f], end2_sems.at[f])
        halves(ring2_close, f)

    step(spread_moment)
    step(core_step, 0, 3)
    step(core_step, 0, 1)
    step(far_step, 0)
    step(core_step, 0, 2)
    step(near_step, 0, 1)
    step(core_step, 0, 0)
    step(near_step, 0, 2)
    step(known)
    step(core_step, 1, 3)
    step(core_step, 1, 1)
    step(core_step, 1, 2)
    step(far_step, 1)
    step(core_step, 1, 0)
    step(middle_step, 0)
    step(spread_far, MOMENT)
    step(near_step, 1, 1)
    step(near_step, 1, 2)
    step(middle_step, 1)
    step(open_step, 0)
    step(gather1_near, MOMENT)
    step(gather1_far, MOMENT)
    step(open_step, 1)
    step(close_step, 0)
    step(norm_open, 0)
    step(share_average)
    step(gather2_first, MOMENT)
    step(close_step, 1)
    step(spread_average)
    step(norm_open, 1)
    step(gather2_near, MOMENT)
    step(norm_middle, 0)
    step(gather2_far, MOMENT)
    step(own, MOMENT, 0)
    step(gather1_near, AVERAGE)
    step(gather1_far, AVERAGE)
    step(own, MOMENT, 1)
    step(gather2_first, AVERAGE)
    step(spread_step)
    step(own, MOMENT, 2)
    step(gather2_last, MOMENT)
    step(gather2_end, MOMENT)
    step(other, MOMENT, 0)
    step(gather2_near, AVERAGE)
    step(norm_middle, 1)
    step(gather2_first, STEP)
    step(gather2_far, AVERAGE)
    step(other, MOMENT, 1)
    step(own, MOMENT, 3)
    step(gather2_near, STEP)
    step(gather2_far, STEP)
    step(other, MOMENT, 2)
    step(clip_average)
    step(own, AVERAGE, 0, 1, 2)
    step(other, AVERAGE, 0)
    step(gather2_last, AVERAGE)
    step(gather2_end, AVERAGE)
    step(own, STEP, 0, 1, 2)
    step(other, STEP, 0)
    step(other, AVERAGE, 1)
    step(gather2_last, STEP)
    step(own, AVERAGE, 3)
    step(gather2_end, STEP)
    step(other, STEP, 1)
    step(other, AVERAGE, 2)
    step(own, STEP, 3)
    step(other, STEP, 2)

    for work, args in steps:
        work(*args)

    wait(ds, send_sems.at[0])
    wait(s_send, send_sems.at[1])
    wait(t_send, send_sems.at[2])
    wait(n1.at[:, pl.ds(0, len(near))], send_sems.at[3])
    wait(n2.at[:, pl.ds(0, len(far))], send_sems.at[4])
    wait(g.at[pl.ds(1, frags), :, 0, pl.ds(0, 3)], send_sems.at[5])
    wait(g.at[:, :, pl.ds(0, 3)], send_sems.at[6])
    wait(h, send_sems.at[7])
    wait(p.at[:, :, pl.ds(0, 3)], send_sems.at[8])


def store(refreshed, moment, refreshed_out, moment_out, sems):
    frags, rows, _ = refreshed.shape
    n = rows // PARTS
    copies = [pltpu.make_async_copy(moment, moment_out, sems.at[frags * PARTS])]
    for f in range(frags):
        for i in range(PARTS):
            at = pl.ds(i * n, n)
            copies.append(pltpu.make_async_copy(refreshed.at[f, at], refreshed_out.at[f, at], sems.at[f * PARTS + i]))
    for copy in copies:
        copy.start()
    for copy in copies:
        copy.wait()


def synchronize(local_weights, global_weights, momentum):
    frags, rows, cols = global_weights.shape
    width = momentum.shape[2]
    zs = lax.axis_size("fsdp")
    assert lax.axis_size("replica") == 2 * RING * RING and frags == 2
    half_rows, quarter = rows // 2, rows // 4
    anywhere = pl.BlockSpec(memory_space=pl.ANY)
    in_vmem = pl.BlockSpec(memory_space=pltpu.VMEM)
    dma = pltpu.SemaphoreType.DMA
    refreshed, moment = pl.pallas_call(
        functools.partial(kernel, zs, rows * zs * cols),
        out_shape=(pltpu.VMEM(global_weights.shape, F32), pltpu.VMEM(momentum.shape, F32)),
        in_specs=[anywhere] * 3,
        out_specs=(in_vmem, in_vmem),
        scratch_shapes=[
            pltpu.VMEM((frags, rows, cols), BF16),
            pltpu.VMEM((frags, rows, width), F32),
            pltpu.VMEM((frags, RING, 2, RING, half_rows, width), BF16),
            pltpu.VMEM((frags, RING, 2, RING, half_rows, width), BF16),
            pltpu.VMEM((frags, 2, RING - 1, 2, RING, quarter, width), BF16),
            pltpu.VMEM((frags, 2, 2, RING, quarter, width), BF16),
            pltpu.VMEM((frags, 2, 2, 2, RING, quarter, width), BF16),
            pltpu.VMEM((frags, 2, half_rows, width), F32),
            pltpu.VMEM((frags, 2, RING - 1, half_rows, width), BF16),
            pltpu.VMEM((frags, 2, RING - 1, half_rows, width), BF16),
            pltpu.VMEM((frags, rows, width), F32),
            pltpu.VMEM((frags, 2 * zs, 8, 128), F32),
            pltpu.VMEM((frags, RING * RING, 8, 128), F32),
            pltpu.VMEM((frags + 1, 2, RING, RING, half_rows, width), BF16),
            pltpu.VMEM((frags + 1, 2, RING, RING, half_rows, width), BF16),
            pltpu.VMEM((2, 2, RING, half_rows, width), BF16),
            dma((RING + 1, 2)),
            dma,
            pltpu.SemaphoreType.REGULAR,
            dma((9,)),
            dma((frags, 2)),
            dma((frags, RING)),
            dma((frags,)),
            dma((frags,)),
            dma((frags,)),
            dma((frags + 1, 7)),
            dma((frags + 1, 4)),
            dma((2, 2)),
        ],
        compiler_params=pltpu.CompilerParams(
            collective_id=0, has_side_effects=True, vmem_limit_bytes=50 * 2**20
        ),
        cost_estimate=pl.CostEstimate(flops=20 * rows * cols, bytes_accessed=20 * frags * rows * cols // 2, transcendentals=0),
    )(local_weights, global_weights, momentum)
    return pl.pallas_call(
        store,
        out_shape=(
            jax.ShapeDtypeStruct(global_weights.shape, F32),
            jax.ShapeDtypeStruct(momentum.shape, F32),
        ),
        in_specs=[in_vmem, in_vmem],
        out_specs=(anywhere, anywhere),
        scratch_shapes=[dma((frags * PARTS + 1,))],
        compiler_params=pltpu.CompilerParams(vmem_limit_bytes=2 * 2**20),
    )(refreshed, moment)


def solution(mesh):
    return jax.shard_map(
        synchronize,
        mesh=mesh,
        in_specs=(
            P("replica", None, "fsdp", None),
            P(None, "fsdp", None),
            P(None, "fsdp", "replica"),
        ),
        out_specs=(P(None, "fsdp", None), P(None, "fsdp", "replica")),
        check_vma=False,
    )
```
